512 devices in a mesh: dp: 32 (over x, y), seq: 16 (over z, core).
Axes of the slice: x: 4, y: 8, z: 8, core: 2. Of those that a mesh axis runs over, the one named last changes fastest.
Arguments:
- queries: bfloat16 [32, 2048, 2048], P('dp', 'seq'), may hold values from -8 to 8
- keys: bfloat16 [32, 2048, 1024], P('dp', 'seq'), may hold values from -8 to 8
- values: bfloat16 [32, 2048, 1024], P('dp', 'seq'), may hold values from -6 to 6
- cotangent: bfloat16 [32, 2048, 2048], P('dp', 'seq'), may hold values from -6 to 6
- out_weight: bfloat16 [2048, 2048], P('seq'), may hold values from -0.125 to 0.125
- segment: int32 [32, 2048], P('dp', 'seq'), may hold values from 0 to 23, as said below
- row_type: int32 [32, 2048], P('dp', 'seq'), may hold values from 0 to 2, as said below
- pair_index: int32 [32, 24], P('dp'), may hold values from 0 to 7, as said below
Outputs:
- query_grad: bfloat16 [32, 2048, 2048], P('dp', 'seq')
- key_grad: bfloat16 [32, 2048, 1024], P('dp', 'seq')
- value_grad: bfloat16 [32, 2048, 1024], P('dp', 'seq')
- weight_grad: float32 [2048, 2048], P('seq', 'dp')
The draws below stay inside these ranges and needn't reach their ends.
Inputs may be any that keep to these rules, and one draw needn't show every extreme that they name: In each row the segment numbers never fall and each segment holds one or more tokens; segments come in groups of six: the prompts of two pairs, then the chosen and rejected responses of those two pairs in any order; the six segments of group g fill exactly the tokens g * 512 to (g + 1) * 512 - 1. `row_type`: all tokens of a segment have one type. `pair_index`: each pair has one prompt segment, one chosen and one rejected segment, the prompt before both responses.
All inputs are finite; a program needn't handle non-finite values.
Results may differ from the reference program's by a relative error of at most 0.035.
Values may be sent and summed in bfloat16 or wider, within the bound.
No kernel may reach another device: no remote copies, remote signals or barrier semaphores. Data moves between devices by JAX's collectives and lax.ppermute only.
A program may use at most 64 MiB of HBM per device.

```python
import jax
import jax.numpy as jnp
from jax import lax

HD = 128
DW = 2048
HQ = 16
KV = 8
SEGS = 24
ROWS = 32
SEQ_LEN = 2048


def layout_draw(key):
    groups = SEGS // 6
    window = SEQ_LEN // groups
    cut_keys = jax.random.split(jax.random.fold_in(key, 101), ROWS * groups)

    def window_cuts(cut_key):
        return jnp.sort(jax.random.permutation(cut_key, window - 1)[:5] + 1)
    inner = jax.vmap(window_cuts)(cut_keys).reshape(ROWS, groups, 5)
    position = jnp.arange(SEQ_LEN)
    local = position % window
    group_of = position // window
    passed = jnp.sum((inner[:, group_of, :] <= local[None, :, None]).astype(jnp.int32), axis=2)
    segment = 6 * group_of[None, :] + passed
    swapped = jax.random.randint(jax.random.fold_in(key, 102), (ROWS, groups), 0, 2)
    ranking = jax.random.randint(jax.random.fold_in(key, 103), (ROWS, groups, 4), 0, 1 << 20) * 4 + jnp.arange(4)
    arrangement = jnp.argsort(ranking, axis=-1, stable=True)
    offsets = 2 * jnp.arange(groups)[None, :]
    prompt_pairs = jnp.stack([offsets + swapped, offsets + 1 - swapped], axis=-1)
    reply_pairs = offsets[..., None] + arrangement // 2
    reply_types = 1 + arrangement % 2
    pair_ids = jnp.concatenate([prompt_pairs, reply_pairs], axis=-1).reshape(ROWS, SEGS)
    type_ids = jnp.concatenate([jnp.zeros((ROWS, groups, 2), jnp.int32), reply_types], axis=-1).reshape(ROWS, SEGS)
    row_type = jnp.take_along_axis(type_ids, segment, axis=1)
    return (segment.astype(jnp.int32), row_type.astype(jnp.int32), pair_ids.astype(jnp.int32))


def draw_segment(key, part):
    shared = layout_draw(key)
    return shared[0]


def draw_row_type(key, part):
    shared = layout_draw(key)
    return shared[1]


def draw_pair_index(key, part):
    shared = layout_draw(key)
    return shared[2]


def draw_queries(key, part):
    key = jax.random.fold_in(key, 1)
    return jnp.clip(jax.random.normal(key, (ROWS, SEQ_LEN, HQ * HD), jnp.float32), -6.0, 6.0).astype(jnp.bfloat16)


def draw_keys(key, part):
    key = jax.random.fold_in(key, 2)
    return jnp.clip(jax.random.normal(key, (ROWS, SEQ_LEN, KV * HD), jnp.float32), -6.0, 6.0).astype(jnp.bfloat16)


def raised(drawn, stream_key, source, target, shards_of, factor):
    def block_of(dim):
        return (jnp.arange(drawn.shape[dim]) // (drawn.shape[dim] // shards_of)).reshape((-1,) + (1,) * (drawn.ndim - 1 - dim))

    first = jax.random.permutation(stream_key, shards_of)[block_of(target)]
    second = (block_of(target) + shards_of // 2) % shards_of
    return jnp.where((block_of(source) == first) | (block_of(source) == second), factor * drawn, drawn)


def levels(rng, shape, shards, smallest, top_value):
    def one(dim, parts):
        steps = jax.random.uniform(jax.random.fold_in(jax.random.fold_in(rng, 6), dim), (parts,), jnp.float32, smallest / len(shards), top_value / len(shards))
        return jnp.repeat(jnp.exp(steps), shape[dim] // parts).reshape((-1,) + (1,) * (len(shape) - dim - 1))

    loudness = one(*shards[0])
    for cut in shards[1:]:
        loudness = loudness * one(*cut)
    return loudness


def centred(stream_key, dims, scale, limit, cuts=(), dtype=jnp.bfloat16):
    result = scale * jax.random.normal(stream_key, dims, jnp.float32)
    if cuts:
        result = result * levels(stream_key, dims, cuts, -0.22, 0.18)
    return jnp.clip(result, -limit, limit).astype(dtype)


def gaussian_with(stream_key, dims, width, reach, cuts, heavy, held_as=jnp.bfloat16):
    values = width * jax.random.normal(stream_key, dims, jnp.float32)
    if cuts:
        values = values * levels(stream_key, dims, cuts, -0.22, 0.18)
    return jnp.clip(raised(values, jax.random.fold_in(stream_key, 3), *heavy), -reach, reach).astype(held_as)


def setup_inputs(seed: int = 0) -> dict:
    key_list = jax.random.split(jax.random.key(seed), 9)
    queries = draw_queries(jax.random.fold_in(key_list[8], 71), 0)
    keys = draw_keys(jax.random.fold_in(key_list[8], 71), 0)
    values = centred(key_list[2], (ROWS, SEQ_LEN, KV * HD), 1.0, 6.0, ((0, 32), (1, 16)))
    cotangent = gaussian_with(key_list[3], (ROWS, SEQ_LEN, DW), 1.0, 6.0, ((0, 32), (1, 16)), (0, 2, 32, 2.75))
    out_weight = centred(key_list[4], (HQ * HD, DW), (HQ * HD) ** -0.5, 0.125, ((0, 16),))
    segment = draw_segment(jax.random.fold_in(key_list[8], 71), 0)
    row_type = draw_row_type(jax.random.fold_in(key_list[8], 71), 0)
    pair_index = draw_pair_index(jax.random.fold_in(key_list[8], 71), 0)
    return {"queries": queries, "keys": keys, "values": values, "cotangent": cotangent, "out_weight": out_weight, "segment": segment, "row_type": row_type, "pair_index": pair_index}


def visible_mask(segment_row, type_row, pair_row):
    position = jnp.arange(segment_row.shape[0])
    pair_token = jnp.take(pair_row, segment_row)
    same_segment = segment_row[:, None] == segment_row[None, :]
    from_prompt = (type_row[None, :] == 0) & (type_row[:, None] != 0) & (pair_token[:, None] == pair_token[None, :])
    causal = position[None, :] <= position[:, None]
    return causal & (same_segment | from_prompt)


def reference(queries, keys, values, cotangent, out_weight, segment, row_type, pair_index):
    score_scale = HD ** -0.5
    weight_heads = out_weight.astype(jnp.float32).reshape(HQ, HD, DW)

    def one_row(accumulated, inputs):
        query_row, key_row, value_row, grad_row, segment_row, type_row, pair_row = inputs
        allowed = visible_mask(segment_row, type_row, pair_row)[None]
        query_head = query_row.astype(jnp.float32).reshape(SEQ_LEN, HQ, HD).transpose(1, 0, 2)
        key_head = jnp.repeat(key_row.astype(jnp.float32).reshape(SEQ_LEN, KV, HD).transpose(1, 0, 2), 2, axis=0)
        value_head = jnp.repeat(value_row.astype(jnp.float32).reshape(SEQ_LEN, KV, HD).transpose(1, 0, 2), 2, axis=0)
        scores = jnp.einsum("hqd,hkd->hqk", query_head, key_head) * score_scale
        row_max = jnp.max(jnp.where(allowed, scores, -jnp.inf), axis=-1, keepdims=True)
        exponent = jnp.where(allowed, jnp.exp(scores - row_max), 0.0)
        attend = exponent / jnp.sum(exponent, axis=-1, keepdims=True)
        attend_low = attend.astype(jnp.bfloat16)
        output_head = jnp.einsum("hqk,hkd->hqd", attend_low.astype(jnp.float32), value_head).astype(jnp.bfloat16)
        grad_out = grad_row.astype(jnp.float32)
        grad_head = jnp.einsum("qc,hdc->hqd", grad_out, weight_heads).astype(jnp.bfloat16)
        accumulated = accumulated + jnp.einsum("hqd,qc->hdc", output_head.astype(jnp.float32), grad_out).reshape(HQ * HD, DW)
        row_delta = jnp.sum(grad_head.astype(jnp.float32) * output_head.astype(jnp.float32), axis=-1, keepdims=True)
        grad_attend = jnp.einsum("hqd,hkd->hqk", grad_head.astype(jnp.float32), value_head)
        grad_scores = (attend * (grad_attend - row_delta) * score_scale).astype(jnp.bfloat16)
        grad_query = jnp.einsum("hqk,hkd->hqd", grad_scores.astype(jnp.float32), key_head).astype(jnp.bfloat16)
        key_part = jnp.einsum("hqk,hqd->hkd", grad_scores.astype(jnp.float32), query_head).astype(jnp.bfloat16)
        value_part = jnp.einsum("hqk,hqd->hkd", attend_low.astype(jnp.float32), grad_head.astype(jnp.float32)).astype(jnp.bfloat16)
        grad_key = jnp.sum(key_part.astype(jnp.float32).reshape(KV, 2, SEQ_LEN, HD), axis=1).astype(jnp.bfloat16)
        grad_value = jnp.sum(value_part.astype(jnp.float32).reshape(KV, 2, SEQ_LEN, HD), axis=1).astype(jnp.bfloat16)
        results = (grad_query.transpose(1, 0, 2).reshape(SEQ_LEN, HQ * HD),
                   grad_key.transpose(1, 0, 2).reshape(SEQ_LEN, KV * HD),
                   grad_value.transpose(1, 0, 2).reshape(SEQ_LEN, KV * HD))
        return accumulated, results

    weight_grad, stacked = lax.scan(one_row, jnp.zeros((HQ * HD, DW), jnp.float32),
                                    (queries, keys, values, cotangent, segment, row_type, pair_index))
    return stacked[0], stacked[1], stacked[2], weight_grad
```

```python
import itertools

import jax
import jax.numpy as jnp
import numpy as np
from jax import lax
from jax.experimental import pallas as pl
from jax.experimental.pallas import tpu as pltpu
from jax.sharding import Mesh
from jax.sharding import PartitionSpec as P

HD = 128
WINDOW = 512
TOK = 128
AXES = ("xh", "xl", "y", "w", "p", "c")
SIZES = (2, 2, 8, 4, 2, 2)
NEAR = ("xl", "p", "c")
FAR = ("xh", "y", "w")
CODE = 16
PAY = 4 * TOK + CODE
NONE = 99
F32 = jnp.float32
BF16 = jnp.bfloat16


def place(*index):
    return int(np.ravel_multi_index(index, SIZES))


def weight_moves(turn):
    moves = []
    for xh, xl, y, w, p, c in itertools.product(*map(range, SIZES)):
        head = 2 * (4 * xl + 2 * p + c) + (w + turn) % 2
        source = place(xh, w // 2, y, head // 4, (head // 2) % 2, head % 2)
        moves.append((source, place(xh, xl, y, w, p, c)))
    return moves


def dot(left, right, dims):
    return lax.dot_general(left, right, (dims, ((), ())), preferred_element_type=F32)


def pack_kernel(q_ref, k_ref, v_ref, seg_ref, type_ref, pair_ref, out_ref):
    for g in range(8):
        out_ref[g, 0:TOK, :] = q_ref[0, :, 2 * g * HD : (2 * g + 1) * HD]
        out_ref[g, TOK : 2 * TOK, :] = q_ref[0, :, (2 * g + 1) * HD : (2 * g + 2) * HD]
        out_ref[g, 2 * TOK : 3 * TOK, :] = k_ref[0, :, g * HD : (g + 1) * HD]
        out_ref[g, 3 * TOK : 4 * TOK, :] = v_ref[0, :, g * HD : (g + 1) * HD]
    seg = seg_ref[...]
    kind = type_ref[...]
    pair = jnp.zeros_like(seg)
    count = pair_ref.shape[1]
    for s in range(count):
        pair = jnp.where(seg == s, pair_ref[0, s], pair)
    as_query = jnp.where(kind != 0, count + pair, NONE)
    as_key = jnp.where(kind == 0, count + pair, NONE)
    row = lax.broadcasted_iota(jnp.int32, (CODE, TOK), 0)
    code = jnp.where(row == 0, seg, jnp.where(row == 1, as_query, jnp.where(row == 2, as_key, 0)))
    code = code.astype(F32).astype(BF16)
    for g in range(8):
        out_ref[g, 4 * TOK :, :] = code


def main_kernel(odd_ref, pay_ref, cot_ref, w0_ref, w1_ref, ret_ref, wg_ref, wbuf, ghbuf, obuf, wacc):
    unit = pl.program_id(0)
    scale = HD ** (-0.5)

    @pl.when(unit == 0)
    def _():
        odd = odd_ref[0]
        wbuf[pl.ds(pl.multiple_of(odd * HD, HD), HD), :] = w0_ref[...]
        wbuf[pl.ds(pl.multiple_of((1 - odd) * HD, HD), HD), :] = w1_ref[...]

    ghbuf[...] = dot(cot_ref[...], wbuf[...], ((1,), (1,))).astype(BF16)

    def rows(first):
        return pay_ref[:, first : first + TOK, :].reshape(WINDOW, HD)

    key = rows(2 * TOK)
    value = rows(3 * TOK)
    code = jnp.concatenate([pay_ref[i, 4 * TOK :, :] for i in range(4)], axis=1)
    code = code.astype(F32)[0:8]
    slot = lax.broadcasted_iota(jnp.int32, (32, WINDOW), 0).astype(F32)
    seg_hot = slot == code[0:1]
    want = jnp.where(seg_hot | (slot == code[1:2]), 1.0, 0.0).astype(BF16)
    have = jnp.where(seg_hot | (slot == code[2:3]), 1.0, 0.0).astype(BF16)

    half = WINDOW // 2
    kparts = [[None, None], [None, None]]
    vparts = [[None, None], [None, None]]
    for block in range(2):
        lo = block * half
        ext = lo + half
        count = dot(want[:, lo:ext], have[:, :ext], ((0,), (0,)))
        t_pos = lax.broadcasted_iota(jnp.int32, (half, ext), 0) + lo
        s_pos = lax.broadcasted_iota(jnp.int32, (half, ext), 1)
        visible = (count > 0.5) & (s_pos <= t_pos)
        for b in range(2):
            query = rows(b * TOK)[lo:ext]
            grad = ghbuf[lo:ext, b * HD : (b + 1) * HD]
            scores = dot(query, key[:ext], ((1,), (1,))) * scale
            scores = jnp.where(visible, scores, -jnp.inf)
            top = jnp.max(scores, axis=-1, keepdims=True)
            exponent = jnp.exp(scores - top)
            attend = exponent * (1.0 / jnp.sum(exponent, axis=-1, keepdims=True))
            low = attend.astype(BF16)
            out = dot(low, value[:ext], ((1,), (0,))).astype(BF16)
            obuf[lo:ext, b * HD : (b + 1) * HD] = out
            delta = jnp.sum(grad.astype(F32) * out.astype(F32), axis=-1, keepdims=True)
            grad_attend = dot(grad, value[:ext], ((1,), (1,)))
            ds = (attend * (grad_attend - delta) * scale).astype(BF16)
            dq = dot(ds, key[:ext], ((1,), (0,))).astype(BF16)
            ret_ref[2 * block : 2 * block + 2, b * TOK : (b + 1) * TOK, :] = dq.reshape(2, TOK, HD)
            dk = dot(ds, query, ((0,), (0,)))
            dv = dot(low, grad, ((0,), (0,)))
            if block == 0:
                kparts[b][0] = dk
                vparts[b][0] = dv
            else:
                kparts[b] = [kparts[b][0] + dk[:half], dk[half:]]
                vparts[b] = [vparts[b][0] + dv[:half], dv[half:]]
    for block in range(2):
        for first, parts in ((2 * TOK, kparts), (3 * TOK, vparts)):
            both = parts[0][block].astype(BF16).astype(F32) + parts[1][block].astype(BF16).astype(F32)
            ret_ref[2 * block : 2 * block + 2, first : first + TOK, :] = both.astype(BF16).reshape(2, TOK, HD)

    part = dot(obuf[...], cot_ref[...], ((0,), (0,)))

    @pl.when(unit == 0)
    def _():
        wacc[...] = part

    @pl.when(unit == 1)
    def _():
        left = lax.broadcasted_iota(jnp.int32, (64, HD), 1) < 64
        total = wacc[...] + part
        for b in range(2):
            for m in range(16):
                upper = total[b * HD : b * HD + 64, m * HD : (m + 1) * HD]
                lower = total[b * HD + 64 : (b + 1) * HD, m * HD : (m + 1) * HD]
                even = jnp.where(left, upper, pltpu.roll(lower, 64, 1))
                odd = jnp.where(left, pltpu.roll(upper, 64, 1), lower)
                for col, piece in ((2 * m, even), (2 * m + 1, odd)):
                    xh, w, y = col // 16, 2 * ((col // 8) % 2) + b, col % 8
                    wg_ref[(xh * 8 + y) * 4 + w] = piece.astype(BF16)


def unpack_kernel(ret_ref, dq_ref, dk_ref, dv_ref):
    for g in range(8):
        dq_ref[0, :, 2 * g * HD : (2 * g + 1) * HD] = ret_ref[g, 0:TOK, :]
        dq_ref[0, :, (2 * g + 1) * HD : (2 * g + 2) * HD] = ret_ref[g, TOK : 2 * TOK, :]
        dk_ref[0, :, g * HD : (g + 1) * HD] = ret_ref[g, 2 * TOK : 3 * TOK, :]
        dv_ref[0, :, g * HD : (g + 1) * HD] = ret_ref[g, 3 * TOK : 4 * TOK, :]


def sum_kernel(got_ref, out_ref):
    out_ref[...] = jnp.sum(got_ref[...].astype(F32), axis=0)


def spread_kernel(sum_ref, out_ref):
    out_ref[0:64, :] = sum_ref[:, 0:64]
    out_ref[64:128, :] = sum_ref[:, 64:128]


VMEM = pl.BlockSpec(memory_space=pltpu.VMEM)
SMEM = pl.BlockSpec(memory_space=pltpu.SMEM)


def call(kernel, out_shape, **kw):
    return pl.pallas_call(
        kernel,
        out_shape=out_shape,
        compiler_params=pltpu.CompilerParams(vmem_limit_bytes=48 << 20),
        **kw,
    )


def shape(dims, dtype=BF16):
    return jax.ShapeDtypeStruct(dims, dtype)


def run_main(odd, arrived, cot, first, second):
    width = cot.shape[1]
    return call(
        main_kernel,
        (shape((8, 4 * TOK, HD)), shape((64, 64, HD))),
        grid=(2,),
        in_specs=[
            SMEM,
            pl.BlockSpec((4, PAY, HD), lambda u: (u, 0, 0)),
            pl.BlockSpec((WINDOW, width), lambda u: (u, 0)),
            pl.BlockSpec((HD, width), lambda u: (0, 0)),
            pl.BlockSpec((HD, width), lambda u: (0, 0)),
        ],
        out_specs=[
            pl.BlockSpec((4, 4 * TOK, HD), lambda u: (u, 0, 0)),
            pl.BlockSpec((64, 64, HD), lambda u: (0, 0, 0)),
        ],
        scratch_shapes=[
            pltpu.VMEM((2 * HD, width), BF16),
            pltpu.VMEM((WINDOW, 2 * HD), BF16),
            pltpu.VMEM((WINDOW, 2 * HD), BF16),
            pltpu.VMEM((2 * HD, width), F32),
        ],
    )(odd, arrived, cot, first, second)


def local(queries, keys, values, cotangent, out_weight, segment, row_type, pair_index):
    first = lax.ppermute(out_weight, AXES, weight_moves(0))
    second = lax.ppermute(out_weight, AXES, weight_moves(1))
    payload = call(
        pack_kernel,
        shape((8, PAY, HD)),
        in_specs=[VMEM] * 5 + [SMEM],
        out_specs=VMEM,
    )(queries, keys, values, segment, row_type, pair_index)
    arrived = lax.all_to_all(payload, NEAR, 0, 0)
    cot = lax.all_gather(cotangent[0], NEAR, axis=0, tiled=True)
    odd = lax.rem(lax.axis_index("w"), 2).astype(jnp.int32).reshape(1)
    back, pieces = run_main(odd, arrived, cot, first, second)
    spread = lax.all_to_all(pieces, FAR, 0, 0)
    home = lax.all_to_all(back, NEAR, 0, 0)
    summed = call(sum_kernel, shape((64, HD), F32), in_specs=[VMEM], out_specs=VMEM)(spread)
    moved = lax.ppermute(summed, AXES, [(b, a) for a, b in weight_moves(0)])
    weight_grad = call(spread_kernel, shape((HD, 64), F32), in_specs=[VMEM], out_specs=VMEM)(moved)
    query_grad, key_grad, value_grad = call(
        unpack_kernel,
        (shape(queries.shape), shape(keys.shape), shape(values.shape)),
        in_specs=[VMEM],
        out_specs=[VMEM] * 3,
    )(home)
    return query_grad, key_grad, value_grad, weight_grad


def solution(mesh):
    fine = Mesh(mesh.devices.reshape(SIZES), AXES)
    dp, seq = AXES[:3], AXES[3:]
    in_specs = (
        P(dp, seq, None),
        P(dp, seq, None),
        P(dp, seq, None),
        P(dp, seq, None),
        P(seq, None),
        P(dp, seq),
        P(dp, seq),
        P(dp, None),
    )
    out_specs = (P(dp, seq, None), P(dp, seq, None), P(dp, seq, None), P(seq, dp))
    return jax.shard_map(local, mesh=fine, in_specs=in_specs, out_specs=out_specs, check_vma=False)
```

```python
import itertools

import jax
import jax.numpy as jnp
import numpy as np
from jax import lax
from jax.experimental import pallas as pl
from jax.experimental.pallas import tpu as pltpu
from jax.sharding import Mesh
from jax.sharding import PartitionSpec as P

HD = 128
WINDOW = 512
HALF = WINDOW // 2
TOK = 128
SCALE = HD ** (-0.5)
AXES = ("x", "yh", "yl", "w", "p", "c")
SIZES = (4, 4, 2, 4, 2, 2)
NEAR = ("yl", "p", "c")
CODE = 16
PAY = 4 * TOK + CODE
NONE = 99
F32 = jnp.float32
BF16 = jnp.bfloat16


def place(*index):
    return int(np.ravel_multi_index(index, SIZES))


def devices():
    return itertools.product(*map(range, SIZES))


def weight_moves():
    moves = []
    for x, yh, yl, w, p, c in devices():
        head = 2 * (4 * yl + 2 * p + c) + x // 2
        source = place(2 * (w // 2) + x % 2, yh, w % 2, head // 4, (head // 2) % 2, head % 2)
        moves.append((source, place(x, yh, yl, w, p, c)))
    return moves


def piece_moves(turn):
    moves = []
    for x, yh, yl, w, p, c in devices():
        piece = (w + turn) % 4
        head = 2 * (4 * yl + 2 * p + c) + piece % 2
        owner = place(x, yh, piece // 2, head // 4, (head // 2) % 2, head % 2)
        moves.append((place(x, yh, yl, w, p, c), owner))
    return moves


def dot(left, right, dims):
    return lax.dot_general(left, right, (dims, ((), ())), preferred_element_type=F32)


def pack_kernel(q_ref, k_ref, v_ref, seg_ref, type_ref, pair_ref, out_ref):
    seg = seg_ref[...]
    kind = type_ref[...]
    pair = jnp.zeros_like(seg)
    count = pair_ref.shape[1]
    for s in range(count):
        pair = jnp.where(seg == s, pair_ref[0, s], pair)
    as_query = jnp.where(kind != 0, count + pair, NONE)
    as_key = jnp.where(kind == 0, count + pair, NONE)
    row = lax.broadcasted_iota(jnp.int32, (CODE, TOK), 0)
    code = jnp.where(row == 0, seg, jnp.where(row == 1, as_query, jnp.where(row == 2, as_key, 0)))
    code = code.astype(F32).astype(BF16)
    for g in range(2):
        out_ref[g, 0:TOK, :] = q_ref[0, :, 2 * g * HD : (2 * g + 1) * HD]
        out_ref[g, TOK : 2 * TOK, :] = q_ref[0, :, (2 * g + 1) * HD : (2 * g + 2) * HD]
        out_ref[g, 2 * TOK : 3 * TOK, :] = k_ref[0, :, g * HD : (g + 1) * HD]
        out_ref[g, 3 * TOK : 4 * TOK, :] = v_ref[0, :, g * HD : (g + 1) * HD]
        out_ref[g, 4 * TOK :, :] = code


def rows(pay_ref, first):
    return pay_ref[:, first : first + TOK, :].reshape(WINDOW, HD)


def hot(pay_ref):
    code = jnp.concatenate([pay_ref[i, 4 * TOK :, :] for i in range(4)], axis=1)
    code = code.astype(F32)[0:8]
    slot = lax.broadcasted_iota(jnp.int32, (32, WINDOW), 0).astype(F32)
    same = slot == code[0:1]
    want = jnp.where(same | (slot == code[1:2]), 1.0, 0.0).astype(BF16)
    have = jnp.where(same | (slot == code[2:3]), 1.0, 0.0).astype(BF16)
    return want, have


def visible_block(want, have, lo, ext):
    count = dot(want[:, lo:ext], have[:, :ext], ((0,), (0,)))
    t_pos = lax.broadcasted_iota(jnp.int32, (ext - lo, ext), 0) + lo
    s_pos = lax.broadcasted_iota(jnp.int32, (ext - lo, ext), 1)
    return (count > 0.5) & (s_pos <= t_pos)


def forward_kernel(pay_ref, after_ref, out_ref, lse_ref):
    del after_ref
    key = rows(pay_ref, 2 * TOK)
    value = rows(pay_ref, 3 * TOK)
    want, have = hot(pay_ref)
    lane = lax.broadcasted_iota(jnp.int32, (HALF, HD), 1)
    for block in range(2):
        lo = block * HALF
        ext = lo + HALF
        visible = visible_block(want, have, lo, ext)
        stats = []
        for b in range(2):
            query = rows(pay_ref, b * TOK)[lo:ext]
            scores = dot(query, key[:ext], ((1,), (1,))) * SCALE
            scores = jnp.where(visible, scores, -jnp.inf)
            top = jnp.max(scores, axis=-1, keepdims=True)
            exponent = jnp.exp(scores - top)
            total = jnp.sum(exponent, axis=-1, keepdims=True)
            low = (exponent * (1.0 / total)).astype(BF16)
            out = dot(low, value[:ext], ((1,), (0,)))
            out_ref[b * HD : (b + 1) * HD, lo:ext] = out.T.astype(BF16)
            stats.append(top + jnp.log(total))
        lse_ref[lo:ext, :] = jnp.where(lane == 0, stats[0], stats[1])


def weight_kernel(out_ref, cot_ref, a_ref, b_ref, c_ref, wg_ref):
    del a_ref, b_ref, c_ref
    total = dot(out_ref[...], cot_ref[...], ((1,), (0,)))
    left = lax.broadcasted_iota(jnp.int32, (64, HD), 1) < 64
    for b in range(2):
        for yh in range(4):
            upper = total[b * HD : b * HD + 64, yh * HD : (yh + 1) * HD]
            lower = total[b * HD + 64 : (b + 1) * HD, yh * HD : (yh + 1) * HD]
            wg_ref[yh, b] = jnp.where(left, upper, pltpu.roll(lower, 64, 1)).astype(BF16)
            wg_ref[yh, 2 + b] = jnp.where(left, pltpu.roll(upper, 64, 1), lower).astype(BF16)


def backward_kernel(x_ref, pay_ref, lse_ref, cot_ref, w0_ref, w1_ref, w2_ref, w3_ref, ret_ref, wbuf, ghbuf):
    @pl.when(pl.program_id(0) == 0)
    def _():
        for turn, quarter in enumerate((w0_ref, w1_ref, w2_ref, w3_ref)):
            first = pl.multiple_of(lax.rem(x_ref[0] + 4 - turn, 4) * 64, 64)
            wbuf[pl.ds(first, 64), :] = quarter[...]

    ghbuf[...] = dot(cot_ref[...], wbuf[...], ((1,), (1,))).astype(BF16)
    key = rows(pay_ref, 2 * TOK)
    value = rows(pay_ref, 3 * TOK)
    want, have = hot(pay_ref)
    kparts = [[None, None], [None, None]]
    vparts = [[None, None], [None, None]]
    for block in range(2):
        lo = block * HALF
        ext = lo + HALF
        visible = visible_block(want, have, lo, ext)
        for b in range(2):
            query = rows(pay_ref, b * TOK)[lo:ext]
            grad = ghbuf[lo:ext, b * HD : (b + 1) * HD]
            scores = dot(query, key[:ext], ((1,), (1,))) * SCALE - lse_ref[lo:ext, b : b + 1]
            attend = jnp.exp(jnp.where(visible, scores, -jnp.inf))
            low = attend.astype(BF16)
            grad_attend = dot(grad, value[:ext], ((1,), (1,)))
            delta = jnp.sum(attend * grad_attend, axis=-1, keepdims=True)
            ds = (attend * (grad_attend - delta) * SCALE).astype(BF16)
            dq = dot(ds, key[:ext], ((1,), (0,))).astype(BF16)
            ret_ref[2 * block : 2 * block + 2, b * TOK : (b + 1) * TOK, :] = dq.reshape(2, TOK, HD)
            dk = dot(ds, query, ((0,), (0,)))
            dv = dot(low, grad, ((0,), (0,)))
            if block == 0:
                kparts[b][0] = dk
                vparts[b][0] = dv
            else:
                kparts[b] = [kparts[b][0] + dk[:HALF], dk[HALF:]]
                vparts[b] = [vparts[b][0] + dv[:HALF], dv[HALF:]]
    for block in range(2):
        for first, parts in ((2 * TOK, kparts), (3 * TOK, vparts)):
            both = parts[0][block].astype(BF16).astype(F32) + parts[1][block].astype(BF16).astype(F32)
            ret_ref[2 * block : 2 * block + 2, first : first + TOK, :] = both.astype(BF16).reshape(2, TOK, HD)


def unpack_kernel(ret_ref, dq_ref, dk_ref, dv_ref):
    for g in range(2):
        dq_ref[0, :, 2 * g * HD : (2 * g + 1) * HD] = ret_ref[g, 0:TOK, :]
        dq_ref[0, :, (2 * g + 1) * HD : (2 * g + 2) * HD] = ret_ref[g, TOK : 2 * TOK, :]
        dk_ref[0, :, g * HD : (g + 1) * HD] = ret_ref[g, 2 * TOK : 3 * TOK, :]
        dv_ref[0, :, g * HD : (g + 1) * HD] = ret_ref[g, 3 * TOK : 4 * TOK, :]


def sum_kernel(w_ref, got_ref, out0_ref, out1_ref, out2_ref, out3_ref, total):
    total[...] = jnp.sum(got_ref[...].astype(F32), axis=0)
    for turn, out_ref in enumerate((out0_ref, out1_ref, out2_ref, out3_ref)):
        out_ref[...] = total[lax.rem(w_ref[0] + turn, 4)].astype(BF16)


def spread_kernel(a_ref, b_ref, c_ref, d_ref, out_ref):
    total = (a_ref[...].astype(F32) + b_ref[...].astype(F32)) + (c_ref[...].astype(F32) + d_ref[...].astype(F32))
    out_ref[:, 0:64] = total[:, 0:64].T
    out_ref[:, 64:128] = total[:, 64:128].T


SMEM = pl.BlockSpec(memory_space=pltpu.SMEM)
ANY = pl.BlockSpec(memory_space=pl.ANY)


def whole(*dims):
    return pl.BlockSpec(dims, lambda *_: (0,) * len(dims))


def call(kernel, out_shape, flops=0, bytes_accessed=0, room=60, **kw):
    return pl.pallas_call(
        kernel,
        out_shape=out_shape,
        compiler_params=pltpu.CompilerParams(vmem_limit_bytes=room << 20),
        cost_estimate=pl.CostEstimate(flops=flops, bytes_accessed=bytes_accessed, transcendentals=0),
        **kw,
    )


def shape(dims, dtype=BF16):
    return jax.ShapeDtypeStruct(dims, dtype)


def run_pack(queries, keys, values, segment, row_type, pair_index):
    return call(
        pack_kernel,
        shape((8, PAY, HD)),
        bytes_accessed=2 << 20,
        grid=(4,),
        in_specs=[
            pl.BlockSpec((1, TOK, 4 * HD), lambda i: (0, 0, i)),
            pl.BlockSpec((1, TOK, 2 * HD), lambda i: (0, 0, i)),
            pl.BlockSpec((1, TOK, 2 * HD), lambda i: (0, 0, i)),
            whole(1, TOK),
            whole(1, TOK),
            SMEM,
        ],
        out_specs=pl.BlockSpec((2, PAY, HD), lambda i: (i, 0, 0)),
    )(queries, keys, values, segment, row_type, pair_index)


def run_forward(arrived, after):
    return call(
        forward_kernel,
        (shape((2 * HD, 2 * WINDOW)), shape((2 * WINDOW, HD), F32)),
        flops=4 << 30,
        bytes_accessed=2 << 20,
        grid=(2,),
        in_specs=[pl.BlockSpec((4, PAY, HD), lambda u: (u, 0, 0)), ANY],
        out_specs=[
            pl.BlockSpec((2 * HD, WINDOW), lambda u: (0, u)),
            pl.BlockSpec((WINDOW, HD), lambda u: (u, 0)),
        ],
    )(arrived, after)


def run_weight(out, cot, after):
    return call(
        weight_kernel,
        shape((16, 4, 64, HD)),
        flops=1 << 30,
        bytes_accessed=6 << 20,
        grid=(4,),
        in_specs=[
            whole(2 * HD, 2 * WINDOW),
            pl.BlockSpec((2 * WINDOW, 512), lambda i: (0, i)),
        ]
        + [ANY] * 3,
        out_specs=pl.BlockSpec((4, 4, 64, HD), lambda i: (i, 0, 0, 0)),
    )(out, cot, *after)


def run_backward(x, arrived, lse, cot, quarters):
    width = cot.shape[1]
    return call(
        backward_kernel,
        shape((8, 4 * TOK, HD)),
        flops=8 << 30,
        bytes_accessed=7 << 20,
        grid=(2,),
        in_specs=[
            SMEM,
            pl.BlockSpec((4, PAY, HD), lambda u: (u, 0, 0)),
            pl.BlockSpec((WINDOW, HD), lambda u: (u, 0)),
            pl.BlockSpec((WINDOW, width), lambda u: (u, 0)),
        ]
        + [whole(64, width)] * 4,
        out_specs=pl.BlockSpec((4, 4 * TOK, HD), lambda u: (u, 0, 0)),
        scratch_shapes=[pltpu.VMEM((2 * HD, width), BF16), pltpu.VMEM((WINDOW, 2 * HD), BF16)],
    )(x, arrived, lse, cot, *quarters)


def run_sum(w, got):
    return call(
        sum_kernel,
        (shape((64, HD)),) * 4,
        room=16,
        bytes_accessed=1 << 20,
        in_specs=[SMEM, pl.BlockSpec(memory_space=pltpu.VMEM)],
        out_specs=[pl.BlockSpec(memory_space=pltpu.VMEM)] * 4,
        scratch_shapes=[pltpu.VMEM((4, 64, HD), F32)],
    )(w, got)


def run_spread(pieces):
    return call(
        spread_kernel,
        shape((64, HD), F32),
        room=16,
        in_specs=[pl.BlockSpec(memory_space=pltpu.VMEM)] * 4,
        out_specs=pl.BlockSpec(memory_space=pltpu.VMEM),
    )(*pieces)


def run_unpack(home, query_shape, key_shape):
    return call(
        unpack_kernel,
        (shape(query_shape), shape(key_shape), shape(key_shape)),
        room=16,
        bytes_accessed=2 << 20,
        grid=(4,),
        in_specs=[pl.BlockSpec((2, 4 * TOK, HD), lambda i: (i, 0, 0))],
        out_specs=[
            pl.BlockSpec((1, TOK, 4 * HD), lambda i: (0, 0, i)),
            pl.BlockSpec((1, TOK, 2 * HD), lambda i: (0, 0, i)),
            pl.BlockSpec((1, TOK, 2 * HD), lambda i: (0, 0, i)),
        ],
    )(home)


def local(queries, keys, values, cotangent, out_weight, segment, row_type, pair_index):
    x = lax.axis_index("x").astype(jnp.int32)
    w = lax.axis_index("w").astype(jnp.int32).reshape(1)
    cot = lax.all_gather(cotangent[0], NEAR, axis=0, tiled=True)
    share = lax.dynamic_slice_in_dim(out_weight, 64 * lax.rem(x, 2), 64, axis=0)
    quarter = lax.ppermute(share, AXES, weight_moves())
    quarters = [quarter] + [
        lax.ppermute(quarter, "x", [(i, (i + turn) % 4) for i in range(4)]) for turn in (1, 2, 3)
    ]
    payload = run_pack(queries, keys, values, segment, row_type, pair_index)
    arrived = lax.all_to_all(payload, NEAR, 0, 0)
    out, lse = run_forward(arrived, quarter)
    pieces = run_weight(out, cot, quarters[1:])
    got = lax.all_to_all(pieces, ("x", "yh"), 0, 0)
    back = run_backward(x.reshape(1), arrived, lse, cot, quarters)
    home = lax.all_to_all(back, NEAR, 0, 0)
    sent = [lax.ppermute(part, AXES, piece_moves(turn)) for turn, part in enumerate(run_sum(w, got))]
    weight_grad = run_spread(sent).T
    query_grad, key_grad, value_grad = run_unpack(home, queries.shape, keys.shape)
    return query_grad, key_grad, value_grad, weight_grad


def solution(mesh):
    fine = Mesh(mesh.devices.reshape(SIZES), AXES)
    dp, seq = AXES[:3], AXES[3:]
    in_specs = (
        P(dp, seq, None),
        P(dp, seq, None),
        P(dp, seq, None),
        P(dp, seq, None),
        P(seq, None),
        P(dp, seq),
        P(dp, seq),
        P(dp, None),
    )
    out_specs = (P(dp, seq, None), P(dp, seq, None), P(dp, seq, None), P(seq, dp))
    return jax.shard_map(local, mesh=fine, in_specs=in_specs, out_specs=out_specs, check_vma=False)
```

```python
import itertools

import jax
import jax.numpy as jnp
import numpy as np
from jax import lax
from jax.experimental import pallas as pl
from jax.experimental.pallas import tpu as pltpu
from jax.sharding import Mesh
from jax.sharding import PartitionSpec as P

HD = 128
WINDOW = 512
HALF = WINDOW // 2
TOK = 128
SCALE = HD ** (-0.5)
AXES = ("x", "yh", "yl", "w", "p", "c")
SIZES = (4, 4, 2, 4, 2, 2)
NEAR = ("yl", "p", "c")
CODE = 16
PAY = 4 * TOK + CODE
NONE = 99
F32 = jnp.float32
BF16 = jnp.bfloat16


def place(*index):
    return int(np.ravel_multi_index(index, SIZES))


def devices():
    return itertools.product(*map(range, SIZES))


def weight_moves():
    moves = []
    for x, yh, yl, w, p, c in devices():
        head = 2 * (4 * yl + 2 * p + c) + x // 2
        source = place(2 * (w // 2) + x % 2, yh, w % 2, head // 4, (head // 2) % 2, head % 2)
        moves.append((source, place(x, yh, yl, w, p, c)))
    return moves


def piece_moves(turn):
    moves = []
    for x, yh, yl, w, p, c in devices():
        piece = (w + turn) % 4
        head = 2 * (4 * yl + 2 * p + c) + piece % 2
        owner = place(x, yh, piece // 2, head // 4, (head // 2) % 2, head % 2)
        moves.append((place(x, yh, yl, w, p, c), owner))
    return moves


def dot(left, right, dims):
    return lax.dot_general(left, right, (dims, ((), ())), preferred_element_type=F32)


def pack_kernel(q_ref, k_ref, v_ref, seg_ref, type_ref, pair_ref, out_ref):
    seg = seg_ref[...]
    kind = type_ref[...]
    pair = jnp.zeros_like(seg)
    count = pair_ref.shape[1]
    for s in range(count):
        pair = jnp.where(seg == s, pair_ref[0, s], pair)
    as_query = jnp.where(kind != 0, count + pair, NONE)
    as_key = jnp.where(kind == 0, count + pair, NONE)
    row = lax.broadcasted_iota(jnp.int32, (CODE, TOK), 0)
    code = jnp.where(row == 0, seg, jnp.where(row == 1, as_query, jnp.where(row == 2, as_key, 0)))
    code = code.astype(F32).astype(BF16)
    for g in range(2):
        out_ref[g, 0:TOK, :] = q_ref[0, :, 2 * g * HD : (2 * g + 1) * HD]
        out_ref[g, TOK : 2 * TOK, :] = q_ref[0, :, (2 * g + 1) * HD : (2 * g + 2) * HD]
        out_ref[g, 2 * TOK : 3 * TOK, :] = k_ref[0, :, g * HD : (g + 1) * HD]
        out_ref[g, 3 * TOK : 4 * TOK, :] = v_ref[0, :, g * HD : (g + 1) * HD]
        out_ref[g, 4 * TOK :, :] = code


def rows(pay_ref, first):
    return pay_ref[:, first : first + TOK, :].reshape(WINDOW, HD)


def hot(pay_ref):
    code = jnp.concatenate([pay_ref[i, 4 * TOK :, :] for i in range(4)], axis=1)
    code = code.astype(F32)[0:8]
    slot = lax.broadcasted_iota(jnp.int32, (32, WINDOW), 0).astype(F32)
    same = slot == code[0:1]
    want = jnp.where(same | (slot == code[1:2]), 1.0, 0.0).astype(BF16)
    have = jnp.where(same | (slot == code[2:3]), 1.0, 0.0).astype(BF16)
    return want, have


def visible_block(want, have, lo, ext):
    count = dot(want[:, lo:ext], have[:, :ext], ((0,), (0,)))
    t_pos = lax.broadcasted_iota(jnp.int32, (ext - lo, ext), 0) + lo
    s_pos = lax.broadcasted_iota(jnp.int32, (ext - lo, ext), 1)
    return (count > 0.5) & (s_pos <= t_pos)


def forward_kernel(half_ref, pay_ref, w_ref, out_ref, lse_ref, share_ref):
    @pl.when(pl.program_id(0) == 0)
    def _():
        share_ref[...] = w_ref[pl.ds(pl.multiple_of(half_ref[0] * 64, 64), 64), :]

    key = rows(pay_ref, 2 * TOK)
    value = rows(pay_ref, 3 * TOK)
    want, have = hot(pay_ref)
    lane = lax.broadcasted_iota(jnp.int32, (HALF, HD), 1)
    for block in range(2):
        lo = block * HALF
        ext = lo + HALF
        visible = visible_block(want, have, lo, ext)
        stats = []
        for b in range(2):
            query = rows(pay_ref, b * TOK)[lo:ext]
            scores = dot(query, key[:ext], ((1,), (1,))) * SCALE
            scores = jnp.where(visible, scores, -jnp.inf)
            top = jnp.max(scores, axis=-1, keepdims=True)
            exponent = jnp.exp(scores - top)
            total = jnp.sum(exponent, axis=-1, keepdims=True)
            low = (exponent * (1.0 / total)).astype(BF16)
            out = dot(low, value[:ext], ((1,), (0,)))
            out_ref[b * HD : (b + 1) * HD, lo:ext] = out.T.astype(BF16)
            stats.append(top + jnp.log(total))
        lse_ref[lo:ext, :] = jnp.where(lane == 0, stats[0], stats[1])


def weight_kernel(out_ref, cot_ref, wg_ref):
    total = dot(out_ref[...], cot_ref[...], ((1,), (0,)))
    left = lax.broadcasted_iota(jnp.int32, (64, HD), 1) < 64
    for b in range(2):
        for yh in range(4):
            upper = total[b * HD : b * HD + 64, yh * HD : (yh + 1) * HD]
            lower = total[b * HD + 64 : (b + 1) * HD, yh * HD : (yh + 1) * HD]
            wg_ref[0, 4 * yh + b] = jnp.where(left, upper, pltpu.roll(lower, 64, 1)).astype(BF16)
            wg_ref[0, 4 * yh + 2 + b] = jnp.where(left, pltpu.roll(upper, 64, 1), lower).astype(BF16)


def backward_kernel(x_ref, pay_ref, lse_ref, cot_ref, w0_ref, w1_ref, w2_ref, w3_ref, ret_ref, wbuf, ghbuf):
    @pl.when(pl.program_id(0) == 0)
    def _():
        for turn, quarter in enumerate((w0_ref, w1_ref, w2_ref, w3_ref)):
            first = pl.multiple_of(lax.rem(x_ref[0] + 4 - turn, 4) * 64, 64)
            wbuf[pl.ds(first, 64), :] = quarter[...]

    ghbuf[...] = dot(cot_ref[...], wbuf[...], ((1,), (1,))).astype(BF16)
    key = rows(pay_ref, 2 * TOK)
    value = rows(pay_ref, 3 * TOK)
    want, have = hot(pay_ref)
    kparts = [[None, None], [None, None]]
    vparts = [[None, None], [None, None]]
    for block in range(2):
        lo = block * HALF
        ext = lo + HALF
        visible = visible_block(want, have, lo, ext)
        for b in range(2):
            query = rows(pay_ref, b * TOK)[lo:ext]
            grad = ghbuf[lo:ext, b * HD : (b + 1) * HD]
            scores = dot(query, key[:ext], ((1,), (1,))) * SCALE - lse_ref[lo:ext, b : b + 1]
            attend = jnp.exp(jnp.where(visible, scores, -jnp.inf))
            low = attend.astype(BF16)
            grad_attend = dot(grad, value[:ext], ((1,), (1,)))
            delta = jnp.sum(attend * grad_attend, axis=-1, keepdims=True)
            ds = (attend * (grad_attend - delta) * SCALE).astype(BF16)
            dq = dot(ds, key[:ext], ((1,), (0,))).astype(BF16)
            ret_ref[2 * block : 2 * block + 2, b * TOK : (b + 1) * TOK, :] = dq.reshape(2, TOK, HD)
            dk = dot(ds, query, ((0,), (0,)))
            dv = dot(low, grad, ((0,), (0,)))
            if block == 0:
                kparts[b][0] = dk
                vparts[b][0] = dv
            else:
                kparts[b] = [kparts[b][0] + dk[:HALF], dk[HALF:]]
                vparts[b] = [vparts[b][0] + dv[:HALF], dv[HALF:]]
    for block in range(2):
        for first, parts in ((2 * TOK, kparts), (3 * TOK, vparts)):
            both = parts[0][block].astype(BF16).astype(F32) + parts[1][block].astype(BF16).astype(F32)
            ret_ref[2 * block : 2 * block + 2, first : first + TOK, :] = both.astype(BF16).reshape(2, TOK, HD)


def unpack_kernel(ret_ref, dq_ref, dk_ref, dv_ref):
    for g in range(2):
        dq_ref[0, :, 2 * g * HD : (2 * g + 1) * HD] = ret_ref[g, 0:TOK, :]
        dq_ref[0, :, (2 * g + 1) * HD : (2 * g + 2) * HD] = ret_ref[g, TOK : 2 * TOK, :]
        dk_ref[0, :, g * HD : (g + 1) * HD] = ret_ref[g, 2 * TOK : 3 * TOK, :]
        dv_ref[0, :, g * HD : (g + 1) * HD] = ret_ref[g, 3 * TOK : 4 * TOK, :]


def near_sum_kernel(yh_ref, got_ref, *out_refs):
    for turn, out_ref in enumerate(out_refs):
        first = pl.multiple_of(lax.rem(yh_ref[0] + turn, 4) * 4, 4)
        out_ref[...] = jnp.sum(got_ref[:, pl.ds(first, 4)].astype(F32), axis=0).astype(BF16)


def far_sum_kernel(w_ref, a_ref, b_ref, c_ref, d_ref, *out_refs):
    for turn, out_ref in enumerate(out_refs):
        piece = lax.rem(w_ref[0] + turn, 4)
        total = (a_ref[piece].astype(F32) + b_ref[piece].astype(F32)) + (
            c_ref[piece].astype(F32) + d_ref[piece].astype(F32)
        )
        out_ref[...] = total.astype(BF16)


def spread_kernel(a_ref, b_ref, c_ref, d_ref, out_ref):
    total = (a_ref[...].astype(F32) + b_ref[...].astype(F32)) + (c_ref[...].astype(F32) + d_ref[...].astype(F32))
    out_ref[:, 0:64] = total[:, 0:64].T
    out_ref[:, 64:128] = total[:, 64:128].T


SMEM = pl.BlockSpec(memory_space=pltpu.SMEM)
VMEM = pl.BlockSpec(memory_space=pltpu.VMEM)


def whole(*dims):
    return pl.BlockSpec(dims, lambda *_: (0,) * len(dims))


def call(kernel, out_shape, flops=0, bytes_accessed=0, room=60, **kw):
    return pl.pallas_call(
        kernel,
        out_shape=out_shape,
        compiler_params=pltpu.CompilerParams(vmem_limit_bytes=room << 20),
        cost_estimate=pl.CostEstimate(flops=flops, bytes_accessed=bytes_accessed, transcendentals=0),
        **kw,
    )


def shape(dims, dtype=BF16):
    return jax.ShapeDtypeStruct(dims, dtype)


def run_pack(queries, keys, values, segment, row_type, pair_index):
    return call(
        pack_kernel,
        shape((8, PAY, HD)),
        bytes_accessed=2 << 20,
        grid=(4,),
        in_specs=[
            pl.BlockSpec((1, TOK, 4 * HD), lambda i: (0, 0, i)),
            pl.BlockSpec((1, TOK, 2 * HD), lambda i: (0, 0, i)),
            pl.BlockSpec((1, TOK, 2 * HD), lambda i: (0, 0, i)),
            whole(1, TOK),
            whole(1, TOK),
            SMEM,
        ],
        out_specs=pl.BlockSpec((2, PAY, HD), lambda i: (i, 0, 0)),
    )(queries, keys, values, segment, row_type, pair_index)


def run_forward(half, arrived, out_weight):
    width = out_weight.shape[1]
    return call(
        forward_kernel,
        (shape((2 * HD, 2 * WINDOW)), shape((2 * WINDOW, HD), F32), shape((64, width))),
        flops=4 << 30,
        bytes_accessed=2 << 20,
        grid=(2,),
        in_specs=[SMEM, pl.BlockSpec((4, PAY, HD), lambda u: (u, 0, 0)), whole(HD, width)],
        out_specs=[
            pl.BlockSpec((2 * HD, WINDOW), lambda u: (0, u)),
            pl.BlockSpec((WINDOW, HD), lambda u: (u, 0)),
            whole(64, width),
        ],
    )(half, arrived, out_weight)


def run_weight(out, cot):
    return call(
        weight_kernel,
        shape((4, 16, 64, HD)),
        flops=1 << 30,
        bytes_accessed=6 << 20,
        grid=(4,),
        in_specs=[
            whole(2 * HD, 2 * WINDOW),
            pl.BlockSpec((2 * WINDOW, 512), lambda i: (0, i)),
        ],
        out_specs=pl.BlockSpec((1, 16, 64, HD), lambda i: (i, 0, 0, 0)),
    )(out, cot)


def run_backward(x, arrived, lse, cot, quarters):
    width = cot.shape[1]
    return call(
        backward_kernel,
        shape((8, 4 * TOK, HD)),
        flops=8 << 30,
        bytes_accessed=7 << 20,
        grid=(2,),
        in_specs=[
            SMEM,
            pl.BlockSpec((4, PAY, HD), lambda u: (u, 0, 0)),
            pl.BlockSpec((WINDOW, HD), lambda u: (u, 0)),
            pl.BlockSpec((WINDOW, width), lambda u: (u, 0)),
        ]
        + [whole(64, width)] * 4,
        out_specs=pl.BlockSpec((4, 4 * TOK, HD), lambda u: (u, 0, 0)),
        scratch_shapes=[pltpu.VMEM((2 * HD, width), BF16), pltpu.VMEM((WINDOW, 2 * HD), BF16)],
    )(x, arrived, lse, cot, *quarters)


def run_near_sum(yh, got):
    return call(
        near_sum_kernel,
        (shape((4, 64, HD)),) * 4,
        room=16,
        bytes_accessed=1 << 20,
        in_specs=[SMEM, VMEM],
        out_specs=[VMEM] * 4,
    )(yh, got)


def run_far_sum(w, parts):
    return call(
        far_sum_kernel,
        (shape((64, HD)),) * 4,
        room=16,
        bytes_accessed=1 << 18,
        in_specs=[SMEM] + [VMEM] * 4,
        out_specs=[VMEM] * 4,
    )(w, *parts)


def run_spread(pieces):
    return call(
        spread_kernel,
        shape((64, HD), F32),
        room=16,
        in_specs=[VMEM] * 4,
        out_specs=VMEM,
    )(*pieces)


def run_unpack(home, query_shape, key_shape):
    return call(
        unpack_kernel,
        (shape(query_shape), shape(key_shape), shape(key_shape)),
        room=16,
        bytes_accessed=2 << 20,
        grid=(4,),
        in_specs=[pl.BlockSpec((2, 4 * TOK, HD), lambda i: (i, 0, 0))],
        out_specs=[
            pl.BlockSpec((1, TOK, 4 * HD), lambda i: (0, 0, i)),
            pl.BlockSpec((1, TOK, 2 * HD), lambda i: (0, 0, i)),
            pl.BlockSpec((1, TOK, 2 * HD), lambda i: (0, 0, i)),
        ],
    )(home)


def place_of(axis):
    return lax.axis_index(axis).astype(jnp.int32).reshape(1)


def shifts(count):
    return [[(i, (i + turn) % count) for i in range(count)] for turn in range(1, count)]


def local(queries, keys, values, cotangent, out_weight, segment, row_type, pair_index):
    x = place_of("x")
    cot = lax.all_gather(cotangent[0], NEAR, axis=0, tiled=True)
    payload = run_pack(queries, keys, values, segment, row_type, pair_index)
    arrived = lax.all_to_all(payload, NEAR, 0, 0)
    out, lse, share = run_forward(lax.rem(x, 2), arrived, out_weight)
    quarter = lax.ppermute(share, AXES, weight_moves())
    quarters = [quarter] + [lax.ppermute(quarter, "x", shift) for shift in shifts(4)]
    pieces = run_weight(out, cot)
    got = lax.all_to_all(pieces, "x", 0, 0)
    back = run_backward(x, arrived, lse, cot, quarters)
    home = lax.all_to_all(back, NEAR, 0, 0)
    own, *others = run_near_sum(place_of("yh"), got)
    parts = [own] + [lax.ppermute(part, "yh", shift) for part, shift in zip(others, shifts(4))]
    parts = run_far_sum(place_of("w"), parts)
    sent = [lax.ppermute(part, AXES, piece_moves(turn)) for turn, part in enumerate(parts)]
    weight_grad = run_spread(sent).T
    query_grad, key_grad, value_grad = run_unpack(home, queries.shape, keys.shape)
    return query_grad, key_grad, value_grad, weight_grad


def solution(mesh):
    fine = Mesh(mesh.devices.reshape(SIZES), AXES)
    dp, seq = AXES[:3], AXES[3:]
    in_specs = (
        P(dp, seq, None),
        P(dp, seq, None),
        P(dp, seq, None),
        P(dp, seq, None),
        P(seq, None),
        P(dp, seq),
        P(dp, seq),
        P(dp, None),
    )
    out_specs = (P(dp, seq, None), P(dp, seq, None), P(dp, seq, None), P(seq, dp))
    return jax.shard_map(local, mesh=fine, in_specs=in_specs, out_specs=out_specs, check_vma=False)
```

```python
import itertools

import jax
import jax.numpy as jnp
import numpy as np
from jax import lax
from jax.experimental import pallas as pl
from jax.experimental.pallas import tpu as pltpu
from jax.sharding import Mesh
from jax.sharding import PartitionSpec as P

HD = 128
WINDOW = 512
HALF = WINDOW // 2
TOK = 128
SCALE = HD ** (-0.5)
AXES = ("xh", "xl", "y", "w", "p", "c")
SIZES = (2, 2, 8, 4, 2, 2)
NEAR = ("xl", "p", "c")
FAR = ("xh", "y")
CODE = 16
PAY = 4 * TOK + CODE
NONE = 99
F32 = jnp.float32
BF16 = jnp.bfloat16


def place(*index):
    return int(np.ravel_multi_index(index, SIZES))


def devices():
    return itertools.product(*map(range, SIZES))


def weight_moves():
    moves = []
    for xh, xl, y, w, p, c in devices():
        head = 2 * (4 * xl + 2 * p + c) + y % 2
        source = place(xh, w // 2, 2 * (y // 2) + w % 2, head // 4, (head // 2) % 2, head % 2)
        moves.append((source, place(xh, xl, y, w, p, c)))
    return moves


def piece_moves(turn):
    moves = []
    for xh, xl, y, w, p, c in devices():
        piece = (w + turn) % 4
        head = 2 * (4 * xl + 2 * p + c) + piece % 2
        owner = place(xh, piece // 2, y, head // 4, (head // 2) % 2, head % 2)
        moves.append((place(xh, xl, y, w, p, c), owner))
    return moves


def dot(left, right, dims):
    return lax.dot_general(left, right, (dims, ((), ())), preferred_element_type=F32)


def pack_kernel(q_ref, k_ref, v_ref, seg_ref, type_ref, pair_ref, out_ref):
    seg = seg_ref[...]
    kind = type_ref[...]
    pair = jnp.zeros_like(seg)
    count = pair_ref.shape[1]
    for s in range(count):
        pair = jnp.where(seg == s, pair_ref[0, s], pair)
    as_query = jnp.where(kind != 0, count + pair, NONE)
    as_key = jnp.where(kind == 0, count + pair, NONE)
    row = lax.broadcasted_iota(jnp.int32, (CODE, TOK), 0)
    code = jnp.where(row == 0, seg, jnp.where(row == 1, as_query, jnp.where(row == 2, as_key, 0)))
    code = code.astype(F32).astype(BF16)
    for g in range(2):
        out_ref[g, 0:TOK, :] = q_ref[0, :, 2 * g * HD : (2 * g + 1) * HD]
        out_ref[g, TOK : 2 * TOK, :] = q_ref[0, :, (2 * g + 1) * HD : (2 * g + 2) * HD]
        out_ref[g, 2 * TOK : 3 * TOK, :] = k_ref[0, :, g * HD : (g + 1) * HD]
        out_ref[g, 3 * TOK : 4 * TOK, :] = v_ref[0, :, g * HD : (g + 1) * HD]
        out_ref[g, 4 * TOK :, :] = code


def rows(pay_ref, first):
    return pay_ref[:, first : first + TOK, :].reshape(WINDOW, HD)


def hot(pay_ref):
    code = jnp.concatenate([pay_ref[i, 4 * TOK :, :] for i in range(4)], axis=1)
    code = code.astype(F32)[0:8]
    slot = lax.broadcasted_iota(jnp.int32, (32, WINDOW), 0).astype(F32)
    same = slot == code[0:1]
    want = jnp.where(same | (slot == code[1:2]), 1.0, 0.0).astype(BF16)
    have = jnp.where(same | (slot == code[2:3]), 1.0, 0.0).astype(BF16)
    return want, have


def visible_block(want, have, lo, ext):
    count = dot(want[:, lo:ext], have[:, :ext], ((0,), (0,)))
    t_pos = lax.broadcasted_iota(jnp.int32, (ext - lo, ext), 0) + lo
    s_pos = lax.broadcasted_iota(jnp.int32, (ext - lo, ext), 1)
    return (count > 0.5) & (s_pos <= t_pos)


def forward_kernel(pay_ref, out_ref, lse_ref):
    key = rows(pay_ref, 2 * TOK)
    value = rows(pay_ref, 3 * TOK)
    want, have = hot(pay_ref)
    lane = lax.broadcasted_iota(jnp.int32, (HALF, HD), 1)
    for block in range(2):
        lo = block * HALF
        ext = lo + HALF
        visible = visible_block(want, have, lo, ext)
        stats = []
        for b in range(2):
            query = rows(pay_ref, b * TOK)[lo:ext]
            scores = dot(query, key[:ext], ((1,), (1,))) * SCALE
            scores = jnp.where(visible, scores, -jnp.inf)
            top = jnp.max(scores, axis=-1, keepdims=True)
            exponent = jnp.exp(scores - top)
            total = jnp.sum(exponent, axis=-1, keepdims=True)
            low = (exponent * (1.0 / total)).astype(BF16)
            out = dot(low, value[:ext], ((1,), (0,)))
            out_ref[b * HD : (b + 1) * HD, lo:ext] = out.T.astype(BF16)
            stats.append(top + jnp.log(total))
        lse_ref[lo:ext, :] = jnp.where(lane == 0, stats[0], stats[1])


def weight_kernel(out_ref, cot_ref, after_ref, wg_ref):
    del after_ref
    total = dot(out_ref[...], cot_ref[...], ((1,), (0,)))
    left = lax.broadcasted_iota(jnp.int32, (64, HD), 1) < 64
    for b in range(2):
        for m in range(4):
            upper = total[b * HD : b * HD + 64, m * HD : (m + 1) * HD]
            lower = total[b * HD + 64 : (b + 1) * HD, m * HD : (m + 1) * HD]
            wg_ref[0, 2 * m, 0, b] = jnp.where(left, upper, pltpu.roll(lower, 64, 1)).astype(BF16)
            wg_ref[0, 2 * m + 1, 0, b] = jnp.where(left, pltpu.roll(upper, 64, 1), lower).astype(BF16)


def backward_kernel(pay_ref, lse_ref, cot_ref, w_ref, ret_ref, wbuf, ghbuf):
    @pl.when(pl.program_id(0) == 0)
    def _():
        for y in range(8):
            first = HD * (y % 2) + 32 * (y // 2)
            wbuf[first : first + 32, :] = w_ref[y]

    ghbuf[...] = dot(cot_ref[...], wbuf[...], ((1,), (1,))).astype(BF16)
    key = rows(pay_ref, 2 * TOK)
    value = rows(pay_ref, 3 * TOK)
    want, have = hot(pay_ref)
    kparts = [[None, None], [None, None]]
    vparts = [[None, None], [None, None]]
    for block in range(2):
        lo = block * HALF
        ext = lo + HALF
        visible = visible_block(want, have, lo, ext)
        for b in range(2):
            query = rows(pay_ref, b * TOK)[lo:ext]
            grad = ghbuf[lo:ext, b * HD : (b + 1) * HD]
            scores = dot(query, key[:ext], ((1,), (1,))) * SCALE - lse_ref[lo:ext, b : b + 1]
            attend = jnp.exp(jnp.where(visible, scores, -jnp.inf))
            low = attend.astype(BF16)
            grad_attend = dot(grad, value[:ext], ((1,), (1,)))
            delta = jnp.sum(attend * grad_attend, axis=-1, keepdims=True)
            ds = (attend * (grad_attend - delta) * SCALE).astype(BF16)
            dq = dot(ds, key[:ext], ((1,), (0,))).astype(BF16)
            ret_ref[2 * block : 2 * block + 2, b * TOK : (b + 1) * TOK, :] = dq.reshape(2, TOK, HD)
            dk = dot(ds, query, ((0,), (0,)))
            dv = dot(low, grad, ((0,), (0,)))
            if block == 0:
                kparts[b][0] = dk
                vparts[b][0] = dv
            else:
                kparts[b] = [kparts[b][0] + dk[:HALF], dk[HALF:]]
                vparts[b] = [vparts[b][0] + dv[:HALF], dv[HALF:]]
    for block in range(2):
        for first, parts in ((2 * TOK, kparts), (3 * TOK, vparts)):
            both = parts[0][block].astype(BF16).astype(F32) + parts[1][block].astype(BF16).astype(F32)
            ret_ref[2 * block : 2 * block + 2, first : first + TOK, :] = both.astype(BF16).reshape(2, TOK, HD)


def unpack_kernel(ret_ref, dq_ref, dk_ref, dv_ref):
    for g in range(2):
        dq_ref[0, :, 2 * g * HD : (2 * g + 1) * HD] = ret_ref[g, 0:TOK, :]
        dq_ref[0, :, (2 * g + 1) * HD : (2 * g + 2) * HD] = ret_ref[g, TOK : 2 * TOK, :]
        dk_ref[0, :, g * HD : (g + 1) * HD] = ret_ref[g, 2 * TOK : 3 * TOK, :]
        dv_ref[0, :, g * HD : (g + 1) * HD] = ret_ref[g, 3 * TOK : 4 * TOK, :]


def sum_kernel(w_ref, got_ref, out0_ref, out1_ref, out2_ref, out3_ref, total):
    total[...] = jnp.sum(got_ref[...].astype(F32), axis=0)
    for turn, out_ref in enumerate((out0_ref, out1_ref, out2_ref, out3_ref)):
        out_ref[...] = total[lax.rem(w_ref[0] + turn, 4)].astype(BF16)


def spread_kernel(a_ref, b_ref, c_ref, d_ref, out_ref):
    total = (a_ref[...].astype(F32) + b_ref[...].astype(F32)) + (c_ref[...].astype(F32) + d_ref[...].astype(F32))
    out_ref[:, 0:64] = total[:, 0:64].T
    out_ref[:, 64:128] = total[:, 64:128].T


SMEM = pl.BlockSpec(memory_space=pltpu.SMEM)
ANY = pl.BlockSpec(memory_space=pl.ANY)


def whole(*dims):
    return pl.BlockSpec(dims, lambda *_: (0,) * len(dims))


def call(kernel, out_shape, flops=0, bytes_accessed=0, room=60, **kw):
    return pl.pallas_call(
        kernel,
        out_shape=out_shape,
        compiler_params=pltpu.CompilerParams(vmem_limit_bytes=room << 20),
        cost_estimate=pl.CostEstimate(flops=flops, bytes_accessed=bytes_accessed, transcendentals=0),
        **kw,
    )


def shape(dims, dtype=BF16):
    return jax.ShapeDtypeStruct(dims, dtype)


def run_pack(queries, keys, values, segment, row_type, pair_index):
    return call(
        pack_kernel,
        shape((8, PAY, HD)),
        bytes_accessed=2 << 20,
        grid=(4,),
        in_specs=[
            pl.BlockSpec((1, TOK, 4 * HD), lambda i: (0, 0, i)),
            pl.BlockSpec((1, TOK, 2 * HD), lambda i: (0, 0, i)),
            pl.BlockSpec((1, TOK, 2 * HD), lambda i: (0, 0, i)),
            whole(1, TOK),
            whole(1, TOK),
            SMEM,
        ],
        out_specs=pl.BlockSpec((2, PAY, HD), lambda i: (i, 0, 0)),
    )(queries, keys, values, segment, row_type, pair_index)


def run_forward(arrived):
    return call(
        forward_kernel,
        (shape((2 * HD, 2 * WINDOW)), shape((2 * WINDOW, HD), F32)),
        flops=4 << 30,
        bytes_accessed=2 << 20,
        grid=(2,),
        in_specs=[pl.BlockSpec((4, PAY, HD), lambda u: (u, 0, 0))],
        out_specs=[
            pl.BlockSpec((2 * HD, WINDOW), lambda u: (0, u)),
            pl.BlockSpec((WINDOW, HD), lambda u: (u, 0)),
        ],
    )(arrived)


def run_weight(out, cot, after):
    return call(
        weight_kernel,
        shape((2, 8, 2, 2, 64, HD)),
        flops=1 << 30,
        bytes_accessed=6 << 20,
        grid=(4,),
        in_specs=[
            whole(2 * HD, 2 * WINDOW),
            pl.BlockSpec((2 * WINDOW, 512), lambda i: (0, i)),
        ]
        + [ANY],
        out_specs=pl.BlockSpec((1, 8, 1, 2, 64, HD), lambda i: (i // 2, 0, i % 2, 0, 0, 0)),
    )(out, cot, after).reshape(16, 4, 64, HD)


def run_backward(arrived, lse, cot, weight):
    width = cot.shape[1]
    return call(
        backward_kernel,
        shape((8, 4 * TOK, HD)),
        flops=8 << 30,
        bytes_accessed=7 << 20,
        grid=(2,),
        in_specs=[
            pl.BlockSpec((4, PAY, HD), lambda u: (u, 0, 0)),
            pl.BlockSpec((WINDOW, HD), lambda u: (u, 0)),
            pl.BlockSpec((WINDOW, width), lambda u: (u, 0)),
            whole(8, 32, width),
        ],
        out_specs=pl.BlockSpec((4, 4 * TOK, HD), lambda u: (u, 0, 0)),
        scratch_shapes=[pltpu.VMEM((2 * HD, width), BF16), pltpu.VMEM((WINDOW, 2 * HD), BF16)],
    )(arrived, lse, cot, weight)


def run_sum(w, got):
    return call(
        sum_kernel,
        (shape((64, HD)),) * 4,
        room=16,
        bytes_accessed=1 << 20,
        in_specs=[SMEM, pl.BlockSpec(memory_space=pltpu.VMEM)],
        out_specs=[pl.BlockSpec(memory_space=pltpu.VMEM)] * 4,
        scratch_shapes=[pltpu.VMEM((4, 64, HD), F32)],
    )(w, got)


def run_spread(pieces):
    return call(
        spread_kernel,
        shape((64, HD), F32),
        room=16,
        in_specs=[pl.BlockSpec(memory_space=pltpu.VMEM)] * 4,
        out_specs=pl.BlockSpec(memory_space=pltpu.VMEM),
    )(*pieces)


def run_unpack(home, query_shape, key_shape):
    return call(
        unpack_kernel,
        (shape(query_shape), shape(key_shape), shape(key_shape)),
        room=16,
        bytes_accessed=2 << 20,
        grid=(4,),
        in_specs=[pl.BlockSpec((2, 4 * TOK, HD), lambda i: (i, 0, 0))],
        out_specs=[
            pl.BlockSpec((1, TOK, 4 * HD), lambda i: (0, 0, i)),
            pl.BlockSpec((1, TOK, 2 * HD), lambda i: (0, 0, i)),
            pl.BlockSpec((1, TOK, 2 * HD), lambda i: (0, 0, i)),
        ],
    )(home)


def local(queries, keys, values, cotangent, out_weight, segment, row_type, pair_index):
    width = out_weight.shape[1]
    y = lax.axis_index("y").astype(jnp.int32)
    w = lax.axis_index("w").astype(jnp.int32).reshape(1)
    share = lax.dynamic_slice_in_dim(out_weight, 32 * lax.div(y, 2), 32, axis=0)
    eighth = lax.ppermute(share, AXES, weight_moves())
    cot = lax.all_gather(cotangent[0], NEAR, axis=0, tiled=True)
    payload = run_pack(queries, keys, values, segment, row_type, pair_index)
    arrived = lax.all_to_all(payload, NEAR, 0, 0)
    weight = lax.all_to_all(jnp.broadcast_to(eighth[None], (8, 32, width)), "y", 0, 0)
    out, lse = run_forward(arrived)
    pieces = run_weight(out, cot, weight)
    got = lax.all_to_all(pieces, FAR, 0, 0)
    back = run_backward(arrived, lse, cot, weight)
    home = lax.all_to_all(back, NEAR, 0, 0)
    sent = [lax.ppermute(part, AXES, piece_moves(turn)) for turn, part in enumerate(run_sum(w, got))]
    weight_grad = run_spread(sent).T
    query_grad, key_grad, value_grad = run_unpack(home, queries.shape, keys.shape)
    return query_grad, key_grad, value_grad, weight_grad


def solution(mesh):
    fine = Mesh(mesh.devices.reshape(SIZES), AXES)
    dp, seq = AXES[:3], AXES[3:]
    in_specs = (
        P(dp, seq, None),
        P(dp, seq, None),
        P(dp, seq, None),
        P(dp, seq, None),
        P(seq, None),
        P(dp, seq),
        P(dp, seq),
        P(dp, None),
    )
    out_specs = (P(dp, seq, None), P(dp, seq, None), P(dp, seq, None), P(seq, dp))
    return jax.shard_map(local, mesh=fine, in_specs=in_specs, out_specs=out_specs, check_vma=False)
```

```python
import itertools

import jax
import jax.numpy as jnp
import numpy as np
from jax import lax
from jax.experimental import pallas as pl
from jax.experimental.pallas import tpu as pltpu
from jax.sharding import Mesh
from jax.sharding import PartitionSpec as P

HD = 128
WINDOW = 512
HALF = WINDOW // 2
TOK = 128
SCALE = HD ** (-0.5)
AXES = ("x", "yh", "yl", "w", "p", "c")
SIZES = (4, 4, 2, 4, 2, 2)
NEAR = ("yl", "p", "c")
FAR = ("x", "yh")
CODE = 16
PAY = 4 * TOK + CODE
NONE = 99
F32 = jnp.float32
BF16 = jnp.bfloat16


def place(*index):
    return int(np.ravel_multi_index(index, SIZES))


def devices():
    return itertools.product(*map(range, SIZES))


def key_head(yl, p, c):
    return yl + 2 * p + 4 * c


def weight_moves():
    moves = []
    for x, yh, yl, w, p, c in devices():
        head = 2 * key_head(yl, p, c) + x // 2
        source = place(2 * (w // 2) + x % 2, yh, (w + head) % 2, head // 4, (head // 2) % 2, head % 2)
        moves.append((source, place(x, yh, yl, w, p, c)))
    return moves


def piece_moves(turn):
    moves = []
    for x, yh, yl, w, p, c in devices():
        piece = (w + turn) % 4
        head = 2 * key_head(yl, p, c) + piece % 2
        owner = place(x, yh, piece // 2, head // 4, (head // 2) % 2, head % 2)
        moves.append((place(x, yh, yl, w, p, c), owner))
    return moves


def dot(left, right, dims):
    return lax.dot_general(left, right, (dims, ((), ())), preferred_element_type=F32)


def pack_kernel(q_ref, k_ref, v_ref, seg_ref, type_ref, pair_ref, out_ref):
    seg = seg_ref[...]
    kind = type_ref[...]
    pair = jnp.zeros_like(seg)
    count = pair_ref.shape[1]
    for s in range(count):
        pair = jnp.where(seg == s, pair_ref[0, s], pair)
    as_query = jnp.where(kind != 0, count + pair, NONE)
    as_key = jnp.where(kind == 0, count + pair, NONE)
    row = lax.broadcasted_iota(jnp.int32, (CODE, TOK), 0)
    code = jnp.where(row == 0, seg, jnp.where(row == 1, as_query, jnp.where(row == 2, as_key, 0)))
    code = code.astype(F32).astype(BF16)
    for g in range(2):
        out_ref[g, 0, 0:TOK, :] = q_ref[0, :, 2 * g * HD : (2 * g + 1) * HD]
        out_ref[g, 0, TOK : 2 * TOK, :] = q_ref[0, :, (2 * g + 1) * HD : (2 * g + 2) * HD]
        out_ref[g, 0, 2 * TOK : 3 * TOK, :] = k_ref[0, :, g * HD : (g + 1) * HD]
        out_ref[g, 0, 3 * TOK : 4 * TOK, :] = v_ref[0, :, g * HD : (g + 1) * HD]
        out_ref[g, 0, 4 * TOK :, :] = code


def rows(pay_ref, first):
    return pay_ref[:, first : first + TOK, :].reshape(WINDOW, HD)


def hot(pay_ref):
    code = jnp.concatenate([pay_ref[i, 4 * TOK :, :] for i in range(4)], axis=1)
    code = code.astype(F32)[0:8]
    slot = lax.broadcasted_iota(jnp.int32, (32, WINDOW), 0).astype(F32)
    same = slot == code[0:1]
    want = jnp.where(same | (slot == code[1:2]), 1.0, 0.0).astype(BF16)
    have = jnp.where(same | (slot == code[2:3]), 1.0, 0.0).astype(BF16)
    return want, have


def visible_block(want, have, lo, ext):
    count = dot(want[:, lo:ext], have[:, :ext], ((0,), (0,)))
    t_pos = lax.broadcasted_iota(jnp.int32, (ext - lo, ext), 0) + lo
    s_pos = lax.broadcasted_iota(jnp.int32, (ext - lo, ext), 1)
    return (count > 0.5) & (s_pos <= t_pos)


def forward_kernel(pay_ref, out_ref, lse_ref):
    key = rows(pay_ref, 2 * TOK)
    value = rows(pay_ref, 3 * TOK)
    want, have = hot(pay_ref)
    lane = lax.broadcasted_iota(jnp.int32, (HALF, HD), 1)
    for block in range(2):
        lo = block * HALF
        ext = lo + HALF
        visible = visible_block(want, have, lo, ext)
        stats = []
        for b in range(2):
            query = rows(pay_ref, b * TOK)[lo:ext]
            scores = dot(query, key[:ext], ((1,), (1,))) * SCALE
            scores = jnp.where(visible, scores, -jnp.inf)
            top = jnp.max(scores, axis=-1, keepdims=True)
            exponent = jnp.exp(scores - top)
            total = jnp.sum(exponent, axis=-1, keepdims=True)
            low = (exponent * (1.0 / total)).astype(BF16)
            out = dot(low, value[:ext], ((1,), (0,)))
            out_ref[b * HD : (b + 1) * HD, lo:ext] = out.T.astype(BF16)
            stats.append(top + jnp.log(total))
        lse_ref[lo:ext, :] = jnp.where(lane == 0, stats[0], stats[1])


def weight_kernel(out_ref, cot_ref, wg_ref):
    total = dot(out_ref[...], cot_ref[...], ((1,), (0,)))
    left = lax.broadcasted_iota(jnp.int32, (64, HD), 1) < 64
    for b in range(2):
        for yh in range(4):
            upper = total[b * HD : b * HD + 64, yh * HD : (yh + 1) * HD]
            lower = total[b * HD + 64 : (b + 1) * HD, yh * HD : (yh + 1) * HD]
            wg_ref[yh, b] = jnp.where(left, upper, pltpu.roll(lower, 64, 1)).astype(BF16)
            wg_ref[yh, 2 + b] = jnp.where(left, pltpu.roll(upper, 64, 1), lower).astype(BF16)


def backward_kernel(pay_ref, lse_ref, cot_ref, w_ref, ret_ref, ghbuf):
    ghbuf[...] = dot(cot_ref[...], w_ref[...], ((1,), (1,))).astype(BF16)
    key = rows(pay_ref, 2 * TOK)
    value = rows(pay_ref, 3 * TOK)
    want, have = hot(pay_ref)
    kparts = [[None, None], [None, None]]
    vparts = [[None, None], [None, None]]
    for block in range(2):
        lo = block * HALF
        ext = lo + HALF
        visible = visible_block(want, have, lo, ext)
        for b in range(2):
            query = rows(pay_ref, b * TOK)[lo:ext]
            grad = ghbuf[lo:ext, b * HD : (b + 1) * HD]
            scores = dot(query, key[:ext], ((1,), (1,))) * SCALE - lse_ref[lo:ext, b : b + 1]
            attend = jnp.exp(jnp.where(visible, scores, -jnp.inf))
            low = attend.astype(BF16)
            grad_attend = dot(grad, value[:ext], ((1,), (1,)))
            delta = jnp.sum(attend * grad_attend, axis=-1, keepdims=True)
            ds = (attend * (grad_attend - delta) * SCALE).astype(BF16)
            dq = dot(ds, key[:ext], ((1,), (0,))).astype(BF16)
            ret_ref[2 * block : 2 * block + 2, b * TOK : (b + 1) * TOK, :] = dq.reshape(2, TOK, HD)
            dk = dot(ds, query, ((0,), (0,)))
            dv = dot(low, grad, ((0,), (0,)))
            if block == 0:
                kparts[b][0] = dk
                vparts[b][0] = dv
            else:
                kparts[b] = [kparts[b][0] + dk[:HALF], dk[HALF:]]
                vparts[b] = [vparts[b][0] + dv[:HALF], dv[HALF:]]
    for block in range(2):
        for first, parts in ((2 * TOK, kparts), (3 * TOK, vparts)):
            both = parts[0][block].astype(BF16).astype(F32) + parts[1][block].astype(BF16).astype(F32)
            ret_ref[2 * block : 2 * block + 2, first : first + TOK, :] = both.astype(BF16).reshape(2, TOK, HD)


def unpack_kernel(ret_ref, dq_ref, dk_ref, dv_ref):
    for g in range(2):
        dq_ref[0, :, 2 * g * HD : (2 * g + 1) * HD] = ret_ref[g, 0, 0:TOK, :]
        dq_ref[0, :, (2 * g + 1) * HD : (2 * g + 2) * HD] = ret_ref[g, 0, TOK : 2 * TOK, :]
        dk_ref[0, :, g * HD : (g + 1) * HD] = ret_ref[g, 0, 2 * TOK : 3 * TOK, :]
        dv_ref[0, :, g * HD : (g + 1) * HD] = ret_ref[g, 0, 3 * TOK : 4 * TOK, :]


def sum_kernel(w_ref, got_ref, out0_ref, out1_ref, out2_ref, out3_ref, total):
    total[...] = jnp.sum(got_ref[...].astype(F32), axis=0)
    for turn, out_ref in enumerate((out0_ref, out1_ref, out2_ref, out3_ref)):
        out_ref[...] = total[lax.rem(w_ref[0] + turn, 4)].astype(BF16)


def spread_kernel(a_ref, b_ref, c_ref, d_ref, out_ref):
    total = (a_ref[...].astype(F32) + b_ref[...].astype(F32)) + (c_ref[...].astype(F32) + d_ref[...].astype(F32))
    out_ref[:, 0:64] = total[:, 0:64].T
    out_ref[:, 64:128] = total[:, 64:128].T


SMEM = pl.BlockSpec(memory_space=pltpu.SMEM)


def whole(*dims):
    return pl.BlockSpec(dims, lambda *_: (0,) * len(dims))


def pair_of_heads(i):
    return 0, 2 * (i % 2) + i // 2, 0, 0


def call(kernel, out_shape, flops=0, bytes_accessed=0, room=60, **kw):
    return pl.pallas_call(
        kernel,
        out_shape=out_shape,
        compiler_params=pltpu.CompilerParams(vmem_limit_bytes=room << 20),
        cost_estimate=pl.CostEstimate(flops=flops, bytes_accessed=bytes_accessed, transcendentals=0),
        **kw,
    )


def shape(dims, dtype=BF16):
    return jax.ShapeDtypeStruct(dims, dtype)


def run_pack(queries, keys, values, segment, row_type, pair_index):
    return call(
        pack_kernel,
        shape((2, 4, PAY, HD)),
        bytes_accessed=2 << 20,
        grid=(4,),
        in_specs=[
            pl.BlockSpec((1, TOK, 4 * HD), lambda i: (0, 0, i)),
            pl.BlockSpec((1, TOK, 2 * HD), lambda i: (0, 0, i)),
            pl.BlockSpec((1, TOK, 2 * HD), lambda i: (0, 0, i)),
            whole(1, TOK),
            whole(1, TOK),
            SMEM,
        ],
        out_specs=pl.BlockSpec((2, 1, PAY, HD), pair_of_heads),
    )(queries, keys, values, segment, row_type, pair_index).reshape(8, PAY, HD)


def run_forward(arrived):
    return call(
        forward_kernel,
        (shape((2 * HD, 2 * WINDOW)), shape((2 * WINDOW, HD), F32)),
        flops=4 << 30,
        bytes_accessed=2 << 20,
        grid=(2,),
        in_specs=[pl.BlockSpec((4, PAY, HD), lambda u: (u, 0, 0))],
        out_specs=[
            pl.BlockSpec((2 * HD, WINDOW), lambda u: (0, u)),
            pl.BlockSpec((WINDOW, HD), lambda u: (u, 0)),
        ],
    )(arrived)


def run_weight(out, cot):
    return call(
        weight_kernel,
        shape((16, 4, 64, HD)),
        flops=1 << 30,
        bytes_accessed=6 << 20,
        grid=(4,),
        in_specs=[
            whole(2 * HD, 2 * WINDOW),
            pl.BlockSpec((2 * WINDOW, 512), lambda i: (0, i)),
        ],
        out_specs=pl.BlockSpec((4, 4, 64, HD), lambda i: (i, 0, 0, 0)),
    )(out, cot)


def run_backward(arrived, lse, cot, weight):
    width = cot.shape[1]
    return call(
        backward_kernel,
        shape((8, 4 * TOK, HD)),
        flops=8 << 30,
        bytes_accessed=7 << 20,
        grid=(2,),
        in_specs=[
            pl.BlockSpec((4, PAY, HD), lambda u: (u, 0, 0)),
            pl.BlockSpec((WINDOW, HD), lambda u: (u, 0)),
            pl.BlockSpec((WINDOW, width), lambda u: (u, 0)),
            whole(2 * HD, width),
        ],
        out_specs=pl.BlockSpec((4, 4 * TOK, HD), lambda u: (u, 0, 0)),
        scratch_shapes=[pltpu.VMEM((WINDOW, 2 * HD), BF16)],
    )(arrived, lse, cot, weight)


def run_sum(w, got):
    return call(
        sum_kernel,
        (shape((64, HD)),) * 4,
        room=16,
        bytes_accessed=1 << 20,
        in_specs=[SMEM, pl.BlockSpec(memory_space=pltpu.VMEM)],
        out_specs=[pl.BlockSpec(memory_space=pltpu.VMEM)] * 4,
        scratch_shapes=[pltpu.VMEM((4, 64, HD), F32)],
    )(w, got)


def run_spread(pieces):
    return call(
        spread_kernel,
        shape((64, HD), F32),
        room=16,
        in_specs=[pl.BlockSpec(memory_space=pltpu.VMEM)] * 4,
        out_specs=pl.BlockSpec(memory_space=pltpu.VMEM),
    )(*pieces)


def run_unpack(home, query_shape, key_shape):
    return call(
        unpack_kernel,
        (shape(query_shape), shape(key_shape), shape(key_shape)),
        room=16,
        bytes_accessed=2 << 20,
        grid=(4,),
        in_specs=[pl.BlockSpec((2, 1, 4 * TOK, HD), pair_of_heads)],
        out_specs=[
            pl.BlockSpec((1, TOK, 4 * HD), lambda i: (0, 0, i)),
            pl.BlockSpec((1, TOK, 2 * HD), lambda i: (0, 0, i)),
            pl.BlockSpec((1, TOK, 2 * HD), lambda i: (0, 0, i)),
        ],
    )(home.reshape(2, 4, 4 * TOK, HD))


def local(queries, keys, values, cotangent, out_weight, segment, row_type, pair_index):
    x = lax.axis_index("x").astype(jnp.int32)
    w = lax.axis_index("w").astype(jnp.int32).reshape(1)
    share = lax.dynamic_slice_in_dim(out_weight, 64 * lax.rem(x, 2), 64, axis=0)
    quarter = lax.ppermute(share, AXES, weight_moves())
    cot = lax.all_gather(cotangent[0], NEAR, axis=0, tiled=True)
    payload = run_pack(queries, keys, values, segment, row_type, pair_index)
    arrived = lax.all_to_all(payload, NEAR, 0, 0)
    weight = lax.all_gather(quarter, "x", axis=0, tiled=True)
    out, lse = run_forward(arrived)
    pieces = run_weight(out, cot)
    got = lax.all_to_all(pieces, FAR, 0, 0)
    back = run_backward(arrived, lse, cot, weight)
    home = lax.all_to_all(back, NEAR, 0, 0)
    sent = [lax.ppermute(part, AXES, piece_moves(turn)) for turn, part in enumerate(run_sum(w, got))]
    weight_grad = run_spread(sent).T
    query_grad, key_grad, value_grad = run_unpack(home, queries.shape, keys.shape)
    return query_grad, key_grad, value_grad, weight_grad


def solution(mesh):
    fine = Mesh(mesh.devices.reshape(SIZES), AXES)
    dp, seq = AXES[:3], AXES[3:]
    in_specs = (
        P(dp, seq, None),
        P(dp, seq, None),
        P(dp, seq, None),
        P(dp, seq, None),
        P(seq, None),
        P(dp, seq),
        P(dp, seq),
        P(dp, None),
    )
    out_specs = (P(dp, seq, None), P(dp, seq, None), P(dp, seq, None), P(seq, dp))
    return jax.shard_map(local, mesh=fine, in_specs=in_specs, out_specs=out_specs, check_vma=False)
```

```python
import itertools

import jax
import jax.numpy as jnp
import numpy as np
from jax import lax
from jax.experimental import pallas as pl
from jax.experimental.pallas import tpu as pltpu
from jax.sharding import Mesh
from jax.sharding import PartitionSpec as P

HD = 128
WINDOW = 512
HALF = WINDOW // 2
TOK = 128
SCALE = HD ** (-0.5)
AXES = ("x", "ya", "yb", "yl", "w", "p", "c")
SIZES = (4, 2, 2, 2, 4, 2, 2)
NEAR = ("yl", "p", "c")
FAR = ("x", "ya", "yb")
SHARE = ("x", "yb")
CODE = 16
PAY = 4 * TOK + CODE
NONE = 99
F32 = jnp.float32
BF16 = jnp.bfloat16


def place(*index):
    return int(np.ravel_multi_index(index, SIZES))


def devices():
    return itertools.product(*map(range, SIZES))


def key_head(yl, p, c):
    return yl + 2 * p + 4 * c


def weight_moves():
    moves = []
    for x, ya, yb, yl, w, p, c in devices():
        head = 2 * key_head(yl, p, c) + x // 2
        source = place(2 * (w // 2) + x % 2, ya, yb, (w + head) % 2, head // 4, (head // 2) % 2, head % 2)
        moves.append((source, place(x, ya, yb, yl, w, p, c)))
    return moves


def piece_moves(turn):
    moves = []
    for x, ya, yb, yl, w, p, c in devices():
        piece = (w + turn) % 4
        head = 2 * key_head(yl, p, c) + piece % 2
        owner = place(x, ya, yb, piece // 2, head // 4, (head // 2) % 2, head % 2)
        moves.append((place(x, ya, yb, yl, w, p, c), owner))
    return moves


def dot(left, right, dims):
    return lax.dot_general(left, right, (dims, ((), ())), preferred_element_type=F32)


def pack_kernel(q_ref, k_ref, v_ref, seg_ref, type_ref, pair_ref, out_ref):
    seg = seg_ref[...]
    kind = type_ref[...]
    pair = jnp.zeros_like(seg)
    count = pair_ref.shape[1]
    for s in range(count):
        pair = jnp.where(seg == s, pair_ref[0, s], pair)
    as_query = jnp.where(kind != 0, count + pair, NONE)
    as_key = jnp.where(kind == 0, count + pair, NONE)
    row = lax.broadcasted_iota(jnp.int32, (CODE, TOK), 0)
    code = jnp.where(row == 0, seg, jnp.where(row == 1, as_query, jnp.where(row == 2, as_key, 0)))
    code = code.astype(F32).astype(BF16)
    for g in range(2):
        out_ref[g, 0, 0:TOK, :] = q_ref[0, :, 2 * g * HD : (2 * g + 1) * HD]
        out_ref[g, 0, TOK : 2 * TOK, :] = q_ref[0, :, (2 * g + 1) * HD : (2 * g + 2) * HD]
        out_ref[g, 0, 2 * TOK : 3 * TOK, :] = k_ref[0, :, g * HD : (g + 1) * HD]
        out_ref[g, 0, 3 * TOK : 4 * TOK, :] = v_ref[0, :, g * HD : (g + 1) * HD]
        out_ref[g, 0, 4 * TOK :, :] = code


def rows(pay_ref, first):
    return pay_ref[:, first : first + TOK, :].reshape(WINDOW, HD)


def hot(pay_ref):
    code = jnp.concatenate([pay_ref[i, 4 * TOK :, :] for i in range(4)], axis=1)
    code = code.astype(F32)[0:8]
    slot = lax.broadcasted_iota(jnp.int32, (32, WINDOW), 0).astype(F32)
    same = slot == code[0:1]
    want = jnp.where(same | (slot == code[1:2]), 1.0, 0.0).astype(BF16)
    have = jnp.where(same | (slot == code[2:3]), 1.0, 0.0).astype(BF16)
    return want, have


def visible_block(want, have, lo, ext):
    count = dot(want[:, lo:ext], have[:, :ext], ((0,), (0,)))
    t_pos = lax.broadcasted_iota(jnp.int32, (ext - lo, ext), 0) + lo
    s_pos = lax.broadcasted_iota(jnp.int32, (ext - lo, ext), 1)
    return (count > 0.5) & (s_pos <= t_pos)


def forward_kernel(pay_ref, out_ref, lse_ref):
    key = rows(pay_ref, 2 * TOK)
    value = rows(pay_ref, 3 * TOK)
    want, have = hot(pay_ref)
    lane = lax.broadcasted_iota(jnp.int32, (HALF, HD), 1)
    for block in range(2):
        lo = block * HALF
        ext = lo + HALF
        visible = visible_block(want, have, lo, ext)
        stats = []
        for b in range(2):
            query = rows(pay_ref, b * TOK)[lo:ext]
            scores = dot(query, key[:ext], ((1,), (1,))) * SCALE
            scores = jnp.where(visible, scores, -jnp.inf)
            top = jnp.max(scores, axis=-1, keepdims=True)
            exponent = jnp.exp(scores - top)
            total = jnp.sum(exponent, axis=-1, keepdims=True)
            low = (exponent * (1.0 / total)).astype(BF16)
            out = dot(low, value[:ext], ((1,), (0,)))
            out_ref[b * HD : (b + 1) * HD, lo:ext] = out.T.astype(BF16)
            stats.append(top + jnp.log(total))
        lse_ref[lo:ext, :] = jnp.where(lane == 0, stats[0], stats[1])


def weight_kernel(out_ref, cot_ref, after_ref, wg_ref):
    del after_ref
    total = dot(out_ref[...], cot_ref[...], ((1,), (0,)))
    left = lax.broadcasted_iota(jnp.int32, (64, HD), 1) < 64
    for b in range(2):
        for m in range(8):
            upper = total[b * HD : b * HD + 64, m * HD : (m + 1) * HD]
            lower = total[b * HD + 64 : (b + 1) * HD, m * HD : (m + 1) * HD]
            wg_ref[m, b] = jnp.where(left, upper, pltpu.roll(lower, 64, 1)).astype(BF16)
            wg_ref[m, 2 + b] = jnp.where(left, pltpu.roll(upper, 64, 1), lower).astype(BF16)


def backward_kernel(pay_ref, lse_ref, cot_ref, w_ref, ret_ref, ghbuf):
    ghbuf[...] = dot(cot_ref[...], w_ref[...], ((1,), (1,))).astype(BF16)
    key = rows(pay_ref, 2 * TOK)
    value = rows(pay_ref, 3 * TOK)
    want, have = hot(pay_ref)
    kparts = [[None, None], [None, None]]
    vparts = [[None, None], [None, None]]
    for block in range(2):
        lo = block * HALF
        ext = lo + HALF
        visible = visible_block(want, have, lo, ext)
        for b in range(2):
            query = rows(pay_ref, b * TOK)[lo:ext]
            grad = ghbuf[lo:ext, b * HD : (b + 1) * HD]
            scores = dot(query, key[:ext], ((1,), (1,))) * SCALE - lse_ref[lo:ext, b : b + 1]
            attend = jnp.exp(jnp.where(visible, scores, -jnp.inf))
            low = attend.astype(BF16)
            grad_attend = dot(grad, value[:ext], ((1,), (1,)))
            delta = jnp.sum(attend * grad_attend, axis=-1, keepdims=True)
            ds = (attend * (grad_attend - delta) * SCALE).astype(BF16)
            dq = dot(ds, key[:ext], ((1,), (0,))).astype(BF16)
            ret_ref[2 * block : 2 * block + 2, b * TOK : (b + 1) * TOK, :] = dq.reshape(2, TOK, HD)
            dk = dot(ds, query, ((0,), (0,)))
            dv = dot(low, grad, ((0,), (0,)))
            if block == 0:
                kparts[b][0] = dk
                vparts[b][0] = dv
            else:
                kparts[b] = [kparts[b][0] + dk[:HALF], dk[HALF:]]
                vparts[b] = [vparts[b][0] + dv[:HALF], dv[HALF:]]
    for block in range(2):
        for first, parts in ((2 * TOK, kparts), (3 * TOK, vparts)):
            both = parts[0][block].astype(BF16).astype(F32) + parts[1][block].astype(BF16).astype(F32)
            ret_ref[2 * block : 2 * block + 2, first : first + TOK, :] = both.astype(BF16).reshape(2, TOK, HD)


def unpack_kernel(ret_ref, dq_ref, dk_ref, dv_ref):
    for g in range(2):
        dq_ref[0, :, 2 * g * HD : (2 * g + 1) * HD] = ret_ref[g, 0, 0:TOK, :]
        dq_ref[0, :, (2 * g + 1) * HD : (2 * g + 2) * HD] = ret_ref[g, 0, TOK : 2 * TOK, :]
        dk_ref[0, :, g * HD : (g + 1) * HD] = ret_ref[g, 0, 2 * TOK : 3 * TOK, :]
        dv_ref[0, :, g * HD : (g + 1) * HD] = ret_ref[g, 0, 3 * TOK : 4 * TOK, :]


def sum_kernel(w_ref, got_ref, out0_ref, out1_ref, out2_ref, out3_ref, total):
    total[...] = jnp.sum(got_ref[...].astype(F32), axis=0)
    for turn, out_ref in enumerate((out0_ref, out1_ref, out2_ref, out3_ref)):
        out_ref[...] = total[lax.rem(w_ref[0] + turn, 4)].astype(BF16)


def spread_kernel(a_ref, b_ref, c_ref, d_ref, out_ref):
    total = (a_ref[...].astype(F32) + b_ref[...].astype(F32)) + (c_ref[...].astype(F32) + d_ref[...].astype(F32))
    out_ref[:, 0:64] = total[:, 0:64].T
    out_ref[:, 64:128] = total[:, 64:128].T


SMEM = pl.BlockSpec(memory_space=pltpu.SMEM)


def whole(*dims):
    return pl.BlockSpec(dims, lambda *_: (0,) * len(dims))


def pair_of_heads(i):
    return 0, 2 * (i % 2) + i // 2, 0, 0


def call(kernel, out_shape, flops=0, bytes_accessed=0, room=60, **kw):
    return pl.pallas_call(
        kernel,
        out_shape=out_shape,
        compiler_params=pltpu.CompilerParams(vmem_limit_bytes=room << 20),
        cost_estimate=pl.CostEstimate(flops=flops, bytes_accessed=bytes_accessed, transcendentals=0),
        **kw,
    )


def shape(dims, dtype=BF16):
    return jax.ShapeDtypeStruct(dims, dtype)


def run_pack(queries, keys, values, segment, row_type, pair_index):
    return call(
        pack_kernel,
        shape((2, 4, PAY, HD)),
        bytes_accessed=2 << 20,
        grid=(4,),
        in_specs=[
            pl.BlockSpec((1, TOK, 4 * HD), lambda i: (0, 0, i)),
            pl.BlockSpec((1, TOK, 2 * HD), lambda i: (0, 0, i)),
            pl.BlockSpec((1, TOK, 2 * HD), lambda i: (0, 0, i)),
            whole(1, TOK),
            whole(1, TOK),
            SMEM,
        ],
        out_specs=pl.BlockSpec((2, 1, PAY, HD), pair_of_heads),
    )(queries, keys, values, segment, row_type, pair_index).reshape(8, PAY, HD)


def run_forward(arrived):
    return call(
        forward_kernel,
        (shape((2 * HD, 2 * WINDOW)), shape((2 * WINDOW, HD), F32)),
        flops=4 << 30,
        bytes_accessed=2 << 20,
        grid=(2,),
        in_specs=[pl.BlockSpec((4, PAY, HD), lambda u: (u, 0, 0))],
        out_specs=[
            pl.BlockSpec((2 * HD, WINDOW), lambda u: (0, u)),
            pl.BlockSpec((WINDOW, HD), lambda u: (u, 0)),
        ],
    )(arrived)


def run_weight(out, cot, after):
    return call(
        weight_kernel,
        shape((16, 4, 64, HD)),
        flops=1 << 30,
        bytes_accessed=6 << 20,
        grid=(2,),
        in_specs=[
            whole(2 * HD, 2 * WINDOW),
            pl.BlockSpec((2 * WINDOW, 1024), lambda i: (0, i)),
            pl.BlockSpec(memory_space=pl.ANY),
        ],
        out_specs=pl.BlockSpec((8, 4, 64, HD), lambda i: (i, 0, 0, 0)),
    )(out, cot, after)


def run_backward(arrived, lse, cot, weight):
    width = cot.shape[1]
    return call(
        backward_kernel,
        shape((8, 4 * TOK, HD)),
        flops=8 << 30,
        bytes_accessed=7 << 20,
        grid=(2,),
        in_specs=[
            pl.BlockSpec((4, PAY, HD), lambda u: (u, 0, 0)),
            pl.BlockSpec((WINDOW, HD), lambda u: (u, 0)),
            pl.BlockSpec((WINDOW, width), lambda u: (u, 0)),
            whole(2 * HD, width),
        ],
        out_specs=pl.BlockSpec((4, 4 * TOK, HD), lambda u: (u, 0, 0)),
        scratch_shapes=[pltpu.VMEM((WINDOW, 2 * HD), BF16)],
    )(arrived, lse, cot, weight)


def run_sum(w, got):
    return call(
        sum_kernel,
        (shape((64, HD)),) * 4,
        room=16,
        bytes_accessed=1 << 20,
        in_specs=[SMEM, pl.BlockSpec(memory_space=pltpu.VMEM)],
        out_specs=[pl.BlockSpec(memory_space=pltpu.VMEM)] * 4,
        scratch_shapes=[pltpu.VMEM((4, 64, HD), F32)],
    )(w, got)


def run_spread(pieces):
    return call(
        spread_kernel,
        shape((64, HD), F32),
        room=16,
        in_specs=[pl.BlockSpec(memory_space=pltpu.VMEM)] * 4,
        out_specs=pl.BlockSpec(memory_space=pltpu.VMEM),
    )(*pieces)


def run_unpack(home, query_shape, key_shape):
    return call(
        unpack_kernel,
        (shape(query_shape), shape(key_shape), shape(key_shape)),
        room=16,
        bytes_accessed=2 << 20,
        grid=(4,),
        in_specs=[pl.BlockSpec((2, 1, 4 * TOK, HD), pair_of_heads)],
        out_specs=[
            pl.BlockSpec((1, TOK, 4 * HD), lambda i: (0, 0, i)),
            pl.BlockSpec((1, TOK, 2 * HD), lambda i: (0, 0, i)),
            pl.BlockSpec((1, TOK, 2 * HD), lambda i: (0, 0, i)),
        ],
    )(home.reshape(2, 4, 4 * TOK, HD))


def local(queries, keys, values, cotangent, out_weight, segment, row_type, pair_index):
    x = lax.axis_index("x").astype(jnp.int32)
    w = lax.axis_index("w").astype(jnp.int32).reshape(1)
    first = 32 * (2 * lax.rem(x, 2) + lax.axis_index("yb").astype(jnp.int32))
    eighth = lax.ppermute(lax.dynamic_slice_in_dim(out_weight, first, 32, axis=0), AXES, weight_moves())
    cot = lax.all_gather(cotangent[0], NEAR, axis=0, tiled=True)
    payload = run_pack(queries, keys, values, segment, row_type, pair_index)
    arrived = lax.all_to_all(payload, NEAR, 0, 0)
    weight = lax.all_to_all(jnp.broadcast_to(eighth[None], (8, *eighth.shape)), SHARE, 0, 0)
    out, lse = run_forward(arrived)
    pieces = run_weight(out, cot, weight)
    got = lax.all_to_all(pieces, FAR, 0, 0)
    back = run_backward(arrived, lse, cot, weight.reshape(-1, weight.shape[2]))
    home = lax.all_to_all(back, NEAR, 0, 0)
    sent = [lax.ppermute(part, AXES, piece_moves(turn)) for turn, part in enumerate(run_sum(w, got))]
    weight_grad = run_spread(sent).T
    query_grad, key_grad, value_grad = run_unpack(home, queries.shape, keys.shape)
    return query_grad, key_grad, value_grad, weight_grad


def solution(mesh):
    fine = Mesh(mesh.devices.reshape(SIZES), AXES)
    dp, seq = AXES[:4], AXES[4:]
    in_specs = (
        P(dp, seq, None),
        P(dp, seq, None),
        P(dp, seq, None),
        P(dp, seq, None),
        P(seq, None),
        P(dp, seq),
        P(dp, seq),
        P(dp, None),
    )
    out_specs = (P(dp, seq, None), P(dp, seq, None), P(dp, seq, None), P(seq, dp))
    return jax.shard_map(local, mesh=fine, in_specs=in_specs, out_specs=out_specs, check_vma=False)
```

```python
import itertools

import jax
import jax.numpy as jnp
import numpy as np
from jax import lax
from jax.experimental import pallas as pl
from jax.experimental.pallas import tpu as pltpu
from jax.sharding import Mesh
from jax.sharding import PartitionSpec as P

HD = 128
WINDOW = 512
HALF = WINDOW // 2
TOK = 128
SCALE = HD ** (-0.5)
AXES = ("x", "yh", "yl", "w", "p", "c")
SIZES = (4, 4, 2, 4, 2, 2)
NEAR = ("yl", "p", "c")
FAR = ("x", "yh")
CODE = 16
PAY = 4 * TOK + CODE
NONE = 99
F32 = jnp.float32
BF16 = jnp.bfloat16


def place(*index):
    return int(np.ravel_multi_index(index, SIZES))


def devices():
    return itertools.product(*map(range, SIZES))


def key_head(yl, p, c):
    return yl + 2 * p + 4 * c


def weight_moves():
    moves = []
    for x, yh, yl, w, p, c in devices():
        head = 2 * key_head(yl, p, c) + x // 2
        source = place(2 * (w // 2) + x % 2, yh, (w + head) % 2, head // 4, (head // 2) % 2, head % 2)
        moves.append((source, place(x, yh, yl, w, p, c)))
    return moves


def piece_moves(turn):
    moves = []
    for x, yh, yl, w, p, c in devices():
        piece = (w + turn) % 4
        head = 2 * key_head(yl, p, c) + piece % 2
        owner = place(x, yh, piece // 2, head // 4, (head // 2) % 2, head % 2)
        moves.append((place(x, yh, yl, w, p, c), owner))
    return moves


def dot(left, right, dims):
    return lax.dot_general(left, right, (dims, ((), ())), preferred_element_type=F32)


def pack_kernel(q_ref, k_ref, v_ref, seg_ref, type_ref, pair_ref, out_ref):
    seg = seg_ref[...]
    kind = type_ref[...]
    pair = jnp.zeros_like(seg)
    count = pair_ref.shape[1]
    for s in range(count):
        pair = jnp.where(seg == s, pair_ref[0, s], pair)
    as_query = jnp.where(kind != 0, count + pair, NONE)
    as_key = jnp.where(kind == 0, count + pair, NONE)
    row = lax.broadcasted_iota(jnp.int32, (CODE, TOK), 0)
    code = jnp.where(row == 0, seg, jnp.where(row == 1, as_query, jnp.where(row == 2, as_key, 0)))
    code = code.astype(F32).astype(BF16)
    for g in range(2):
        out_ref[g, 0, 0:TOK, :] = q_ref[0, :, 2 * g * HD : (2 * g + 1) * HD]
        out_ref[g, 0, TOK : 2 * TOK, :] = q_ref[0, :, (2 * g + 1) * HD : (2 * g + 2) * HD]
        out_ref[g, 0, 2 * TOK : 3 * TOK, :] = k_ref[0, :, g * HD : (g + 1) * HD]
        out_ref[g, 0, 3 * TOK : 4 * TOK, :] = v_ref[0, :, g * HD : (g + 1) * HD]
        out_ref[g, 0, 4 * TOK :, :] = code


def rows(pay_ref, first):
    return pay_ref[:, first : first + TOK, :].reshape(WINDOW, HD)


def hot(pay_ref):
    code = jnp.concatenate([pay_ref[i, 4 * TOK :, :] for i in range(4)], axis=1)
    code = code.astype(F32)[0:8]
    slot = lax.broadcasted_iota(jnp.int32, (32, WINDOW), 0).astype(F32)
    same = slot == code[0:1]
    want = jnp.where(same | (slot == code[1:2]), 1.0, 0.0).astype(BF16)
    have = jnp.where(same | (slot == code[2:3]), 1.0, 0.0).astype(BF16)
    return want, have


def visible_block(want, have, lo, ext):
    count = dot(want[:, lo:ext], have[:, :ext], ((0,), (0,)))
    t_pos = lax.broadcasted_iota(jnp.int32, (ext - lo, ext), 0) + lo
    s_pos = lax.broadcasted_iota(jnp.int32, (ext - lo, ext), 1)
    return (count > 0.5) & (s_pos <= t_pos)


def forward_kernel(pay_ref, out_ref, lse_ref):
    key = rows(pay_ref, 2 * TOK)
    value = rows(pay_ref, 3 * TOK)
    want, have = hot(pay_ref)
    lane = lax.broadcasted_iota(jnp.int32, (HALF, HD), 1)
    for block in range(2):
        lo = block * HALF
        ext = lo + HALF
        visible = visible_block(want, have, lo, ext)
        stats = []
        for b in range(2):
            query = rows(pay_ref, b * TOK)[lo:ext]
            scores = dot(query, key[:ext], ((1,), (1,))) * SCALE
            scores = jnp.where(visible, scores, -jnp.inf)
            top = jnp.max(scores, axis=-1, keepdims=True)
            exponent = jnp.exp(scores - top)
            total = jnp.sum(exponent, axis=-1, keepdims=True)
            low = (exponent * (1.0 / total)).astype(BF16)
            out = dot(low, value[:ext], ((1,), (0,)))
            out_ref[b * HD : (b + 1) * HD, lo:ext] = out.T.astype(BF16)
            stats.append(top + jnp.log(total))
        lse_ref[lo:ext, :] = jnp.where(lane == 0, stats[0], stats[1])


def weight_kernel(out_ref, cot_ref, w_ref, wg_ref, share_ref):
    @pl.when(pl.program_id(0) == 0)
    def _():
        share_ref[...] = w_ref[...]

    total = dot(out_ref[...], cot_ref[...], ((1,), (0,)))
    left = lax.broadcasted_iota(jnp.int32, (64, HD), 1) < 64
    for b in range(2):
        for m in range(8):
            upper = total[b * HD : b * HD + 64, m * HD : (m + 1) * HD]
            lower = total[b * HD + 64 : (b + 1) * HD, m * HD : (m + 1) * HD]
            wg_ref[m, b] = jnp.where(left, upper, pltpu.roll(lower, 64, 1)).astype(BF16)
            wg_ref[m, 2 + b] = jnp.where(left, pltpu.roll(upper, 64, 1), lower).astype(BF16)


def backward_kernel(x_ref, pay_ref, lse_ref, cot_ref, w0_ref, w1_ref, w2_ref, w3_ref, ret_ref, wbuf, ghbuf):
    @pl.when(pl.program_id(0) == 0)
    def _():
        for turn, quarter in enumerate((w0_ref, w1_ref, w2_ref, w3_ref)):
            first = pl.multiple_of(lax.rem(x_ref[0] + 4 - turn, 4) * 64, 64)
            wbuf[pl.ds(first, 64), :] = quarter[...]

    ghbuf[...] = dot(cot_ref[...], wbuf[...], ((1,), (1,))).astype(BF16)
    key = rows(pay_ref, 2 * TOK)
    value = rows(pay_ref, 3 * TOK)
    want, have = hot(pay_ref)
    kparts = [[None, None], [None, None]]
    vparts = [[None, None], [None, None]]
    for block in range(2):
        lo = block * HALF
        ext = lo + HALF
        visible = visible_block(want, have, lo, ext)
        for b in range(2):
            query = rows(pay_ref, b * TOK)[lo:ext]
            grad = ghbuf[lo:ext, b * HD : (b + 1) * HD]
            scores = dot(query, key[:ext], ((1,), (1,))) * SCALE - lse_ref[lo:ext, b : b + 1]
            attend = jnp.exp(jnp.where(visible, scores, -jnp.inf))
            low = attend.astype(BF16)
            grad_attend = dot(grad, value[:ext], ((1,), (1,)))
            delta = jnp.sum(attend * grad_attend, axis=-1, keepdims=True)
            ds = (attend * (grad_attend - delta) * SCALE).astype(BF16)
            dq = dot(ds, key[:ext], ((1,), (0,))).astype(BF16)
            ret_ref[2 * block : 2 * block + 2, b * TOK : (b + 1) * TOK, :] = dq.reshape(2, TOK, HD)
            dk = dot(ds, query, ((0,), (0,)))
            dv = dot(low, grad, ((0,), (0,)))
            if block == 0:
                kparts[b][0] = dk
                vparts[b][0] = dv
            else:
                kparts[b] = [kparts[b][0] + dk[:HALF], dk[HALF:]]
                vparts[b] = [vparts[b][0] + dv[:HALF], dv[HALF:]]
    for block in range(2):
        for first, parts in ((2 * TOK, kparts), (3 * TOK, vparts)):
            both = parts[0][block].astype(BF16).astype(F32) + parts[1][block].astype(BF16).astype(F32)
            ret_ref[2 * block : 2 * block + 2, first : first + TOK, :] = both.astype(BF16).reshape(2, TOK, HD)


def unpack_kernel(ret_ref, dq_ref, dk_ref, dv_ref):
    for g in range(2):
        dq_ref[0, :, 2 * g * HD : (2 * g + 1) * HD] = ret_ref[g, 0, 0:TOK, :]
        dq_ref[0, :, (2 * g + 1) * HD : (2 * g + 2) * HD] = ret_ref[g, 0, TOK : 2 * TOK, :]
        dk_ref[0, :, g * HD : (g + 1) * HD] = ret_ref[g, 0, 2 * TOK : 3 * TOK, :]
        dv_ref[0, :, g * HD : (g + 1) * HD] = ret_ref[g, 0, 3 * TOK : 4 * TOK, :]


def sum_kernel(w_ref, got_ref, out0_ref, out1_ref, out2_ref, out3_ref, total):
    total[...] = jnp.sum(got_ref[...].astype(F32), axis=0)
    for turn, out_ref in enumerate((out0_ref, out1_ref, out2_ref, out3_ref)):
        out_ref[...] = total[lax.rem(w_ref[0] + turn, 4)].astype(BF16)


def spread_kernel(a_ref, b_ref, c_ref, d_ref, out_ref):
    total = (a_ref[...].astype(F32) + b_ref[...].astype(F32)) + (c_ref[...].astype(F32) + d_ref[...].astype(F32))
    out_ref[:, 0:64] = total[:, 0:64].T
    out_ref[:, 64:128] = total[:, 64:128].T


SMEM = pl.BlockSpec(memory_space=pltpu.SMEM)


def whole(*dims):
    return pl.BlockSpec(dims, lambda *_: (0,) * len(dims))


def pair_of_heads(i):
    return 0, 2 * (i % 2) + i // 2, 0, 0


def call(kernel, out_shape, flops=0, bytes_accessed=0, room=60, **kw):
    return pl.pallas_call(
        kernel,
        out_shape=out_shape,
        compiler_params=pltpu.CompilerParams(vmem_limit_bytes=room << 20),
        cost_estimate=pl.CostEstimate(flops=flops, bytes_accessed=bytes_accessed, transcendentals=0),
        **kw,
    )


def shape(dims, dtype=BF16):
    return jax.ShapeDtypeStruct(dims, dtype)


def run_pack(queries, keys, values, segment, row_type, pair_index):
    return call(
        pack_kernel,
        shape((2, 4, PAY, HD)),
        bytes_accessed=2 << 20,
        grid=(4,),
        in_specs=[
            pl.BlockSpec((1, TOK, 4 * HD), lambda i: (0, 0, i)),
            pl.BlockSpec((1, TOK, 2 * HD), lambda i: (0, 0, i)),
            pl.BlockSpec((1, TOK, 2 * HD), lambda i: (0, 0, i)),
            whole(1, TOK),
            whole(1, TOK),
            SMEM,
        ],
        out_specs=pl.BlockSpec((2, 1, PAY, HD), pair_of_heads),
    )(queries, keys, values, segment, row_type, pair_index).reshape(8, PAY, HD)


def run_forward(arrived):
    return call(
        forward_kernel,
        (shape((2 * HD, 2 * WINDOW)), shape((2 * WINDOW, HD), F32)),
        flops=4 << 30,
        bytes_accessed=2 << 20,
        grid=(2,),
        in_specs=[pl.BlockSpec((4, PAY, HD), lambda u: (u, 0, 0))],
        out_specs=[
            pl.BlockSpec((2 * HD, WINDOW), lambda u: (0, u)),
            pl.BlockSpec((WINDOW, HD), lambda u: (u, 0)),
        ],
    )(arrived)


def run_weight(out, cot, quarter):
    return call(
        weight_kernel,
        (shape((16, 4, 64, HD)), shape(quarter.shape)),
        flops=1 << 30,
        bytes_accessed=6 << 20,
        grid=(2,),
        in_specs=[
            whole(2 * HD, 2 * WINDOW),
            pl.BlockSpec((2 * WINDOW, 1024), lambda i: (0, i)),
            whole(*quarter.shape),
        ],
        out_specs=[pl.BlockSpec((8, 4, 64, HD), lambda i: (i, 0, 0, 0)), whole(*quarter.shape)],
    )(out, cot, quarter)


def run_backward(x, arrived, lse, cot, quarters):
    width = cot.shape[1]
    return call(
        backward_kernel,
        shape((8, 4 * TOK, HD)),
        flops=8 << 30,
        bytes_accessed=7 << 20,
        grid=(2,),
        in_specs=[
            SMEM,
            pl.BlockSpec((4, PAY, HD), lambda u: (u, 0, 0)),
            pl.BlockSpec((WINDOW, HD), lambda u: (u, 0)),
            pl.BlockSpec((WINDOW, width), lambda u: (u, 0)),
        ]
        + [whole(64, width)] * 4,
        out_specs=pl.BlockSpec((4, 4 * TOK, HD), lambda u: (u, 0, 0)),
        scratch_shapes=[pltpu.VMEM((2 * HD, width), BF16), pltpu.VMEM((WINDOW, 2 * HD), BF16)],
    )(x, arrived, lse, cot, *quarters)


def run_sum(w, got):
    return call(
        sum_kernel,
        (shape((64, HD)),) * 4,
        room=16,
        bytes_accessed=1 << 20,
        in_specs=[SMEM, pl.BlockSpec(memory_space=pltpu.VMEM)],
        out_specs=[pl.BlockSpec(memory_space=pltpu.VMEM)] * 4,
        scratch_shapes=[pltpu.VMEM((4, 64, HD), F32)],
    )(w, got)


def run_spread(pieces):
    return call(
        spread_kernel,
        shape((64, HD), F32),
        room=16,
        in_specs=[pl.BlockSpec(memory_space=pltpu.VMEM)] * 4,
        out_specs=pl.BlockSpec(memory_space=pltpu.VMEM),
    )(*pieces)


def run_unpack(home, query_shape, key_shape):
    return call(
        unpack_kernel,
        (shape(query_shape), shape(key_shape), shape(key_shape)),
        room=16,
        bytes_accessed=2 << 20,
        grid=(4,),
        in_specs=[pl.BlockSpec((2, 1, 4 * TOK, HD), pair_of_heads)],
        out_specs=[
            pl.BlockSpec((1, TOK, 4 * HD), lambda i: (0, 0, i)),
            pl.BlockSpec((1, TOK, 2 * HD), lambda i: (0, 0, i)),
            pl.BlockSpec((1, TOK, 2 * HD), lambda i: (0, 0, i)),
        ],
    )(home.reshape(2, 4, 4 * TOK, HD))


def local(queries, keys, values, cotangent, out_weight, segment, row_type, pair_index):
    x = lax.axis_index("x").astype(jnp.int32)
    w = lax.axis_index("w").astype(jnp.int32).reshape(1)
    share = lax.dynamic_slice_in_dim(out_weight, 64 * lax.rem(x, 2), 64, axis=0)
    quarter = lax.ppermute(share, AXES, weight_moves())
    cot = lax.all_gather(cotangent[0], NEAR, axis=0, tiled=True)
    payload = run_pack(queries, keys, values, segment, row_type, pair_index)
    arrived = lax.all_to_all(payload, NEAR, 0, 0)
    out, lse = run_forward(arrived)
    pieces, share = run_weight(out, cot, quarter)
    got = lax.all_to_all(pieces, FAR, 0, 0)
    quarters = [share] + [
        lax.ppermute(share, "x", [(i, (i + turn) % 4) for i in range(4)]) for turn in (1, 2, 3)
    ]
    back = run_backward(x.reshape(1), arrived, lse, cot, quarters)
    home = lax.all_to_all(back, NEAR, 0, 0)
    sent = [lax.ppermute(part, AXES, piece_moves(turn)) for turn, part in enumerate(run_sum(w, got))]
    weight_grad = run_spread(sent).T
    query_grad, key_grad, value_grad = run_unpack(home, queries.shape, keys.shape)
    return query_grad, key_grad, value_grad, weight_grad


def solution(mesh):
    fine = Mesh(mesh.devices.reshape(SIZES), AXES)
    dp, seq = AXES[:3], AXES[3:]
    in_specs = (
        P(dp, seq, None),
        P(dp, seq, None),
        P(dp, seq, None),
        P(dp, seq, None),
        P(seq, None),
        P(dp, seq),
        P(dp, seq),
        P(dp, None),
    )
    out_specs = (P(dp, seq, None), P(dp, seq, None), P(dp, seq, None), P(seq, dp))
    return jax.shard_map(local, mesh=fine, in_specs=in_specs, out_specs=out_specs, check_vma=False)
```

```python
import itertools

import jax
import jax.numpy as jnp
import numpy as np
from jax import lax
from jax.experimental import pallas as pl
from jax.experimental.pallas import tpu as pltpu
from jax.sharding import Mesh
from jax.sharding import PartitionSpec as P

HD = 128
WINDOW = 512
HALF = WINDOW // 2
TOK = 128
SCALE = HD ** (-0.5)
AXES = ("x", "yh", "yl", "w", "p", "c")
SIZES = (4, 4, 2, 4, 2, 2)
NEAR = ("yl", "p", "c")
FAR = ("x", "yh")
CODE = 16
PAY = 4 * TOK + CODE
NONE = 99
F32 = jnp.float32
BF16 = jnp.bfloat16


def place(*index):
    return int(np.ravel_multi_index(index, SIZES))


def devices():
    return itertools.product(*map(range, SIZES))


def key_head(yl, p, c):
    return yl + 2 * p + 4 * c


def weight_moves():
    moves = []
    for x, yh, yl, w, p, c in devices():
        head = 2 * key_head(yl, p, c) + x // 2
        source = place(2 * (w // 2) + x % 2, yh, (w + head) % 2, head // 4, (head // 2) % 2, head % 2)
        moves.append((source, place(x, yh, yl, w, p, c)))
    return moves


def piece_moves():
    moves = []
    for x, yh, yl, w, p, c in devices():
        head = 2 * key_head(yl, p, c) + w % 2
        owner = place(x, yh, w // 2, head // 4, (head // 2) % 2, head % 2)
        moves.append((place(x, yh, yl, w, p, c), owner))
    return moves


def dot(left, right, dims):
    return lax.dot_general(left, right, (dims, ((), ())), preferred_element_type=F32)


def pack_kernel(q_ref, k_ref, v_ref, seg_ref, type_ref, pair_ref, out_ref):
    seg = seg_ref[...]
    kind = type_ref[...]
    pair = jnp.zeros_like(seg)
    count = pair_ref.shape[1]
    for s in range(count):
        pair = jnp.where(seg == s, pair_ref[0, s], pair)
    as_query = jnp.where(kind != 0, count + pair, NONE)
    as_key = jnp.where(kind == 0, count + pair, NONE)
    row = lax.broadcasted_iota(jnp.int32, (CODE, TOK), 0)
    code = jnp.where(row == 0, seg, jnp.where(row == 1, as_query, jnp.where(row == 2, as_key, 0)))
    code = code.astype(F32).astype(BF16)
    for g in range(2):
        out_ref[g, 0, 0:TOK, :] = q_ref[0, :, 2 * g * HD : (2 * g + 1) * HD]
        out_ref[g, 0, TOK : 2 * TOK, :] = q_ref[0, :, (2 * g + 1) * HD : (2 * g + 2) * HD]
        out_ref[g, 0, 2 * TOK : 3 * TOK, :] = k_ref[0, :, g * HD : (g + 1) * HD]
        out_ref[g, 0, 3 * TOK : 4 * TOK, :] = v_ref[0, :, g * HD : (g + 1) * HD]
        out_ref[g, 0, 4 * TOK :, :] = code


def rows(pay_ref, first):
    return pay_ref[:, first : first + TOK, :].reshape(WINDOW, HD)


def hot(pay_ref):
    code = jnp.concatenate([pay_ref[i, 4 * TOK :, :] for i in range(4)], axis=1)
    code = code.astype(F32)[0:8]
    slot = lax.broadcasted_iota(jnp.int32, (32, WINDOW), 0).astype(F32)
    same = slot == code[0:1]
    want = jnp.where(same | (slot == code[1:2]), 1.0, 0.0).astype(BF16)
    have = jnp.where(same | (slot == code[2:3]), 1.0, 0.0).astype(BF16)
    return want, have


def visible_block(want, have, lo, ext):
    count = dot(want[:, lo:ext], have[:, :ext], ((0,), (0,)))
    t_pos = lax.broadcasted_iota(jnp.int32, (ext - lo, ext), 0) + lo
    s_pos = lax.broadcasted_iota(jnp.int32, (ext - lo, ext), 1)
    return (count > 0.5) & (s_pos <= t_pos)


def forward_kernel(pay_ref, out_ref, lse_ref):
    key = rows(pay_ref, 2 * TOK)
    value = rows(pay_ref, 3 * TOK)
    want, have = hot(pay_ref)
    lane = lax.broadcasted_iota(jnp.int32, (HALF, HD), 1)
    for block in range(2):
        lo = block * HALF
        ext = lo + HALF
        visible = visible_block(want, have, lo, ext)
        stats = []
        for b in range(2):
            query = rows(pay_ref, b * TOK)[lo:ext]
            scores = dot(query, key[:ext], ((1,), (1,))) * SCALE
            scores = jnp.where(visible, scores, -jnp.inf)
            top = jnp.max(scores, axis=-1, keepdims=True)
            exponent = jnp.exp(scores - top)
            total = jnp.sum(exponent, axis=-1, keepdims=True)
            low = (exponent * (1.0 / total)).astype(BF16)
            out = dot(low, value[:ext], ((1,), (0,)))
            out_ref[b * HD : (b + 1) * HD, lo:ext] = out.T.astype(BF16)
            stats.append(top + jnp.log(total))
        lse_ref[lo:ext, :] = jnp.where(lane == 0, stats[0], stats[1])


def weight_kernel(out_ref, cot_ref, a_ref, b_ref, c_ref, wg_ref):
    del a_ref, b_ref, c_ref
    total = dot(out_ref[...], cot_ref[...], ((1,), (0,)))
    left = lax.broadcasted_iota(jnp.int32, (64, HD), 1) < 64
    for b in range(2):
        for m in range(8):
            upper = total[b * HD : b * HD + 64, m * HD : (m + 1) * HD]
            lower = total[b * HD + 64 : (b + 1) * HD, m * HD : (m + 1) * HD]
            wg_ref[m, b] = jnp.where(left, upper, pltpu.roll(lower, 64, 1)).astype(BF16)
            wg_ref[m, 2 + b] = jnp.where(left, pltpu.roll(upper, 64, 1), lower).astype(BF16)


def backward_kernel(x_ref, pay_ref, lse_ref, cot_ref, w0_ref, w1_ref, w2_ref, w3_ref, ret_ref, wbuf, ghbuf):
    @pl.when(pl.program_id(0) == 0)
    def _():
        for turn, quarter in enumerate((w0_ref, w1_ref, w2_ref, w3_ref)):
            first = pl.multiple_of(lax.rem(x_ref[0] + 4 - turn, 4) * 64, 64)
            wbuf[pl.ds(first, 64), :] = quarter[...]

    ghbuf[...] = dot(cot_ref[...], wbuf[...], ((1,), (1,))).astype(BF16)
    key = rows(pay_ref, 2 * TOK)
    value = rows(pay_ref, 3 * TOK)
    want, have = hot(pay_ref)
    kparts = [[None, None], [None, None]]
    vparts = [[None, None], [None, None]]
    for block in range(2):
        lo = block * HALF
        ext = lo + HALF
        visible = visible_block(want, have, lo, ext)
        for b in range(2):
            query = rows(pay_ref, b * TOK)[lo:ext]
            grad = ghbuf[lo:ext, b * HD : (b + 1) * HD]
            scores = dot(query, key[:ext], ((1,), (1,))) * SCALE - lse_ref[lo:ext, b : b + 1]
            attend = jnp.exp(jnp.where(visible, scores, -jnp.inf))
            low = attend.astype(BF16)
            grad_attend = dot(grad, value[:ext], ((1,), (1,)))
            delta = jnp.sum(attend * grad_attend, axis=-1, keepdims=True)
            ds = (attend * (grad_attend - delta) * SCALE).astype(BF16)
            dq = dot(ds, key[:ext], ((1,), (0,))).astype(BF16)
            ret_ref[2 * block : 2 * block + 2, b * TOK : (b + 1) * TOK, :] = dq.reshape(2, TOK, HD)
            dk = dot(ds, query, ((0,), (0,)))
            dv = dot(low, grad, ((0,), (0,)))
            if block == 0:
                kparts[b][0] = dk
                vparts[b][0] = dv
            else:
                kparts[b] = [kparts[b][0] + dk[:HALF], dk[HALF:]]
                vparts[b] = [vparts[b][0] + dv[:HALF], dv[HALF:]]
    for block in range(2):
        for first, parts in ((2 * TOK, kparts), (3 * TOK, vparts)):
            both = parts[0][block].astype(BF16).astype(F32) + parts[1][block].astype(BF16).astype(F32)
            ret_ref[2 * block : 2 * block + 2, first : first + TOK, :] = both.astype(BF16).reshape(2, TOK, HD)


def unpack_kernel(ret_ref, dq_ref, dk_ref, dv_ref):
    for g in range(2):
        dq_ref[0, :, 2 * g * HD : (2 * g + 1) * HD] = ret_ref[g, 0, 0:TOK, :]
        dq_ref[0, :, (2 * g + 1) * HD : (2 * g + 2) * HD] = ret_ref[g, 0, TOK : 2 * TOK, :]
        dk_ref[0, :, g * HD : (g + 1) * HD] = ret_ref[g, 0, 2 * TOK : 3 * TOK, :]
        dv_ref[0, :, g * HD : (g + 1) * HD] = ret_ref[g, 0, 3 * TOK : 4 * TOK, :]


def near_sum_kernel(got_ref, out_ref):
    out_ref[...] = jnp.sum(got_ref[...].astype(F32), axis=0).astype(BF16)


def far_sum_kernel(w_ref, got_ref, out_ref):
    total = jnp.sum(got_ref[:, w_ref[0]].astype(F32), axis=0)
    out_ref[:, 0:64] = total[:, 0:64].T
    out_ref[:, 64:128] = total[:, 64:128].T


SMEM = pl.BlockSpec(memory_space=pltpu.SMEM)
VMEM = pl.BlockSpec(memory_space=pltpu.VMEM)


def whole(*dims):
    return pl.BlockSpec(dims, lambda *_: (0,) * len(dims))


def pair_of_heads(i):
    return 0, 2 * (i % 2) + i // 2, 0, 0


def call(kernel, out_shape, flops=0, bytes_accessed=0, room=60, **kw):
    return pl.pallas_call(
        kernel,
        out_shape=out_shape,
        compiler_params=pltpu.CompilerParams(vmem_limit_bytes=room << 20),
        cost_estimate=pl.CostEstimate(flops=flops, bytes_accessed=bytes_accessed, transcendentals=0),
        **kw,
    )


def shape(dims, dtype=BF16):
    return jax.ShapeDtypeStruct(dims, dtype)


def run_pack(queries, keys, values, segment, row_type, pair_index):
    return call(
        pack_kernel,
        shape((2, 4, PAY, HD)),
        bytes_accessed=2 << 20,
        grid=(4,),
        in_specs=[
            pl.BlockSpec((1, TOK, 4 * HD), lambda i: (0, 0, i)),
            pl.BlockSpec((1, TOK, 2 * HD), lambda i: (0, 0, i)),
            pl.BlockSpec((1, TOK, 2 * HD), lambda i: (0, 0, i)),
            whole(1, TOK),
            whole(1, TOK),
            SMEM,
        ],
        out_specs=pl.BlockSpec((2, 1, PAY, HD), pair_of_heads),
    )(queries, keys, values, segment, row_type, pair_index).reshape(8, PAY, HD)


def run_forward(arrived):
    return call(
        forward_kernel,
        (shape((2 * HD, 2 * WINDOW)), shape((2 * WINDOW, HD), F32)),
        flops=4 << 30,
        bytes_accessed=2 << 20,
        grid=(2,),
        in_specs=[pl.BlockSpec((4, PAY, HD), lambda u: (u, 0, 0))],
        out_specs=[
            pl.BlockSpec((2 * HD, WINDOW), lambda u: (0, u)),
            pl.BlockSpec((WINDOW, HD), lambda u: (u, 0)),
        ],
    )(arrived)


def run_weight(out, cot, after):
    return call(
        weight_kernel,
        shape((16, 4, 64, HD)),
        flops=1 << 30,
        bytes_accessed=6 << 20,
        grid=(2,),
        in_specs=[
            whole(2 * HD, 2 * WINDOW),
            pl.BlockSpec((2 * WINDOW, 1024), lambda i: (0, i)),
        ]
        + [pl.BlockSpec(memory_space=pl.ANY)] * 3,
        out_specs=pl.BlockSpec((8, 4, 64, HD), lambda i: (i, 0, 0, 0)),
    )(out, cot, *after)


def run_backward(x, arrived, lse, cot, quarters):
    width = cot.shape[1]
    return call(
        backward_kernel,
        shape((8, 4 * TOK, HD)),
        flops=8 << 30,
        bytes_accessed=7 << 20,
        grid=(2,),
        in_specs=[
            SMEM,
            pl.BlockSpec((4, PAY, HD), lambda u: (u, 0, 0)),
            pl.BlockSpec((WINDOW, HD), lambda u: (u, 0)),
            pl.BlockSpec((WINDOW, width), lambda u: (u, 0)),
        ]
        + [whole(64, width)] * 4,
        out_specs=pl.BlockSpec((4, 4 * TOK, HD), lambda u: (u, 0, 0)),
        scratch_shapes=[pltpu.VMEM((2 * HD, width), BF16), pltpu.VMEM((WINDOW, 2 * HD), BF16)],
    )(x, arrived, lse, cot, *quarters)


def run_near_sum(got):
    return call(
        near_sum_kernel,
        shape(got.shape[1:]),
        room=16,
        bytes_accessed=1 << 20,
        in_specs=[VMEM],
        out_specs=VMEM,
    )(got)


def run_far_sum(w, got):
    return call(
        far_sum_kernel,
        shape((64, HD), F32),
        room=16,
        bytes_accessed=1 << 18,
        in_specs=[SMEM, VMEM],
        out_specs=VMEM,
    )(w, got)


def run_unpack(home, query_shape, key_shape):
    return call(
        unpack_kernel,
        (shape(query_shape), shape(key_shape), shape(key_shape)),
        room=16,
        bytes_accessed=2 << 20,
        grid=(4,),
        in_specs=[pl.BlockSpec((2, 1, 4 * TOK, HD), pair_of_heads)],
        out_specs=[
            pl.BlockSpec((1, TOK, 4 * HD), lambda i: (0, 0, i)),
            pl.BlockSpec((1, TOK, 2 * HD), lambda i: (0, 0, i)),
            pl.BlockSpec((1, TOK, 2 * HD), lambda i: (0, 0, i)),
        ],
    )(home.reshape(2, 4, 4 * TOK, HD))


def local(queries, keys, values, cotangent, out_weight, segment, row_type, pair_index):
    x = lax.axis_index("x").astype(jnp.int32)
    w = lax.axis_index("w").astype(jnp.int32).reshape(1)
    share = lax.dynamic_slice_in_dim(out_weight, 64 * lax.rem(x, 2), 64, axis=0)
    quarter = lax.ppermute(share, AXES, weight_moves())
    cot = lax.all_gather(cotangent[0], NEAR, axis=0, tiled=True)
    payload = run_pack(queries, keys, values, segment, row_type, pair_index)
    arrived = lax.all_to_all(payload, NEAR, 0, 0)
    out, lse = run_forward(arrived)
    quarters = [quarter] + [
        lax.ppermute(quarter, "x", [(i, (i + turn) % 4) for i in range(4)]) for turn in (1, 2, 3)
    ]
    pieces = run_weight(out, cot, quarters[1:])
    got = lax.all_to_all(pieces, FAR, 0, 0)
    back = run_backward(x.reshape(1), arrived, lse, cot, quarters)
    home = lax.all_to_all(back, NEAR, 0, 0)
    windows = lax.all_gather(run_near_sum(got), "w", axis=0)
    weight_grad = lax.ppermute(run_far_sum(w, windows), AXES, piece_moves()).T
    query_grad, key_grad, value_grad = run_unpack(home, queries.shape, keys.shape)
    return query_grad, key_grad, value_grad, weight_grad


def solution(mesh):
    fine = Mesh(mesh.devices.reshape(SIZES), AXES)
    dp, seq = AXES[:3], AXES[3:]
    in_specs = (
        P(dp, seq, None),
        P(dp, seq, None),
        P(dp, seq, None),
        P(dp, seq, None),
        P(seq, None),
        P(dp, seq),
        P(dp, seq),
        P(dp, None),
    )
    out_specs = (P(dp, seq, None), P(dp, seq, None), P(dp, seq, None), P(seq, dp))
    return jax.shard_map(local, mesh=fine, in_specs=in_specs, out_specs=out_specs, check_vma=False)
```

```python
import itertools

import jax
import jax.numpy as jnp
import numpy as np
from jax import lax
from jax.experimental import pallas as pl
from jax.experimental.pallas import tpu as pltpu
from jax.sharding import Mesh
from jax.sharding import PartitionSpec as P

HD = 128
WINDOW = 512
HALF = WINDOW // 2
TOK = 128
SCALE = HD ** (-0.5)
AXES = ("x", "yh", "yl", "w", "p", "c")
SIZES = (4, 4, 2, 4, 2, 2)
NEAR = ("yl", "p", "c")
FAR = ("x", "yh")
CODE = 16
PAY = 4 * TOK + CODE
NONE = 99
F32 = jnp.float32
BF16 = jnp.bfloat16


def place(*index):
    return int(np.ravel_multi_index(index, SIZES))


def devices():
    return itertools.product(*map(range, SIZES))


def key_head(yl, p, c):
    return yl + 2 * p + 4 * c


def weight_moves():
    moves = []
    for x, yh, yl, w, p, c in devices():
        head = 2 * key_head(yl, p, c) + x // 2
        source = place(2 * (w // 2) + x % 2, yh, (w + head) % 2, head // 4, (head // 2) % 2, head % 2)
        moves.append((source, place(x, yh, yl, w, p, c)))
    return moves


def piece_moves():
    moves = []
    for x, yh, yl, w, p, c in devices():
        head = 2 * key_head(yl, p, c) + w % 2
        owner = place(x, yh, w // 2, head // 4, (head // 2) % 2, head % 2)
        moves.append((place(x, yh, yl, w, p, c), owner))
    return moves


def dot(left, right, dims):
    return lax.dot_general(left, right, (dims, ((), ())), preferred_element_type=F32)


def pack_kernel(q_ref, k_ref, v_ref, seg_ref, type_ref, pair_ref, out_ref):
    seg = seg_ref[...]
    kind = type_ref[...]
    pair = jnp.zeros_like(seg)
    count = pair_ref.shape[1]
    for s in range(count):
        pair = jnp.where(seg == s, pair_ref[0, s], pair)
    as_query = jnp.where(kind != 0, count + pair, NONE)
    as_key = jnp.where(kind == 0, count + pair, NONE)
    row = lax.broadcasted_iota(jnp.int32, (CODE, TOK), 0)
    code = jnp.where(row == 0, seg, jnp.where(row == 1, as_query, jnp.where(row == 2, as_key, 0)))
    code = code.astype(F32).astype(BF16)
    for g in range(2):
        out_ref[g, 0, 0:TOK, :] = q_ref[0, :, 2 * g * HD : (2 * g + 1) * HD]
        out_ref[g, 0, TOK : 2 * TOK, :] = q_ref[0, :, (2 * g + 1) * HD : (2 * g + 2) * HD]
        out_ref[g, 0, 2 * TOK : 3 * TOK, :] = k_ref[0, :, g * HD : (g + 1) * HD]
        out_ref[g, 0, 3 * TOK : 4 * TOK, :] = v_ref[0, :, g * HD : (g + 1) * HD]
        out_ref[g, 0, 4 * TOK :, :] = code


def rows(pay_ref, first):
    return pay_ref[:, first : first + TOK, :].reshape(WINDOW, HD)


def hot(pay_ref):
    code = jnp.concatenate([pay_ref[i, 4 * TOK :, :] for i in range(4)], axis=1)
    code = code.astype(F32)[0:8]
    slot = lax.broadcasted_iota(jnp.int32, (32, WINDOW), 0).astype(F32)
    same = slot == code[0:1]
    want = jnp.where(same | (slot == code[1:2]), 1.0, 0.0).astype(BF16)
    have = jnp.where(same | (slot == code[2:3]), 1.0, 0.0).astype(BF16)
    return want, have


def visible_block(want, have, lo, ext):
    count = dot(want[:, lo:ext], have[:, :ext], ((0,), (0,)))
    t_pos = lax.broadcasted_iota(jnp.int32, (ext - lo, ext), 0) + lo
    s_pos = lax.broadcasted_iota(jnp.int32, (ext - lo, ext), 1)
    return (count > 0.5) & (s_pos <= t_pos)


def forward_kernel(pay_ref, out_ref, lse_ref):
    key = rows(pay_ref, 2 * TOK)
    value = rows(pay_ref, 3 * TOK)
    want, have = hot(pay_ref)
    lane = lax.broadcasted_iota(jnp.int32, (HALF, HD), 1)
    for block in range(2):
        lo = block * HALF
        ext = lo + HALF
        visible = visible_block(want, have, lo, ext)
        stats = []
        for b in range(2):
            query = rows(pay_ref, b * TOK)[lo:ext]
            scores = dot(query, key[:ext], ((1,), (1,))) * SCALE
            scores = jnp.where(visible, scores, -jnp.inf)
            top = jnp.max(scores, axis=-1, keepdims=True)
            exponent = jnp.exp(scores - top)
            total = jnp.sum(exponent, axis=-1, keepdims=True)
            low = (exponent * (1.0 / total)).astype(BF16)
            out = dot(low, value[:ext], ((1,), (0,)))
            out_ref[b * HD : (b + 1) * HD, lo:ext] = out.T.astype(BF16)
            stats.append(top + jnp.log(total))
        lse_ref[lo:ext, :] = jnp.where(lane == 0, stats[0], stats[1])


def weight_kernel(out_ref, cot_ref, a_ref, b_ref, c_ref, wg_ref):
    del a_ref, b_ref, c_ref
    total = dot(out_ref[...], cot_ref[...], ((1,), (0,)))
    left = lax.broadcasted_iota(jnp.int32, (64, HD), 1) < 64
    for b in range(2):
        for m in range(8):
            upper = total[b * HD : b * HD + 64, m * HD : (m + 1) * HD]
            lower = total[b * HD + 64 : (b + 1) * HD, m * HD : (m + 1) * HD]
            wg_ref[m, b] = jnp.where(left, upper, pltpu.roll(lower, 64, 1)).astype(BF16)
            wg_ref[m, 2 + b] = jnp.where(left, pltpu.roll(upper, 64, 1), lower).astype(BF16)


def backward_kernel(me_ref, pay_ref, lse_ref, cot_ref, w0_ref, w1_ref, w2_ref, w3_ref, *refs):
    *out_refs, wbuf, ghbuf, ret_ref = refs

    @pl.when(pl.program_id(0) == 0)
    def _():
        for turn, quarter in enumerate((w0_ref, w1_ref, w2_ref, w3_ref)):
            first = pl.multiple_of(lax.rem(me_ref[0] + 4 - turn, 4) * 64, 64)
            wbuf[pl.ds(first, 64), :] = quarter[...]

    ghbuf[...] = dot(cot_ref[...], wbuf[...], ((1,), (1,))).astype(BF16)
    key = rows(pay_ref, 2 * TOK)
    value = rows(pay_ref, 3 * TOK)
    want, have = hot(pay_ref)
    kparts = [[None, None], [None, None]]
    vparts = [[None, None], [None, None]]
    for block in range(2):
        lo = block * HALF
        ext = lo + HALF
        visible = visible_block(want, have, lo, ext)
        for b in range(2):
            query = rows(pay_ref, b * TOK)[lo:ext]
            grad = ghbuf[lo:ext, b * HD : (b + 1) * HD]
            scores = dot(query, key[:ext], ((1,), (1,))) * SCALE - lse_ref[lo:ext, b : b + 1]
            attend = jnp.exp(jnp.where(visible, scores, -jnp.inf))
            low = attend.astype(BF16)
            grad_attend = dot(grad, value[:ext], ((1,), (1,)))
            delta = jnp.sum(attend * grad_attend, axis=-1, keepdims=True)
            ds = (attend * (grad_attend - delta) * SCALE).astype(BF16)
            dq = dot(ds, key[:ext], ((1,), (0,))).astype(BF16)
            ret_ref[2 * block : 2 * block + 2, b * TOK : (b + 1) * TOK, :] = dq.reshape(2, TOK, HD)
            dk = dot(ds, query, ((0,), (0,)))
            dv = dot(low, grad, ((0,), (0,)))
            if block == 0:
                kparts[b][0] = dk
                vparts[b][0] = dv
            else:
                kparts[b] = [kparts[b][0] + dk[:HALF], dk[HALF:]]
                vparts[b] = [vparts[b][0] + dv[:HALF], dv[HALF:]]
    for block in range(2):
        for first, parts in ((2 * TOK, kparts), (3 * TOK, vparts)):
            both = parts[0][block].astype(BF16).astype(F32) + parts[1][block].astype(BF16).astype(F32)
            ret_ref[2 * block : 2 * block + 2, first : first + TOK, :] = both.astype(BF16).reshape(2, TOK, HD)
    for step in range(2):

        @pl.when(pl.program_id(0) == step)
        def _():
            for k in range(4):
                out_refs[4 * step + k][...] = ret_ref[jnp.bitwise_xor(me_ref[2], k)]


def unpack_kernel(me_ref, *refs):
    *got_refs, dq_ref, dk_ref, dv_ref = refs
    for k, got_ref in enumerate(got_refs):
        source = jnp.bitwise_xor(4 * me_ref[1] + me_ref[2], k)
        head = key_head(source // 4, (source // 2) % 2, source % 2)
        near = pl.ds(pl.multiple_of(head * HD, HD), HD)
        dq_ref[0, :, pl.ds(pl.multiple_of(head * 2 * HD, HD), HD)] = got_ref[0:TOK, :]
        dq_ref[0, :, pl.ds(pl.multiple_of(head * 2 * HD + HD, HD), HD)] = got_ref[TOK : 2 * TOK, :]
        dk_ref[0, :, near] = got_ref[2 * TOK : 3 * TOK, :]
        dv_ref[0, :, near] = got_ref[3 * TOK : 4 * TOK, :]


def near_sum_kernel(got_ref, out_ref):
    out_ref[...] = jnp.sum(got_ref[...].astype(F32), axis=0).astype(BF16)


def far_sum_kernel(w_ref, got_ref, out_ref):
    total = jnp.sum(got_ref[:, w_ref[0]].astype(F32), axis=0)
    out_ref[:, 0:64] = total[:, 0:64].T
    out_ref[:, 64:128] = total[:, 64:128].T


SMEM = pl.BlockSpec(memory_space=pltpu.SMEM)
VMEM = pl.BlockSpec(memory_space=pltpu.VMEM)


def whole(*dims):
    return pl.BlockSpec(dims, lambda *_: (0,) * len(dims))


def pair_of_heads(i):
    return 0, 2 * (i % 2) + i // 2, 0, 0


def call(kernel, out_shape, flops=0, bytes_accessed=0, room=60, **kw):
    return pl.pallas_call(
        kernel,
        out_shape=out_shape,
        compiler_params=pltpu.CompilerParams(vmem_limit_bytes=room << 20),
        cost_estimate=pl.CostEstimate(flops=flops, bytes_accessed=bytes_accessed, transcendentals=0),
        **kw,
    )


def shape(dims, dtype=BF16):
    return jax.ShapeDtypeStruct(dims, dtype)


def run_pack(queries, keys, values, segment, row_type, pair_index):
    return call(
        pack_kernel,
        shape((2, 4, PAY, HD)),
        bytes_accessed=2 << 20,
        grid=(4,),
        in_specs=[
            pl.BlockSpec((1, TOK, 4 * HD), lambda i: (0, 0, i)),
            pl.BlockSpec((1, TOK, 2 * HD), lambda i: (0, 0, i)),
            pl.BlockSpec((1, TOK, 2 * HD), lambda i: (0, 0, i)),
            whole(1, TOK),
            whole(1, TOK),
            SMEM,
        ],
        out_specs=pl.BlockSpec((2, 1, PAY, HD), pair_of_heads),
    )(queries, keys, values, segment, row_type, pair_index).reshape(8, PAY, HD)


def run_forward(arrived):
    return call(
        forward_kernel,
        (shape((2 * HD, 2 * WINDOW)), shape((2 * WINDOW, HD), F32)),
        flops=4 << 30,
        bytes_accessed=2 << 20,
        grid=(2,),
        in_specs=[pl.BlockSpec((4, PAY, HD), lambda u: (u, 0, 0))],
        out_specs=[
            pl.BlockSpec((2 * HD, WINDOW), lambda u: (0, u)),
            pl.BlockSpec((WINDOW, HD), lambda u: (u, 0)),
        ],
    )(arrived)


def run_weight(out, cot, after):
    return call(
        weight_kernel,
        shape((16, 4, 64, HD)),
        flops=1 << 30,
        bytes_accessed=6 << 20,
        grid=(2,),
        in_specs=[
            whole(2 * HD, 2 * WINDOW),
            pl.BlockSpec((2 * WINDOW, 1024), lambda i: (0, i)),
        ]
        + [pl.BlockSpec(memory_space=pl.ANY)] * 3,
        out_specs=pl.BlockSpec((8, 4, 64, HD), lambda i: (i, 0, 0, 0)),
    )(out, cot, *after)


def run_backward(me, arrived, lse, cot, quarters):
    width = cot.shape[1]

    def row(step, me_ref):
        return jnp.bitwise_xor(step, me_ref[1])

    grid_spec = pltpu.PrefetchScalarGridSpec(
        num_scalar_prefetch=1,
        grid=(2,),
        in_specs=[
            pl.BlockSpec((4, PAY, HD), lambda i, me_ref: (row(i, me_ref), 0, 0)),
            pl.BlockSpec((WINDOW, HD), lambda i, me_ref: (row(i, me_ref), 0)),
            pl.BlockSpec((WINDOW, width), lambda i, me_ref: (row(i, me_ref), 0)),
        ]
        + [whole(64, width)] * 4,
        out_specs=[whole(4 * TOK, HD)] * 8,
        scratch_shapes=[
            pltpu.VMEM((2 * HD, width), BF16),
            pltpu.VMEM((WINDOW, 2 * HD), BF16),
            pltpu.VMEM((4, 4 * TOK, HD), BF16),
        ],
    )
    return call(
        backward_kernel,
        (shape((4 * TOK, HD)),) * 8,
        flops=8 << 30,
        bytes_accessed=7 << 20,
        grid_spec=grid_spec,
    )(me, arrived, lse, cot, *quarters)


def run_near_sum(got):
    return call(
        near_sum_kernel,
        shape(got.shape[1:]),
        room=16,
        bytes_accessed=1 << 20,
        in_specs=[VMEM],
        out_specs=VMEM,
    )(got)


def run_far_sum(w, got):
    return call(
        far_sum_kernel,
        shape((64, HD), F32),
        room=16,
        bytes_accessed=1 << 18,
        in_specs=[SMEM, VMEM],
        out_specs=VMEM,
    )(w, got)


def run_unpack(me, home, query_shape, key_shape):
    return call(
        unpack_kernel,
        (shape(query_shape), shape(key_shape), shape(key_shape)),
        room=16,
        bytes_accessed=2 << 20,
        in_specs=[SMEM] + [VMEM] * 8,
        out_specs=[whole(*query_shape), whole(*key_shape), whole(*key_shape)],
    )(me, *home)


def local(queries, keys, values, cotangent, out_weight, segment, row_type, pair_index):
    x = lax.axis_index("x").astype(jnp.int32)
    w = lax.axis_index("w").astype(jnp.int32).reshape(1)
    share = lax.dynamic_slice_in_dim(out_weight, 64 * lax.rem(x, 2), 64, axis=0)
    quarter = lax.ppermute(share, AXES, weight_moves())
    cot = lax.all_gather(cotangent[0], NEAR, axis=0, tiled=True)
    payload = run_pack(queries, keys, values, segment, row_type, pair_index)
    arrived = lax.all_to_all(payload, NEAR, 0, 0)
    out, lse = run_forward(arrived)
    quarters = [quarter] + [
        lax.ppermute(quarter, "x", [(i, (i + turn) % 4) for i in range(4)]) for turn in (1, 2, 3)
    ]
    pieces = run_weight(out, cot, quarters[1:])
    got = lax.all_to_all(pieces, FAR, 0, 0)
    me = jnp.stack([x, lax.axis_index("yl"), 2 * lax.axis_index("p") + lax.axis_index("c")]).astype(jnp.int32)
    own, *others = run_backward(me, arrived, lse, cot, quarters)
    home = [own] + [
        lax.ppermute(other, NEAR, [(i, i ^ (k + 1)) for i in range(8)]) for k, other in enumerate(others)
    ]
    windows = lax.all_gather(run_near_sum(got), "w", axis=0)
    weight_grad = lax.ppermute(run_far_sum(w, windows), AXES, piece_moves()).T
    query_grad, key_grad, value_grad = run_unpack(me, home, queries.shape, keys.shape)
    return query_grad, key_grad, value_grad, weight_grad


def solution(mesh):
    fine = Mesh(mesh.devices.reshape(SIZES), AXES)
    dp, seq = AXES[:3], AXES[3:]
    in_specs = (
        P(dp, seq, None),
        P(dp, seq, None),
        P(dp, seq, None),
        P(dp, seq, None),
        P(seq, None),
        P(dp, seq),
        P(dp, seq),
        P(dp, None),
    )
    out_specs = (P(dp, seq, None), P(dp, seq, None), P(dp, seq, None), P(seq, dp))
    return jax.shard_map(local, mesh=fine, in_specs=in_specs, out_specs=out_specs, check_vma=False)
```

```python
import itertools

import jax
import jax.numpy as jnp
import numpy as np
from jax import lax
from jax.experimental import pallas as pl
from jax.experimental.pallas import tpu as pltpu
from jax.sharding import Mesh
from jax.sharding import PartitionSpec as P

HD = 128
WINDOW = 512
HALF = WINDOW // 2
TOK = 128
SCALE = HD ** (-0.5)
AXES = ("x", "yh", "yl", "w", "p", "c")
SIZES = (4, 4, 2, 4, 2, 2)
NEAR = ("yl", "p", "c")
FAR = ("x", "yh", "w")
CODE = 16
PAY = 4 * TOK + CODE
NONE = 99
F32 = jnp.float32
BF16 = jnp.bfloat16


def place(*index):
    return int(np.ravel_multi_index(index, SIZES))


def devices():
    return itertools.product(*map(range, SIZES))


def key_head(yl, p, c):
    return yl + 2 * p + 4 * c


def weight_moves():
    moves = []
    for x, yh, yl, w, p, c in devices():
        head = 2 * key_head(yl, p, c) + x // 2
        source = place(2 * (w // 2) + x % 2, yh, (w + head) % 2, head // 4, (head // 2) % 2, head % 2)
        moves.append((source, place(x, yh, yl, w, p, c)))
    return moves


def piece_moves():
    moves = []
    for x, yh, yl, w, p, c in devices():
        head = 2 * key_head(yl, p, c) + w % 2
        owner = place(x, yh, w // 2, head // 4, (head // 2) % 2, head % 2)
        moves.append((place(x, yh, yl, w, p, c), owner))
    return moves


def dot(left, right, dims):
    return lax.dot_general(left, right, (dims, ((), ())), preferred_element_type=F32)


def pack_kernel(q_ref, k_ref, v_ref, seg_ref, type_ref, pair_ref, out_ref):
    seg = seg_ref[...]
    kind = type_ref[...]
    pair = jnp.zeros_like(seg)
    count = pair_ref.shape[1]
    for s in range(count):
        pair = jnp.where(seg == s, pair_ref[0, s], pair)
    as_query = jnp.where(kind != 0, count + pair, NONE)
    as_key = jnp.where(kind == 0, count + pair, NONE)
    row = lax.broadcasted_iota(jnp.int32, (CODE, TOK), 0)
    code = jnp.where(row == 0, seg, jnp.where(row == 1, as_query, jnp.where(row == 2, as_key, 0)))
    code = code.astype(F32).astype(BF16)
    for g in range(2):
        out_ref[g, 0, 0:TOK, :] = q_ref[0, :, 2 * g * HD : (2 * g + 1) * HD]
        out_ref[g, 0, TOK : 2 * TOK, :] = q_ref[0, :, (2 * g + 1) * HD : (2 * g + 2) * HD]
        out_ref[g, 0, 2 * TOK : 3 * TOK, :] = k_ref[0, :, g * HD : (g + 1) * HD]
        out_ref[g, 0, 3 * TOK : 4 * TOK, :] = v_ref[0, :, g * HD : (g + 1) * HD]
        out_ref[g, 0, 4 * TOK :, :] = code


def rows(pay_ref, first):
    return pay_ref[:, first : first + TOK, :].reshape(WINDOW, HD)


def hot(pay_ref):
    code = jnp.concatenate([pay_ref[i, 4 * TOK :, :] for i in range(4)], axis=1)
    code = code.astype(F32)[0:8]
    slot = lax.broadcasted_iota(jnp.int32, (32, WINDOW), 0).astype(F32)
    same = slot == code[0:1]
    want = jnp.where(same | (slot == code[1:2]), 1.0, 0.0).astype(BF16)
    have = jnp.where(same | (slot == code[2:3]), 1.0, 0.0).astype(BF16)
    return want, have


def visible_block(want, have, lo, ext):
    count = dot(want[:, lo:ext], have[:, :ext], ((0,), (0,)))
    t_pos = lax.broadcasted_iota(jnp.int32, (ext - lo, ext), 0) + lo
    s_pos = lax.broadcasted_iota(jnp.int32, (ext - lo, ext), 1)
    return (count > 0.5) & (s_pos <= t_pos)


def forward_kernel(pay_ref, out_ref, lse_ref):
    key = rows(pay_ref, 2 * TOK)
    value = rows(pay_ref, 3 * TOK)
    want, have = hot(pay_ref)
    lane = lax.broadcasted_iota(jnp.int32, (HALF, HD), 1)
    for block in range(2):
        lo = block * HALF
        ext = lo + HALF
        visible = visible_block(want, have, lo, ext)
        stats = []
        for b in range(2):
            query = rows(pay_ref, b * TOK)[lo:ext]
            scores = dot(query, key[:ext], ((1,), (1,))) * SCALE
            scores = jnp.where(visible, scores, -jnp.inf)
            top = jnp.max(scores, axis=-1, keepdims=True)
            exponent = jnp.exp(scores - top)
            total = jnp.sum(exponent, axis=-1, keepdims=True)
            low = (exponent * (1.0 / total)).astype(BF16)
            out = dot(low, value[:ext], ((1,), (0,)))
            out_ref[b * HD : (b + 1) * HD, lo:ext] = out.T.astype(BF16)
            stats.append(top + jnp.log(total))
        lse_ref[lo:ext, :] = jnp.where(lane == 0, stats[0], stats[1])


def weight_kernel(out_ref, cot_ref, a_ref, b_ref, c_ref, wg_ref):
    del a_ref, b_ref, c_ref
    total = dot(out_ref[...], cot_ref[...], ((1,), (0,)))
    left = lax.broadcasted_iota(jnp.int32, (64, HD), 1) < 64
    for b in range(2):
        for m in range(8):
            upper = total[b * HD : b * HD + 64, m * HD : (m + 1) * HD]
            lower = total[b * HD + 64 : (b + 1) * HD, m * HD : (m + 1) * HD]
            wg_ref[4 * m + b] = jnp.where(left, upper, pltpu.roll(lower, 64, 1)).astype(BF16)
            wg_ref[4 * m + 2 + b] = jnp.where(left, pltpu.roll(upper, 64, 1), lower).astype(BF16)


def backward_kernel(me_ref, pay_ref, lse_ref, cot_ref, w0_ref, w1_ref, w2_ref, w3_ref, *refs):
    *out_refs, wbuf, ghbuf, ret_ref = refs

    @pl.when(pl.program_id(0) == 0)
    def _():
        for turn, quarter in enumerate((w0_ref, w1_ref, w2_ref, w3_ref)):
            first = pl.multiple_of(lax.rem(me_ref[0] + 4 - turn, 4) * 64, 64)
            wbuf[pl.ds(first, 64), :] = quarter[...]

    ghbuf[...] = dot(cot_ref[...], wbuf[...], ((1,), (1,))).astype(BF16)
    key = rows(pay_ref, 2 * TOK)
    value = rows(pay_ref, 3 * TOK)
    want, have = hot(pay_ref)
    kparts = [[None, None], [None, None]]
    vparts = [[None, None], [None, None]]
    for block in range(2):
        lo = block * HALF
        ext = lo + HALF
        visible = visible_block(want, have, lo, ext)
        for b in range(2):
            query = rows(pay_ref, b * TOK)[lo:ext]
            grad = ghbuf[lo:ext, b * HD : (b + 1) * HD]
            scores = dot(query, key[:ext], ((1,), (1,))) * SCALE - lse_ref[lo:ext, b : b + 1]
            attend = jnp.exp(jnp.where(visible, scores, -jnp.inf))
            low = attend.astype(BF16)
            grad_attend = dot(grad, value[:ext], ((1,), (1,)))
            delta = jnp.sum(attend * grad_attend, axis=-1, keepdims=True)
            ds = (attend * (grad_attend - delta) * SCALE).astype(BF16)
            dq = dot(ds, key[:ext], ((1,), (0,))).astype(BF16)
            ret_ref[2 * block : 2 * block + 2, b * TOK : (b + 1) * TOK, :] = dq.reshape(2, TOK, HD)
            dk = dot(ds, query, ((0,), (0,)))
            dv = dot(low, grad, ((0,), (0,)))
            if block == 0:
                kparts[b][0] = dk
                vparts[b][0] = dv
            else:
                kparts[b] = [kparts[b][0] + dk[:HALF], dk[HALF:]]
                vparts[b] = [vparts[b][0] + dv[:HALF], dv[HALF:]]
    for block in range(2):
        for first, parts in ((2 * TOK, kparts), (3 * TOK, vparts)):
            both = parts[0][block].astype(BF16).astype(F32) + parts[1][block].astype(BF16).astype(F32)
            ret_ref[2 * block : 2 * block + 2, first : first + TOK, :] = both.astype(BF16).reshape(2, TOK, HD)
    for step in range(2):

        @pl.when(pl.program_id(0) == step)
        def _():
            for k in range(4):
                out_refs[4 * step + k][...] = ret_ref[jnp.bitwise_xor(me_ref[2], k)]


def unpack_kernel(me_ref, *refs):
    *got_refs, dq_ref, dk_ref, dv_ref = refs
    for k, got_ref in enumerate(got_refs):
        source = jnp.bitwise_xor(4 * me_ref[1] + me_ref[2], k)
        head = key_head(source // 4, (source // 2) % 2, source % 2)
        near = pl.ds(pl.multiple_of(head * HD, HD), HD)
        dq_ref[0, :, pl.ds(pl.multiple_of(head * 2 * HD, HD), HD)] = got_ref[0:TOK, :]
        dq_ref[0, :, pl.ds(pl.multiple_of(head * 2 * HD + HD, HD), HD)] = got_ref[TOK : 2 * TOK, :]
        dk_ref[0, :, near] = got_ref[2 * TOK : 3 * TOK, :]
        dv_ref[0, :, near] = got_ref[3 * TOK : 4 * TOK, :]


def sum_kernel(got_ref, out_ref):
    total = jnp.sum(got_ref[...].astype(F32), axis=0)
    out_ref[:, 0:64] = total[:, 0:64].T
    out_ref[:, 64:128] = total[:, 64:128].T


SMEM = pl.BlockSpec(memory_space=pltpu.SMEM)
VMEM = pl.BlockSpec(memory_space=pltpu.VMEM)


def whole(*dims):
    return pl.BlockSpec(dims, lambda *_: (0,) * len(dims))


def pair_of_heads(i):
    return 0, 2 * (i % 2) + i // 2, 0, 0


def call(kernel, out_shape, flops=0, bytes_accessed=0, room=60, **kw):
    return pl.pallas_call(
        kernel,
        out_shape=out_shape,
        compiler_params=pltpu.CompilerParams(vmem_limit_bytes=room << 20),
        cost_estimate=pl.CostEstimate(flops=flops, bytes_accessed=bytes_accessed, transcendentals=0),
        **kw,
    )


def shape(dims, dtype=BF16):
    return jax.ShapeDtypeStruct(dims, dtype)


def run_pack(queries, keys, values, segment, row_type, pair_index):
    return call(
        pack_kernel,
        shape((2, 4, PAY, HD)),
        bytes_accessed=2 << 20,
        grid=(4,),
        in_specs=[
            pl.BlockSpec((1, TOK, 4 * HD), lambda i: (0, 0, i)),
            pl.BlockSpec((1, TOK, 2 * HD), lambda i: (0, 0, i)),
            pl.BlockSpec((1, TOK, 2 * HD), lambda i: (0, 0, i)),
            whole(1, TOK),
            whole(1, TOK),
            SMEM,
        ],
        out_specs=pl.BlockSpec((2, 1, PAY, HD), pair_of_heads),
    )(queries, keys, values, segment, row_type, pair_index).reshape(8, PAY, HD)


def run_forward(arrived):
    return call(
        forward_kernel,
        (shape((2 * HD, 2 * WINDOW)), shape((2 * WINDOW, HD), F32)),
        flops=4 << 30,
        bytes_accessed=2 << 20,
        grid=(2,),
        in_specs=[pl.BlockSpec((4, PAY, HD), lambda u: (u, 0, 0))],
        out_specs=[
            pl.BlockSpec((2 * HD, WINDOW), lambda u: (0, u)),
            pl.BlockSpec((WINDOW, HD), lambda u: (u, 0)),
        ],
    )(arrived)


def run_weight(out, cot, after):
    return call(
        weight_kernel,
        shape((64, 64, HD)),
        flops=1 << 30,
        bytes_accessed=6 << 20,
        grid=(2,),
        in_specs=[
            whole(2 * HD, 2 * WINDOW),
            pl.BlockSpec((2 * WINDOW, 1024), lambda i: (0, i)),
        ]
        + [pl.BlockSpec(memory_space=pl.ANY)] * 3,
        out_specs=pl.BlockSpec((32, 64, HD), lambda i: (i, 0, 0)),
    )(out, cot, *after)


def run_backward(me, arrived, lse, cot, quarters):
    width = cot.shape[1]

    def row(step, me_ref):
        return jnp.bitwise_xor(step, me_ref[1])

    grid_spec = pltpu.PrefetchScalarGridSpec(
        num_scalar_prefetch=1,
        grid=(2,),
        in_specs=[
            pl.BlockSpec((4, PAY, HD), lambda i, me_ref: (row(i, me_ref), 0, 0)),
            pl.BlockSpec((WINDOW, HD), lambda i, me_ref: (row(i, me_ref), 0)),
            pl.BlockSpec((WINDOW, width), lambda i, me_ref: (row(i, me_ref), 0)),
        ]
        + [whole(64, width)] * 4,
        out_specs=[whole(4 * TOK, HD)] * 8,
        scratch_shapes=[
            pltpu.VMEM((2 * HD, width), BF16),
            pltpu.VMEM((WINDOW, 2 * HD), BF16),
            pltpu.VMEM((4, 4 * TOK, HD), BF16),
        ],
    )
    return call(
        backward_kernel,
        (shape((4 * TOK, HD)),) * 8,
        flops=8 << 30,
        bytes_accessed=7 << 20,
        grid_spec=grid_spec,
    )(me, arrived, lse, cot, *quarters)


def run_sum(got):
    return call(
        sum_kernel,
        shape((64, HD), F32),
        room=16,
        bytes_accessed=1 << 20,
        in_specs=[VMEM],
        out_specs=VMEM,
    )(got)


def run_unpack(me, home, query_shape, key_shape):
    return call(
        unpack_kernel,
        (shape(query_shape), shape(key_shape), shape(key_shape)),
        room=16,
        bytes_accessed=2 << 20,
        in_specs=[SMEM] + [VMEM] * 8,
        out_specs=[whole(*query_shape), whole(*key_shape), whole(*key_shape)],
    )(me, *home)


def local(queries, keys, values, cotangent, out_weight, segment, row_type, pair_index):
    x = lax.axis_index("x").astype(jnp.int32)
    share = lax.dynamic_slice_in_dim(out_weight, 64 * lax.rem(x, 2), 64, axis=0)
    quarter = lax.ppermute(share, AXES, weight_moves())
    cot = lax.all_gather(cotangent[0], NEAR, axis=0, tiled=True)
    payload = run_pack(queries, keys, values, segment, row_type, pair_index)
    arrived = lax.all_to_all(payload, NEAR, 0, 0)
    out, lse = run_forward(arrived)
    quarters = [quarter] + [
        lax.ppermute(quarter, "x", [(i, (i + turn) % 4) for i in range(4)]) for turn in (1, 2, 3)
    ]
    pieces = run_weight(out, cot, quarters[1:])
    got = lax.all_to_all(pieces, FAR, 0, 0)
    me = jnp.stack([x, lax.axis_index("yl"), 2 * lax.axis_index("p") + lax.axis_index("c")]).astype(jnp.int32)
    own, *others = run_backward(me, arrived, lse, cot, quarters)
    home = [own] + [
        lax.ppermute(other, NEAR, [(i, i ^ (k + 1)) for i in range(8)]) for k, other in enumerate(others)
    ]
    weight_grad = lax.ppermute(run_sum(got), AXES, piece_moves()).T
    query_grad, key_grad, value_grad = run_unpack(me, home, queries.shape, keys.shape)
    return query_grad, key_grad, value_grad, weight_grad


def solution(mesh):
    fine = Mesh(mesh.devices.reshape(SIZES), AXES)
    dp, seq = AXES[:3], AXES[3:]
    in_specs = (
        P(dp, seq, None),
        P(dp, seq, None),
        P(dp, seq, None),
        P(dp, seq, None),
        P(seq, None),
        P(dp, seq),
        P(dp, seq),
        P(dp, None),
    )
    out_specs = (P(dp, seq, None), P(dp, seq, None), P(dp, seq, None), P(seq, dp))
    return jax.shard_map(local, mesh=fine, in_specs=in_specs, out_specs=out_specs, check_vma=False)
```

```python
import itertools

import jax
import jax.numpy as jnp
import numpy as np
from jax import lax
from jax.experimental import pallas as pl
from jax.experimental.pallas import tpu as pltpu
from jax.sharding import Mesh
from jax.sharding import PartitionSpec as P

HD = 128
WINDOW = 512
HALF = WINDOW // 2
TOK = 128
SCALE = HD ** (-0.5)
AXES = ("x", "yh", "yl", "w", "p", "c")
SIZES = (4, 4, 2, 4, 2, 2)
NEAR = ("yl", "p", "c")
FAR = ("x", "yh", "w")
CODE = 16
PAY = 4 * TOK + CODE
NONE = 99
F32 = jnp.float32
BF16 = jnp.bfloat16


def place(*index):
    return int(np.ravel_multi_index(index, SIZES))


def devices():
    return itertools.product(*map(range, SIZES))


def key_head(yl, p, c):
    return yl + 2 * p + 4 * c


def weight_moves():
    moves = []
    for x, yh, yl, w, p, c in devices():
        head = 2 * key_head(yl, p, c) + x // 2
        source = place(2 * (w // 2) + x % 2, yh, (w + head) % 2, head // 4, (head // 2) % 2, head % 2)
        moves.append((source, place(x, yh, yl, w, p, c)))
    return moves


def piece_moves():
    moves = []
    for x, yh, yl, w, p, c in devices():
        head = 2 * key_head(yl, p, c) + w % 2
        owner = place(x, yh, w // 2, head // 4, (head // 2) % 2, head % 2)
        moves.append((place(x, yh, yl, w, p, c), owner))
    return moves


def dot(left, right, dims):
    return lax.dot_general(left, right, (dims, ((), ())), preferred_element_type=F32)


def pack_kernel(q_ref, k_ref, v_ref, seg_ref, type_ref, pair_ref, out_ref):
    seg = seg_ref[...]
    kind = type_ref[...]
    pair = jnp.zeros_like(seg)
    count = pair_ref.shape[1]
    for s in range(count):
        pair = jnp.where(seg == s, pair_ref[0, s], pair)
    as_query = jnp.where(kind != 0, count + pair, NONE)
    as_key = jnp.where(kind == 0, count + pair, NONE)
    row = lax.broadcasted_iota(jnp.int32, (CODE, TOK), 0)
    code = jnp.where(row == 0, seg, jnp.where(row == 1, as_query, jnp.where(row == 2, as_key, 0)))
    code = code.astype(F32).astype(BF16)
    for g in range(2):
        out_ref[g, 0, 0:TOK, :] = q_ref[0, :, 2 * g * HD : (2 * g + 1) * HD]
        out_ref[g, 0, TOK : 2 * TOK, :] = q_ref[0, :, (2 * g + 1) * HD : (2 * g + 2) * HD]
        out_ref[g, 0, 2 * TOK : 3 * TOK, :] = k_ref[0, :, g * HD : (g + 1) * HD]
        out_ref[g, 0, 3 * TOK : 4 * TOK, :] = v_ref[0, :, g * HD : (g + 1) * HD]
        out_ref[g, 0, 4 * TOK :, :] = code


def rows(pay_ref, first):
    return pay_ref[:, first : first + TOK, :].reshape(WINDOW, HD)


def hot(pay_ref):
    code = jnp.concatenate([pay_ref[i, 4 * TOK :, :] for i in range(4)], axis=1)
    code = code.astype(F32)[0:8]
    slot = lax.broadcasted_iota(jnp.int32, (32, WINDOW), 0).astype(F32)
    same = slot == code[0:1]
    want = jnp.where(same | (slot == code[1:2]), 1.0, 0.0).astype(BF16)
    have = jnp.where(same | (slot == code[2:3]), 1.0, 0.0).astype(BF16)
    return want, have


def visible_block(want, have, lo, ext):
    count = dot(want[:, lo:ext], have[:, :ext], ((0,), (0,)))
    t_pos = lax.broadcasted_iota(jnp.int32, (ext - lo, ext), 0) + lo
    s_pos = lax.broadcasted_iota(jnp.int32, (ext - lo, ext), 1)
    return (count > 0.5) & (s_pos <= t_pos)


def forward_kernel(pay_ref, out_ref, lse_ref):
    key = rows(pay_ref, 2 * TOK)
    value = rows(pay_ref, 3 * TOK)
    want, have = hot(pay_ref)
    lane = lax.broadcasted_iota(jnp.int32, (HALF, HD), 1)
    for block in range(2):
        lo = block * HALF
        ext = lo + HALF
        visible = visible_block(want, have, lo, ext)
        stats = []
        for b in range(2):
            query = rows(pay_ref, b * TOK)[lo:ext]
            scores = dot(query, key[:ext], ((1,), (1,))) * SCALE
            scores = jnp.where(visible, scores, -jnp.inf)
            top = jnp.max(scores, axis=-1, keepdims=True)
            exponent = jnp.exp(scores - top)
            total = jnp.sum(exponent, axis=-1, keepdims=True)
            low = (exponent * (1.0 / total)).astype(BF16)
            out = dot(low, value[:ext], ((1,), (0,)))
            out_ref[b * HD : (b + 1) * HD, lo:ext] = out.T.astype(BF16)
            stats.append(top + jnp.log(total))
        lse_ref[lo:ext, :] = jnp.where(lane == 0, stats[0], stats[1])


def weight_kernel(out_ref, cot_ref, a_ref, b_ref, c_ref, wg_ref):
    del a_ref, b_ref, c_ref
    total = dot(out_ref[...], cot_ref[...], ((1,), (0,)))
    left = lax.broadcasted_iota(jnp.int32, (64, HD), 1) < 64
    for b in range(2):
        for m in range(8):
            upper = total[b * HD : b * HD + 64, m * HD : (m + 1) * HD]
            lower = total[b * HD + 64 : (b + 1) * HD, m * HD : (m + 1) * HD]
            wg_ref[4 * m + b] = jnp.where(left, upper, pltpu.roll(lower, 64, 1)).astype(BF16)
            wg_ref[4 * m + 2 + b] = jnp.where(left, pltpu.roll(upper, 64, 1), lower).astype(BF16)


def backward_kernel(me_ref, pay_ref, lse_ref, cot_ref, w0_ref, w1_ref, w2_ref, w3_ref, *refs):
    *out_refs, wbuf, ghbuf, ret_ref = refs

    @pl.when(pl.program_id(0) == 0)
    def _():
        for turn, quarter in enumerate((w0_ref, w1_ref, w2_ref, w3_ref)):
            first = pl.multiple_of(lax.rem(me_ref[0] + 4 - turn, 4) * 64, 64)
            wbuf[pl.ds(first, 64), :] = quarter[...]

    ghbuf[...] = dot(cot_ref[...], wbuf[...], ((1,), (1,))).astype(BF16)
    key = rows(pay_ref, 2 * TOK)
    value = rows(pay_ref, 3 * TOK)
    want, have = hot(pay_ref)
    kparts = [[None, None], [None, None]]
    vparts = [[None, None], [None, None]]
    for block in range(2):
        lo = block * HALF
        ext = lo + HALF
        visible = visible_block(want, have, lo, ext)
        for b in range(2):
            query = rows(pay_ref, b * TOK)[lo:ext]
            grad = ghbuf[lo:ext, b * HD : (b + 1) * HD]
            scores = dot(query, key[:ext], ((1,), (1,))) * SCALE - lse_ref[lo:ext, b : b + 1]
            attend = jnp.exp(jnp.where(visible, scores, -jnp.inf))
            low = attend.astype(BF16)
            grad_attend = dot(grad, value[:ext], ((1,), (1,)))
            delta = jnp.sum(attend * grad_attend, axis=-1, keepdims=True)
            ds = (attend * (grad_attend - delta) * SCALE).astype(BF16)
            dq = dot(ds, key[:ext], ((1,), (0,))).astype(BF16)
            ret_ref[2 * block : 2 * block + 2, b * TOK : (b + 1) * TOK, :] = dq.reshape(2, TOK, HD)
            dk = dot(ds, query, ((0,), (0,)))
            dv = dot(low, grad, ((0,), (0,)))
            if block == 0:
                kparts[b][0] = dk
                vparts[b][0] = dv
            else:
                kparts[b] = [kparts[b][0] + dk[:HALF], dk[HALF:]]
                vparts[b] = [vparts[b][0] + dv[:HALF], dv[HALF:]]
    for block in range(2):
        for first, parts in ((2 * TOK, kparts), (3 * TOK, vparts)):
            both = parts[0][block].astype(BF16).astype(F32) + parts[1][block].astype(BF16).astype(F32)
            ret_ref[2 * block : 2 * block + 2, first : first + TOK, :] = both.astype(BF16).reshape(2, TOK, HD)
    for step in range(2):

        @pl.when(pl.program_id(0) == step)
        def _():
            for k in range(4):
                out_refs[4 * step + k][...] = ret_ref[jnp.bitwise_xor(me_ref[2], k)]


def unpack_kernel(me_ref, *refs):
    *got_refs, dq_ref, dk_ref, dv_ref = refs
    for k, got_ref in enumerate(got_refs):
        source = jnp.bitwise_xor(4 * me_ref[1] + me_ref[2], k)
        head = key_head(source // 4, (source // 2) % 2, source % 2)
        near = pl.ds(pl.multiple_of(head * HD, HD), HD)
        dq_ref[0, :, pl.ds(pl.multiple_of(head * 2 * HD, HD), HD)] = got_ref[0:TOK, :]
        dq_ref[0, :, pl.ds(pl.multiple_of(head * 2 * HD + HD, HD), HD)] = got_ref[TOK : 2 * TOK, :]
        dk_ref[0, :, near] = got_ref[2 * TOK : 3 * TOK, :]
        dv_ref[0, :, near] = got_ref[3 * TOK : 4 * TOK, :]


def sum_kernel(got_ref, out_ref):
    total = jnp.sum(got_ref[...].astype(F32), axis=0)
    out_ref[:, 0:64] = total[:, 0:64].T
    out_ref[:, 64:128] = total[:, 64:128].T


SMEM = pl.BlockSpec(memory_space=pltpu.SMEM)
VMEM = pl.BlockSpec(memory_space=pltpu.VMEM)


def whole(*dims):
    return pl.BlockSpec(dims, lambda *_: (0,) * len(dims))


def pair_of_heads(i):
    return 0, 2 * (i % 2) + i // 2, 0, 0


def call(kernel, out_shape, flops=0, bytes_accessed=0, room=60, **kw):
    return pl.pallas_call(
        kernel,
        out_shape=out_shape,
        compiler_params=pltpu.CompilerParams(vmem_limit_bytes=room << 20),
        cost_estimate=pl.CostEstimate(flops=flops, bytes_accessed=bytes_accessed, transcendentals=0),
        **kw,
    )


def shape(dims, dtype=BF16):
    return jax.ShapeDtypeStruct(dims, dtype)


def run_pack(queries, keys, values, segment, row_type, pair_index):
    return call(
        pack_kernel,
        shape((2, 4, PAY, HD)),
        bytes_accessed=2 << 20,
        grid=(4,),
        in_specs=[
            pl.BlockSpec((1, TOK, 4 * HD), lambda i: (0, 0, i)),
            pl.BlockSpec((1, TOK, 2 * HD), lambda i: (0, 0, i)),
            pl.BlockSpec((1, TOK, 2 * HD), lambda i: (0, 0, i)),
            whole(1, TOK),
            whole(1, TOK),
            SMEM,
        ],
        out_specs=pl.BlockSpec((2, 1, PAY, HD), pair_of_heads),
    )(queries, keys, values, segment, row_type, pair_index).reshape(8, PAY, HD)


def hold_kernel(value_ref, after_ref, out_ref):
    del value_ref, after_ref, out_ref


def run_hold(value, after):
    return call(
        hold_kernel,
        shape(value.shape),
        in_specs=[pl.BlockSpec(memory_space=pl.ANY)] * 2,
        out_specs=pl.BlockSpec(memory_space=pl.ANY),
        input_output_aliases={0: 0},
    )(value, after)


def run_forward(arrived):
    return call(
        forward_kernel,
        (shape((2 * HD, 2 * WINDOW)), shape((2 * WINDOW, HD), F32)),
        flops=4 << 30,
        bytes_accessed=2 << 20,
        grid=(2,),
        in_specs=[pl.BlockSpec((4, PAY, HD), lambda u: (u, 0, 0))],
        out_specs=[
            pl.BlockSpec((2 * HD, WINDOW), lambda u: (0, u)),
            pl.BlockSpec((WINDOW, HD), lambda u: (u, 0)),
        ],
    )(arrived)


def run_weight(out, cot, after):
    return call(
        weight_kernel,
        shape((64, 64, HD)),
        flops=1 << 30,
        bytes_accessed=6 << 20,
        grid=(2,),
        in_specs=[
            whole(2 * HD, 2 * WINDOW),
            pl.BlockSpec((2 * WINDOW, 1024), lambda i: (0, i)),
        ]
        + [pl.BlockSpec(memory_space=pl.ANY)] * 3,
        out_specs=pl.BlockSpec((32, 64, HD), lambda i: (i, 0, 0)),
    )(out, cot, *after)


def run_backward(me, arrived, lse, cot, quarters):
    width = cot.shape[1]

    def row(step, me_ref):
        return jnp.bitwise_xor(step, me_ref[1])

    grid_spec = pltpu.PrefetchScalarGridSpec(
        num_scalar_prefetch=1,
        grid=(2,),
        in_specs=[
            pl.BlockSpec((4, PAY, HD), lambda i, me_ref: (row(i, me_ref), 0, 0)),
            pl.BlockSpec((WINDOW, HD), lambda i, me_ref: (row(i, me_ref), 0)),
            pl.BlockSpec((WINDOW, width), lambda i, me_ref: (row(i, me_ref), 0)),
        ]
        + [whole(64, width)] * 4,
        out_specs=[whole(4 * TOK, HD)] * 8,
        scratch_shapes=[
            pltpu.VMEM((2 * HD, width), BF16),
            pltpu.VMEM((WINDOW, 2 * HD), BF16),
            pltpu.VMEM((4, 4 * TOK, HD), BF16),
        ],
    )
    return call(
        backward_kernel,
        (shape((4 * TOK, HD)),) * 8,
        flops=8 << 30,
        bytes_accessed=7 << 20,
        grid_spec=grid_spec,
    )(me, arrived, lse, cot, *quarters)


def run_sum(got):
    return call(
        sum_kernel,
        shape((64, HD), F32),
        room=16,
        bytes_accessed=1 << 20,
        in_specs=[VMEM],
        out_specs=VMEM,
    )(got)


def run_unpack(me, home, query_shape, key_shape):
    return call(
        unpack_kernel,
        (shape(query_shape), shape(key_shape), shape(key_shape)),
        room=16,
        bytes_accessed=2 << 20,
        in_specs=[SMEM] + [VMEM] * 8,
        out_specs=[whole(*query_shape), whole(*key_shape), whole(*key_shape)],
    )(me, *home)


def local(queries, keys, values, cotangent, out_weight, segment, row_type, pair_index):
    x = lax.axis_index("x").astype(jnp.int32)
    share = lax.dynamic_slice_in_dim(out_weight, 64 * lax.rem(x, 2), 64, axis=0)
    quarter = lax.ppermute(share, AXES, weight_moves())
    cot = lax.all_gather(cotangent[0], NEAR, axis=0, tiled=True)
    payload = run_pack(queries, keys, values, segment, row_type, pair_index)
    arrived = lax.all_to_all(run_hold(payload, quarter), NEAR, 0, 0)
    out, lse = run_forward(arrived)
    quarters = [quarter] + [
        lax.ppermute(quarter, "x", [(i, (i + turn) % 4) for i in range(4)]) for turn in (1, 2, 3)
    ]
    pieces = run_weight(out, cot, quarters[1:])
    got = lax.all_to_all(pieces, FAR, 0, 0)
    me = jnp.stack([x, lax.axis_index("yl"), 2 * lax.axis_index("p") + lax.axis_index("c")]).astype(jnp.int32)
    own, *others = run_backward(me, arrived, lse, cot, quarters)
    home = [own] + [
        lax.ppermute(other, NEAR, [(i, i ^ (k + 1)) for i in range(8)]) for k, other in enumerate(others)
    ]
    weight_grad = lax.ppermute(run_sum(got), AXES, piece_moves()).T
    query_grad, key_grad, value_grad = run_unpack(me, home, queries.shape, keys.shape)
    return query_grad, key_grad, value_grad, weight_grad


def solution(mesh):
    fine = Mesh(mesh.devices.reshape(SIZES), AXES)
    dp, seq = AXES[:3], AXES[3:]
    in_specs = (
        P(dp, seq, None),
        P(dp, seq, None),
        P(dp, seq, None),
        P(dp, seq, None),
        P(seq, None),
        P(dp, seq),
        P(dp, seq),
        P(dp, None),
    )
    out_specs = (P(dp, seq, None), P(dp, seq, None), P(dp, seq, None), P(seq, dp))
    return jax.shard_map(local, mesh=fine, in_specs=in_specs, out_specs=out_specs, check_vma=False)
```

```python
import itertools

import jax
import jax.numpy as jnp
import numpy as np
from jax import lax
from jax.experimental import pallas as pl
from jax.experimental.pallas import tpu as pltpu
from jax.sharding import Mesh
from jax.sharding import PartitionSpec as P

HD = 128
WINDOW = 512
HALF = WINDOW // 2
TOK = 128
SCALE = HD ** (-0.5)
AXES = ("x", "yh", "yl", "w", "p", "c")
SIZES = (4, 4, 2, 4, 2, 2)
NEAR = ("yl", "p", "c")
FAR = ("x", "yh", "w")
CODE = 16
PAY = 4 * TOK + CODE
NONE = 99
F32 = jnp.float32
BF16 = jnp.bfloat16


def place(*index):
    return int(np.ravel_multi_index(index, SIZES))


def devices():
    return itertools.product(*map(range, SIZES))


def key_head(yl, p, c):
    return yl + 2 * p + 4 * c


def weight_moves():
    moves = []
    for x, yh, yl, w, p, c in devices():
        head = 2 * key_head(yl, p, c) + x // 2
        source = place(2 * (w // 2) + x % 2, yh, (w + head) % 2, head // 4, (head // 2) % 2, head % 2)
        moves.append((source, place(x, yh, yl, w, p, c)))
    return moves


def piece_moves():
    moves = []
    for x, yh, yl, w, p, c in devices():
        head = 2 * key_head(yl, p, c) + w % 2
        owner = place(x, yh, w // 2, head // 4, (head // 2) % 2, head % 2)
        moves.append((place(x, yh, yl, w, p, c), owner))
    return moves


def dot(left, right, dims):
    return lax.dot_general(left, right, (dims, ((), ())), preferred_element_type=F32)


def pack_kernel(q_ref, k_ref, v_ref, seg_ref, type_ref, pair_ref, out_ref):
    seg = seg_ref[...]
    kind = type_ref[...]
    pair = jnp.zeros_like(seg)
    count = pair_ref.shape[1]
    for s in range(count):
        pair = jnp.where(seg == s, pair_ref[0, s], pair)
    as_query = jnp.where(kind != 0, count + pair, NONE)
    as_key = jnp.where(kind == 0, count + pair, NONE)
    row = lax.broadcasted_iota(jnp.int32, (CODE, TOK), 0)
    code = jnp.where(row == 0, seg, jnp.where(row == 1, as_query, jnp.where(row == 2, as_key, 0)))
    code = code.astype(F32).astype(BF16)
    for g in range(2):
        out_ref[g, 0, 0:TOK, :] = q_ref[0, :, 2 * g * HD : (2 * g + 1) * HD]
        out_ref[g, 0, TOK : 2 * TOK, :] = q_ref[0, :, (2 * g + 1) * HD : (2 * g + 2) * HD]
        out_ref[g, 0, 2 * TOK : 3 * TOK, :] = k_ref[0, :, g * HD : (g + 1) * HD]
        out_ref[g, 0, 3 * TOK : 4 * TOK, :] = v_ref[0, :, g * HD : (g + 1) * HD]
        out_ref[g, 0, 4 * TOK :, :] = code


def rows(pay_ref, first):
    return pay_ref[:, first : first + TOK, :].reshape(WINDOW, HD)


def hot(pay_ref):
    code = jnp.concatenate([pay_ref[i, 4 * TOK :, :] for i in range(4)], axis=1)
    code = code.astype(F32)[0:8]
    slot = lax.broadcasted_iota(jnp.int32, (32, WINDOW), 0).astype(F32)
    same = slot == code[0:1]
    want = jnp.where(same | (slot == code[1:2]), 1.0, 0.0).astype(BF16)
    have = jnp.where(same | (slot == code[2:3]), 1.0, 0.0).astype(BF16)
    return want, have


def visible_block(want, have, lo, ext):
    count = dot(want[:, lo:ext], have[:, :ext], ((0,), (0,)))
    t_pos = lax.broadcasted_iota(jnp.int32, (ext - lo, ext), 0) + lo
    s_pos = lax.broadcasted_iota(jnp.int32, (ext - lo, ext), 1)
    return (count > 0.5) & (s_pos <= t_pos)


def forward_kernel(pay_ref, out_ref, lse_ref):
    key = rows(pay_ref, 2 * TOK)
    value = rows(pay_ref, 3 * TOK)
    want, have = hot(pay_ref)
    lane = lax.broadcasted_iota(jnp.int32, (HALF, HD), 1)
    for block in range(2):
        lo = block * HALF
        ext = lo + HALF
        visible = visible_block(want, have, lo, ext)
        stats = []
        for b in range(2):
            query = rows(pay_ref, b * TOK)[lo:ext]
            scores = dot(query, key[:ext], ((1,), (1,))) * SCALE
            scores = jnp.where(visible, scores, -jnp.inf)
            top = jnp.max(scores, axis=-1, keepdims=True)
            exponent = jnp.exp(scores - top)
            total = jnp.sum(exponent, axis=-1, keepdims=True)
            low = (exponent * (1.0 / total)).astype(BF16)
            out = dot(low, value[:ext], ((1,), (0,)))
            out_ref[b * HD : (b + 1) * HD, lo:ext] = out.T.astype(BF16)
            stats.append(top + jnp.log(total))
        lse_ref[lo:ext, :] = jnp.where(lane == 0, stats[0], stats[1])


def weight_kernel(out_ref, cot_ref, a_ref, b_ref, c_ref, wg_ref):
    del a_ref, b_ref, c_ref
    total = dot(out_ref[...], cot_ref[...], ((1,), (0,)))
    left = lax.broadcasted_iota(jnp.int32, (64, HD), 1) < 64
    for b in range(2):
        for m in range(8):
            upper = total[b * HD : b * HD + 64, m * HD : (m + 1) * HD]
            lower = total[b * HD + 64 : (b + 1) * HD, m * HD : (m + 1) * HD]
            wg_ref[4 * m + b] = jnp.where(left, upper, pltpu.roll(lower, 64, 1)).astype(BF16)
            wg_ref[4 * m + 2 + b] = jnp.where(left, pltpu.roll(upper, 64, 1), lower).astype(BF16)


def backward_kernel(me_ref, pay_ref, lse_ref, cot_ref, w0_ref, w1_ref, w2_ref, w3_ref, *refs):
    *out_refs, wbuf, ghbuf, ret_ref, abuf, cbuf, sem = refs
    now = pl.program_id(0)

    def fetch(step):
        first = pl.multiple_of(jnp.bitwise_xor(step, me_ref[1]) * WINDOW, WINDOW)
        return pltpu.make_async_copy(cot_ref.at[pl.ds(first, WINDOW)], cbuf.at[step], sem.at[step])

    @pl.when(now == 0)
    def _():
        fetch(0).start()
        fetch(1).start()
        for turn, quarter in enumerate((w0_ref, w1_ref, w2_ref, w3_ref)):
            first = pl.multiple_of(lax.rem(me_ref[0] + 4 - turn, 4) * 64, 64)
            wbuf[pl.ds(first, 64), :] = quarter[...]

    key = rows(pay_ref, 2 * TOK)
    value = rows(pay_ref, 3 * TOK)
    want, have = hot(pay_ref)
    for block in range(2):
        lo = block * HALF
        ext = lo + HALF
        visible = visible_block(want, have, lo, ext)
        for b in range(2):
            query = rows(pay_ref, b * TOK)[lo:ext]
            scores = dot(query, key[:ext], ((1,), (1,))) * SCALE - lse_ref[lo:ext, b : b + 1]
            abuf[b, lo:ext, :ext] = jnp.exp(jnp.where(visible, scores, -jnp.inf))
    fetch(now).wait()
    ghbuf[...] = dot(cbuf[now], wbuf[...], ((1,), (1,))).astype(BF16)
    kparts = [[None, None], [None, None]]
    vparts = [[None, None], [None, None]]
    for block in range(2):
        lo = block * HALF
        ext = lo + HALF
        for b in range(2):
            query = rows(pay_ref, b * TOK)[lo:ext]
            grad = ghbuf[lo:ext, b * HD : (b + 1) * HD]
            attend = abuf[b, lo:ext, :ext]
            low = attend.astype(BF16)
            grad_attend = dot(grad, value[:ext], ((1,), (1,)))
            delta = jnp.sum(attend * grad_attend, axis=-1, keepdims=True)
            ds = (attend * (grad_attend - delta) * SCALE).astype(BF16)
            dq = dot(ds, key[:ext], ((1,), (0,))).astype(BF16)
            ret_ref[2 * block : 2 * block + 2, b * TOK : (b + 1) * TOK, :] = dq.reshape(2, TOK, HD)
            dk = dot(ds, query, ((0,), (0,)))
            dv = dot(low, grad, ((0,), (0,)))
            if block == 0:
                kparts[b][0] = dk
                vparts[b][0] = dv
            else:
                kparts[b] = [kparts[b][0] + dk[:HALF], dk[HALF:]]
                vparts[b] = [vparts[b][0] + dv[:HALF], dv[HALF:]]
    for block in range(2):
        for first, parts in ((2 * TOK, kparts), (3 * TOK, vparts)):
            both = parts[0][block].astype(BF16).astype(F32) + parts[1][block].astype(BF16).astype(F32)
            ret_ref[2 * block : 2 * block + 2, first : first + TOK, :] = both.astype(BF16).reshape(2, TOK, HD)
    for step in range(2):

        @pl.when(pl.program_id(0) == step)
        def _():
            for k in range(4):
                out_refs[4 * step + k][...] = ret_ref[jnp.bitwise_xor(me_ref[2], k)]


def unpack_kernel(me_ref, *refs):
    *got_refs, dq_ref, dk_ref, dv_ref = refs
    for k, got_ref in enumerate(got_refs):
        source = jnp.bitwise_xor(4 * me_ref[1] + me_ref[2], k)
        head = key_head(source // 4, (source // 2) % 2, source % 2)
        near = pl.ds(pl.multiple_of(head * HD, HD), HD)
        dq_ref[0, :, pl.ds(pl.multiple_of(head * 2 * HD, HD), HD)] = got_ref[0:TOK, :]
        dq_ref[0, :, pl.ds(pl.multiple_of(head * 2 * HD + HD, HD), HD)] = got_ref[TOK : 2 * TOK, :]
        dk_ref[0, :, near] = got_ref[2 * TOK : 3 * TOK, :]
        dv_ref[0, :, near] = got_ref[3 * TOK : 4 * TOK, :]


def sum_kernel(got_ref, out_ref):
    total = jnp.sum(got_ref[...].astype(F32), axis=0)
    out_ref[:, 0:64] = total[:, 0:64].T
    out_ref[:, 64:128] = total[:, 64:128].T


SMEM = pl.BlockSpec(memory_space=pltpu.SMEM)
VMEM = pl.BlockSpec(memory_space=pltpu.VMEM)


def whole(*dims):
    return pl.BlockSpec(dims, lambda *_: (0,) * len(dims))


def pair_of_heads(i):
    return 0, 2 * (i % 2) + i // 2, 0, 0


def call(kernel, out_shape, flops=0, bytes_accessed=0, room=60, **kw):
    return pl.pallas_call(
        kernel,
        out_shape=out_shape,
        compiler_params=pltpu.CompilerParams(vmem_limit_bytes=room << 20),
        cost_estimate=pl.CostEstimate(flops=flops, bytes_accessed=bytes_accessed, transcendentals=0),
        **kw,
    )


def shape(dims, dtype=BF16):
    return jax.ShapeDtypeStruct(dims, dtype)


def run_pack(queries, keys, values, segment, row_type, pair_index):
    return call(
        pack_kernel,
        shape((2, 4, PAY, HD)),
        bytes_accessed=2 << 20,
        grid=(4,),
        in_specs=[
            pl.BlockSpec((1, TOK, 4 * HD), lambda i: (0, 0, i)),
            pl.BlockSpec((1, TOK, 2 * HD), lambda i: (0, 0, i)),
            pl.BlockSpec((1, TOK, 2 * HD), lambda i: (0, 0, i)),
            whole(1, TOK),
            whole(1, TOK),
            SMEM,
        ],
        out_specs=pl.BlockSpec((2, 1, PAY, HD), pair_of_heads),
    )(queries, keys, values, segment, row_type, pair_index).reshape(8, PAY, HD)


def hold_kernel(value_ref, after_ref, out_ref):
    del value_ref, after_ref, out_ref


def run_hold(value, after):
    return call(
        hold_kernel,
        shape(value.shape),
        in_specs=[pl.BlockSpec(memory_space=pl.ANY)] * 2,
        out_specs=pl.BlockSpec(memory_space=pl.ANY),
        input_output_aliases={0: 0},
    )(value, after)


def run_forward(arrived):
    return call(
        forward_kernel,
        (shape((2 * HD, 2 * WINDOW)), shape((2 * WINDOW, HD), F32)),
        room=40,
        flops=4 << 30,
        bytes_accessed=2 << 20,
        grid=(2,),
        in_specs=[pl.BlockSpec((4, PAY, HD), lambda u: (u, 0, 0))],
        out_specs=[
            pl.BlockSpec((2 * HD, WINDOW), lambda u: (0, u)),
            pl.BlockSpec((WINDOW, HD), lambda u: (u, 0)),
        ],
    )(arrived)


def run_weight(out, cot, after):
    return call(
        weight_kernel,
        shape((64, 64, HD)),
        flops=1 << 30,
        bytes_accessed=6 << 20,
        grid=(2,),
        in_specs=[
            whole(2 * HD, 2 * WINDOW),
            pl.BlockSpec((2 * WINDOW, 1024), lambda i: (0, i)),
        ]
        + [pl.BlockSpec(memory_space=pl.ANY)] * 3,
        out_specs=pl.BlockSpec((32, 64, HD), lambda i: (i, 0, 0)),
    )(out, cot, *after)


def run_backward(me, arrived, lse, cot, quarters):
    width = cot.shape[1]

    def row(step, me_ref):
        return jnp.bitwise_xor(step, me_ref[1])

    grid_spec = pltpu.PrefetchScalarGridSpec(
        num_scalar_prefetch=1,
        grid=(2,),
        in_specs=[
            pl.BlockSpec((4, PAY, HD), lambda i, me_ref: (row(i, me_ref), 0, 0)),
            pl.BlockSpec((WINDOW, HD), lambda i, me_ref: (row(i, me_ref), 0)),
            pl.BlockSpec(memory_space=pltpu.HBM),
        ]
        + [whole(64, width)] * 4,
        out_specs=[whole(4 * TOK, HD)] * 8,
        scratch_shapes=[
            pltpu.VMEM((2 * HD, width), BF16),
            pltpu.VMEM((WINDOW, 2 * HD), BF16),
            pltpu.VMEM((4, 4 * TOK, HD), BF16),
            pltpu.VMEM((2, WINDOW, WINDOW), F32),
            pltpu.VMEM((2, WINDOW, width), BF16),
            pltpu.SemaphoreType.DMA((2,)),
        ],
    )
    return call(
        backward_kernel,
        (shape((4 * TOK, HD)),) * 8,
        flops=8 << 30,
        bytes_accessed=7 << 20,
        grid_spec=grid_spec,
    )(me, arrived, lse, cot, *quarters)


def run_sum(got):
    return call(
        sum_kernel,
        shape((64, HD), F32),
        room=16,
        bytes_accessed=1 << 20,
        in_specs=[VMEM],
        out_specs=VMEM,
    )(got)


def run_unpack(me, home, query_shape, key_shape):
    return call(
        unpack_kernel,
        (shape(query_shape), shape(key_shape), shape(key_shape)),
        room=16,
        bytes_accessed=2 << 20,
        in_specs=[SMEM] + [VMEM] * 8,
        out_specs=[whole(*query_shape), whole(*key_shape), whole(*key_shape)],
    )(me, *home)


def local(queries, keys, values, cotangent, out_weight, segment, row_type, pair_index):
    x = lax.axis_index("x").astype(jnp.int32)
    share = lax.dynamic_slice_in_dim(out_weight, 64 * lax.rem(x, 2), 64, axis=0)
    quarter = lax.ppermute(share, AXES, weight_moves())
    cot = lax.all_gather(cotangent[0], NEAR, axis=0, tiled=True)
    payload = run_pack(queries, keys, values, segment, row_type, pair_index)
    arrived = lax.all_to_all(run_hold(payload, quarter), NEAR, 0, 0)
    out, lse = run_forward(arrived)
    quarters = [quarter] + [
        lax.ppermute(quarter, "x", [(i, (i + turn) % 4) for i in range(4)]) for turn in (1, 2, 3)
    ]
    pieces = run_weight(out, cot, quarters[1:])
    got = lax.all_to_all(pieces, FAR, 0, 0)
    me = jnp.stack([x, lax.axis_index("yl"), 2 * lax.axis_index("p") + lax.axis_index("c")]).astype(jnp.int32)
    own, *others = run_backward(me, arrived, lse, cot, quarters)
    home = [own] + [
        lax.ppermute(other, NEAR, [(i, i ^ (k + 1)) for i in range(8)]) for k, other in enumerate(others)
    ]
    weight_grad = lax.ppermute(run_sum(got), AXES, piece_moves()).T
    query_grad, key_grad, value_grad = run_unpack(me, home, queries.shape, keys.shape)
    return query_grad, key_grad, value_grad, weight_grad


def solution(mesh):
    fine = Mesh(mesh.devices.reshape(SIZES), AXES)
    dp, seq = AXES[:3], AXES[3:]
    in_specs = (
        P(dp, seq, None),
        P(dp, seq, None),
        P(dp, seq, None),
        P(dp, seq, None),
        P(seq, None),
        P(dp, seq),
        P(dp, seq),
        P(dp, None),
    )
    out_specs = (P(dp, seq, None), P(dp, seq, None), P(dp, seq, None), P(seq, dp))
    return jax.shard_map(local, mesh=fine, in_specs=in_specs, out_specs=out_specs, check_vma=False)
```
